256 devices in a mesh: layer: 8 (over y, core), front: 32 (over z, x).
Axes of the slice: x: 4, y: 4, z: 8, core: 2. Of those that a mesh axis runs over, the one named last changes fastest.
Arguments:
- sources_down: float32 [8, 32, 2, 32, 256], P('layer', 'front'), may hold values from -6 to 6
- sources_up: float32 [8, 32, 2, 32, 256], P('layer', 'front'), may hold values from -6 to 6
- leaf_inverse: float32 [8, 32, 2, 256, 256], P('layer', 'front'), may hold values from -0.25 to 0.25
- coupling: float32 [8, 32, 2, 512, 256], P('layer', 'front'), may hold values from -0.25 to 0.25
- sep_inverse: float32 [8, 32, 2, 256, 256], P('layer', 'front'), may hold values from -0.25 to 0.25
- inject_top: float32 [8, 32, 2, 128, 256], P('layer', 'front'), may hold values from -0.125 to 0.125
- inject_bottom: float32 [8, 32, 2, 128, 256], P('layer', 'front'), may hold values from -0.125 to 0.125
- targets: int32 [8, 32, 16, 1], P('layer', 'front'), may hold values from 0 to 31; in each aligned block of 16 rows (0 to 15, 16 to 31, ..., all dimensions but the last counted through in order) at most 2 rows name the same one
- offsets: int32 [8, 32, 16], P('layer', 'front'), may hold values from 0 to 7
Outputs:
- field_down: float32 [8, 32, 2, 32, 256], P('layer', 'front')
- field_up: float32 [8, 32, 2, 32, 256], P('layer', 'front')
The draws below stay inside these ranges and needn't reach their ends.
Inputs may be any that keep to these rules, and one draw needn't show every extreme that they name: `targets`: the 16 blocks of one leaf name one separator at most 2 times, and in every draw some leaf names one separator exactly 2 times.
All inputs are finite; a program needn't handle non-finite values.
Results may differ from the reference program's by a relative error of at most 0.00019.
Values sent between devices are 32-bit elements; how exact they have to be, the bound alone decides.
No kernel may reach another device: no remote copies, remote signals or barrier semaphores. Data moves between devices by JAX's collectives and lax.ppermute only.
A program may use at most 64 MiB of HBM per device.

```python
import math
import jax
import jax.numpy as jnp
import numpy as np
from jax import lax

P_SIZE = 256
B = 512
Q = 256
TR = 128
RB = 32
S = 32
NB = 16
QB = 8
CAP = 2
LAYERS = 8
LEAVES = 32


def set_ends(entries, rng, low, high):
    spot = [jax.random.randint(jax.random.fold_in(rng, axis), (), 0, length) for axis, length in enumerate(entries.shape)]
    main_axis = entries.shape.index(max(entries.shape))
    neighbour = spot[:main_axis] + [(spot[main_axis] + 1) % entries.shape[main_axis]] + spot[main_axis + 1:]
    return entries.at[tuple(spot)].set(low).at[tuple(neighbour)].set(high)


def shard_levels(key, dims, pieces, low, high):
    level = 1.0
    for dim, parts in pieces:
        steps = jax.random.uniform(jax.random.fold_in(jax.random.fold_in(key, 6), dim), (parts,), jnp.float32, low / len(pieces), high / len(pieces))
        level = level * jnp.repeat(jnp.exp(steps), dims[dim] // parts).reshape((-1,) + (1,) * (len(dims) - 1 - dim))
    return level


def routed_block(rng, own, number, rows, amount, top, most, lean):
    order = jax.random.permutation(rng, amount)
    crowded, ordinary = portions_of(amount, rows * top, most, lean, True), portions_of(amount, rows * top, most, lean, False)
    places = jnp.arange(amount)

    def named(lengths, turn):
        used = int((lengths > 0).sum())
        fixed = max(1, used // 4)
        passed = fixed + (places - fixed + turn * (used - fixed)) % max(1, amount - fixed)
        return jnp.zeros((amount,), jnp.int32).at[order[jnp.where(places < fixed, places, passed)]].set(jnp.asarray(lengths, jnp.int32))

    lengths = jnp.where(number % 4 == 0, named(crowded, number // 4), named(ordinary, number - number // 4 - 1))
    mixed = jax.random.permutation(jax.random.fold_in(own, 3), amount)
    donor, taker = mixed[0:amount // 2 * 2:2], mixed[1:amount // 2 * 2:2]
    room = jnp.minimum(lengths[donor] - 1, most - lengths[taker]) // 2
    room = jnp.where((donor == order[0]) | (taker == order[0]) | (lengths[taker] == 0), 0, jnp.maximum(room, 0))
    passed = jax.random.randint(jax.random.fold_in(own, 4), (amount // 2,), 0, 1 << 20) % (room + 1)
    lengths = lengths.at[donor].add(-passed).at[taker].add(passed)
    items = jnp.searchsorted(jnp.cumsum(lengths), jnp.arange(rows * top), side="right").astype(jnp.int32)
    listing = items.reshape(top, rows).T
    listing = listing[jax.random.permutation(jax.random.fold_in(own, 1), rows)]
    turn = jax.random.randint(jax.random.fold_in(own, 2), (rows, 1), 0, top)
    return jnp.take_along_axis(listing, (jnp.arange(top)[None, :] + turn) % top, axis=1)


def portions_of(amount, total, bound, lean, full):
    loads = [(1 << 20) // math.isqrt(rank ** lean) + 1 for rank in range(1, amount + 1)]
    largest = bound if full else min(bound, max(-(-total // amount), total * loads[0] // sum(loads)))
    least = 1 if total - largest >= amount - 1 else 0
    holding, rest = [largest] + [least] * (amount - 1), total - largest - least * (amount - 1)
    while rest > 0:
        free = [i for i in range(1, amount) if holding[i] < largest] or [i for i in range(1, amount) if holding[i] < bound]
        pool, budget = sum([loads[i] for i in free]), rest
        for i in free:
            more = min(bound - holding[i], max(1, budget * loads[i] // pool), rest)
            holding[i] = holding[i] + more
            rest = rest - more
    return np.array(holding)


def normal_values(stream_key, extent, deviation, bound, shards=(), kind=jnp.bfloat16):
    gain = shard_levels(stream_key, extent, shards, -0.22, 0.18) if shards else 1.0
    values = jax.random.normal(stream_key, extent, jnp.float32) * deviation * gain
    return jnp.minimum(jnp.maximum(values, -bound), bound).astype(kind)


def setup_inputs(seed: int = 0) -> dict:
    key_list = jax.random.split(jax.random.key(seed), 10)
    sources_down = normal_values(key_list[0], (LAYERS, LEAVES, 2, S, P_SIZE), 1.0, 6.0, ((0, 8), (1, 32)), jnp.float32)
    sources_up = normal_values(key_list[1], (LAYERS, LEAVES, 2, S, P_SIZE), 1.0, 6.0, ((0, 8), (1, 32)), jnp.float32)
    leaf_inverse = normal_values(key_list[2], (LAYERS, LEAVES, 2, P_SIZE, P_SIZE), (2 * P_SIZE) ** -0.5, 0.25, ((0, 8), (1, 32)), jnp.float32)
    coupling = normal_values(key_list[3], (LAYERS, LEAVES, 2, B, P_SIZE), (2 * P_SIZE) ** -0.5, 0.25, ((0, 8), (1, 32)), jnp.float32)
    sep_inverse = normal_values(key_list[4], (LAYERS, LEAVES, 2, Q, Q), (2 * Q) ** -0.5, 0.25, ((0, 8), (1, 32)), jnp.float32)
    inject_top = normal_values(key_list[5], (LAYERS, LEAVES, 2, TR, P_SIZE), (16 * TR) ** -0.5, 0.125, ((0, 8), (1, 32)), jnp.float32)
    inject_bottom = normal_values(key_list[6], (LAYERS, LEAVES, 2, TR, P_SIZE), (16 * TR) ** -0.5, 0.125, ((0, 8), (1, 32)), jnp.float32)
    targets_keys = jax.random.split(jax.random.fold_in(key_list[7], 1), LAYERS * LEAVES * NB // NB)
    targets_turns = jax.random.permutation(jax.random.fold_in(key_list[7], 3), LAYERS * LEAVES * NB // NB)
    targets = jax.vmap(lambda own, number: routed_block(jax.random.fold_in(key_list[7], 2), own, number, NB, LEAVES, 1, CAP, 2))(targets_keys, targets_turns).reshape((LAYERS, LEAVES, NB, 1))
    offsets = set_ends(jax.random.randint(key_list[8], (LAYERS, LEAVES, NB), 0, QB), jax.random.fold_in(key_list[8], 1), 0, QB - 1).astype(jnp.int32)
    return dict(sources_down=sources_down, sources_up=sources_up, leaf_inverse=leaf_inverse, coupling=coupling, sep_inverse=sep_inverse, inject_top=inject_top, inject_bottom=inject_bottom, targets=targets, offsets=offsets)


precise = lax.Precision.HIGHEST


def complex_product(pattern, first, second):
    real_part = jnp.einsum(pattern, first[0], second[0], precision=precise) - jnp.einsum(pattern, first[1], second[1], precision=precise)
    imag_part = jnp.einsum(pattern, first[0], second[1], precision=precise) + jnp.einsum(pattern, first[1], second[0], precision=precise)
    return real_part, imag_part


def layer_solve(rhs_pair, leaf_matrix, coupling_rows, sep_matrix, target_list, offset_list):
    leaves = rhs_pair[0].shape[0]
    columns = rhs_pair[0].shape[1]
    leaf_pair = (leaf_matrix[:, 0], leaf_matrix[:, 1])
    coupling_pair = (coupling_rows[:, 0], coupling_rows[:, 1])
    interior = complex_product("fcq,fpq->fcp", rhs_pair, leaf_pair)
    update = complex_product("fcp,fbp->fbc", interior, coupling_pair)
    position = (target_list.astype(jnp.int32) * QB + offset_list.astype(jnp.int32)).reshape(-1).astype(jnp.int32)

    def assemble(part):
        blocks = part.reshape(leaves * NB, RB, columns)
        return jax.ops.segment_sum(blocks, position, num_segments=leaves * QB).reshape(leaves, Q, columns)

    sep_rhs = (assemble(update[0]), assemble(update[1]))
    sep_pair = (sep_matrix[:, 0], sep_matrix[:, 1])
    solved = complex_product("fqc,fpq->fpc", sep_rhs, sep_pair)

    def fetch(part):
        return part.reshape(leaves * QB, RB, columns)[position].reshape(leaves, B, columns)

    returned = (fetch(solved[0]), fetch(solved[1]))
    pushed = complex_product("fbc,fbp->fcp", returned, coupling_pair)
    correction = complex_product("fcq,fpq->fcp", pushed, leaf_pair)
    return interior[0] + correction[0], interior[1] + correction[1]


def sweep(sources, inject, leaf_inverse, coupling, sep_inverse, targets, offsets, order, upward):
    leaves = sources.shape[1]
    blank = jnp.zeros((leaves, S, TR), sources.dtype)
    trace = (blank, blank)
    fields = {}
    for depth_index in order:
        mapping = inject[depth_index]
        injected = complex_product("fct,ftp->fcp", trace, (mapping[:, 0], mapping[:, 1]))
        rhs_pair = (sources[depth_index][:, 0] + injected[0], sources[depth_index][:, 1] + injected[1])
        field = layer_solve(rhs_pair, leaf_inverse[depth_index], coupling[depth_index], sep_inverse[depth_index], targets[depth_index][:, :, 0], offsets[depth_index])
        fields[depth_index] = jnp.stack(field, axis=1)
        if upward:
            trace = (field[0][:, :, :TR], field[1][:, :, :TR])
        else:
            trace = (field[0][:, :, P_SIZE - TR:], field[1][:, :, P_SIZE - TR:])
    return jnp.stack([fields[index] for index in range(sources.shape[0])])


def reference(sources_down, sources_up, leaf_inverse, coupling, sep_inverse, inject_top, inject_bottom, targets, offsets):
    layers = sources_down.shape[0]
    field_down = sweep(sources_down, inject_top, leaf_inverse, coupling, sep_inverse, targets, offsets, list(range(layers)), False)
    field_up = sweep(sources_up, inject_bottom, leaf_inverse, coupling, sep_inverse, targets, offsets, list(range(layers - 1, -1, -1)), True)
    return field_down, field_up
```

```python
import functools

import jax
import jax.numpy as jnp
from jax import lax
from jax.experimental import pallas as pl
from jax.experimental.pallas import tpu as pltpu
from jax.sharding import PartitionSpec as P


P_SIZE = 256
Q = 256
TR = 128
RB = 32
S = 32
NB = 16
QB = 8
CAP = 2
HALF = 16
GROUP = 32
LANES = 128

f32 = jnp.float32
bf16 = jnp.bfloat16
VMEM_LIMIT = 48 * 1024 * 1024
smem = pl.BlockSpec(memory_space=pltpu.SMEM)
vmem = pl.BlockSpec(memory_space=pltpu.VMEM)
hbm = pl.BlockSpec(memory_space=pl.ANY)
NN = (((1,), (0,)), ((), ()))
NT = (((1,), (1,)), ((), ()))


def halves(value):
    high = value.astype(bf16)
    return high, (value - high.astype(f32)).astype(bf16)


def dot(first, second, dims=NN):
    return lax.dot_general(first, second, dims, preferred_element_type=f32)


def product(first, second, dims=NN):
    first_high, first_low = halves(first)
    second_high, second_low = halves(second)
    return (
        dot(first_high, second_high, dims)
        + dot(first_high, second_low, dims)
        + dot(first_low, second_high, dims)
    )


def narrow_product(first, second):
    first_high, first_low = halves(first)
    second_high, second_low = halves(second)
    both = dot(first_high, jnp.concatenate([second_high, second_low], axis=1))
    return both[:, :LANES] + both[:, LANES:] + dot(first_low, second_high)


def complex_pair(first, second, dims=NN):
    real = product(first[0], second[0], dims) - product(first[1], second[1], dims)
    imag = product(first[0], second[1], dims) + product(first[1], second[0], dims)
    return real, imag


def lane_ids(rows):
    return lax.broadcasted_iota(jnp.int32, (rows, LANES), 1)


def turned(value):
    lanes = lane_ids(value.shape[0])
    ahead = pltpu.roll(value, LANES - HALF, 1)
    behind = pltpu.roll(value, HALF, 1)
    return jnp.where(lanes % GROUP < HALF, -ahead, behind)


def pick(group, choices):
    return jnp.where(
        group == 0,
        choices[0],
        jnp.where(group == 1, choices[1], jnp.where(group == 2, choices[2], choices[3])),
    )


def rotations(value):
    return [value] + [pltpu.roll(value, GROUP * turn, 1) for turn in (1, 2, 3)]


def spread_group(rolled, group, source):
    return pick(group, [rolled[(place - source) % 4] for place in range(4)])


def unpack(packed):
    count = packed.shape[0]
    flat = packed.reshape(count * 8, LANES)
    group = lane_ids(count * 8) // GROUP
    rolled = rotations(flat)
    parts = [spread_group(rolled, group, k).reshape(count, 8, LANES) for k in range(4)]
    return jnp.stack(parts, axis=1).reshape(count * RB, LANES)


def unpack_both(packed):
    count = packed.shape[0]
    flat = packed.reshape(count * 8, LANES)
    return unpack(packed), unpack(turned(flat).reshape(count, 8, LANES))


def pack(spread):
    count = spread.shape[0] // RB
    parts = spread.reshape(count, 4, 8, LANES)
    group = lax.broadcasted_iota(jnp.int32, (count, 8, LANES), 2) // GROUP
    return pick(group, [parts[:, k] for k in range(4)])


def slots_kernel(targets_ref, offsets_ref, slots_ref, slot_offsets_ref, used_ref):
    leaves = slot_offsets_ref.shape[0] // CAP
    for leaf in range(leaves):
        used_ref[leaf] = 0
    for slot in range(leaves * CAP):
        slot_offsets_ref[slot] = QB
    for block in range(NB):
        target = targets_ref[block]
        rank = used_ref[target]
        used_ref[target] = rank + 1
        slot = target * CAP + rank
        slots_ref[block] = slot
        slot_offsets_ref[slot] = offsets_ref[block]


def source_kernel(
    place_ref, down_ref, up_ref, leaf_ref, coupling_ref, own_u_ref, other_u_ref, own_y_ref, other_y_ref
):
    core = place_ref[0] % 2
    own_row = pl.multiple_of(core * HALF, HALF)
    other_row = pl.multiple_of((1 - core) * HALF, HALF)
    rows, turned_rows = [], []
    for source in (down_ref, up_ref):
        for start in (own_row, other_row):
            real = source[0, pl.ds(start, HALF), :]
            imag = source[1, pl.ds(start, HALF), :]
            rows += [real, imag]
            turned_rows += [-imag, real]
    y = product(leaf_ref[0], jnp.concatenate(rows, axis=0), NT) + product(
        leaf_ref[1], jnp.concatenate(turned_rows, axis=0), NT
    )
    u = narrow_product(coupling_ref[0], y) + narrow_product(coupling_ref[1], turned(y))
    rolled = rotations(y)
    y_group = lane_ids(P_SIZE) // GROUP
    parts = u.reshape(NB, 4, 8, LANES)
    u_group = lane_ids(NB * 8) // GROUP
    for sweep in range(2):
        for side, (u_ref, y_ref) in enumerate(((own_u_ref, own_y_ref), (other_u_ref, other_y_ref))):
            source = 2 * sweep + side
            y_ref[sweep] = spread_group(rolled, y_group, source)
            choices = []
            for k in range(4):
                part = parts[:, k].reshape(NB * 8, LANES)
                turn = (k - source) % 4
                choices.append(pltpu.roll(part, GROUP * turn, 1) if turn else part)
            u_ref[sweep] = pick(u_group, choices).reshape(NB, 8, LANES)


def operator_kernel(leaf_ref, coupling_ref, top_ref, bottom_ref, forward_ref, back_ref):
    leaf = (leaf_ref[0], leaf_ref[1])
    coupling = (coupling_ref[0], coupling_ref[1])
    inject = tuple(
        jnp.concatenate([top_ref[part], bottom_ref[part]], axis=0) for part in range(2)
    )
    local = complex_pair(leaf, inject, NT)
    update = complex_pair(coupling, local)
    for sweep in range(2):
        for part in range(2):
            columns = slice(sweep * TR, sweep * TR + TR)
            place = slice(part * TR, part * TR + TR)
            forward_ref[sweep, : NB * RB, place] = update[part][:, columns]
            forward_ref[sweep, NB * RB :, place] = local[part][:, columns]
    back = complex_pair(leaf, coupling, NT)
    back_ref[0] = back[0]
    back_ref[1] = back[1]


def stage_place(place_ref, stage):
    row = place_ref[0] // 2
    core = place_ref[0] % 2
    sweep = jnp.where(row == stage, 0, 1)
    first = jnp.where(sweep == core, 0, 1)
    return sweep, first


def start_either(choice, first_ref, second_ref, target_ref, semaphore):
    @pl.when(choice == 0)
    def _():
        pltpu.make_async_copy(first_ref, target_ref, semaphore).start()

    @pl.when(choice != 0)
    def _():
        pltpu.make_async_copy(second_ref, target_ref, semaphore).start()


def wait_for(source_ref, target_ref, semaphore):
    pltpu.make_async_copy(source_ref, target_ref, semaphore).wait()


def send_blocks(choice, own_slots_ref, other_slots_ref, packed, send_ref):
    for block in range(NB):
        slot = jnp.where(choice == 0, own_slots_ref[block], other_slots_ref[block])
        send_ref[slot] = packed[block]


def first_kernel(place_ref, own_slots_ref, other_slots_ref, own_u_ref, other_u_ref, send_ref):
    sweep, first = stage_place(place_ref, 0)
    packed = jnp.where(first == 0, own_u_ref[sweep], other_u_ref[sweep])
    send_blocks(first, own_slots_ref, other_slots_ref, packed, send_ref)


def separator_kernel(
    stage,
    step,
    place_ref,
    own_offsets_ref,
    other_offsets_ref,
    arrived_ref,
    own_sep_ref,
    other_sep_ref,
    reply_ref,
    sep_ref,
    even_ref,
    odd_ref,
    solved_ref,
    semaphore,
):
    sweep, first = stage_place(place_ref, stage)
    choice = first if step == 0 else 1 - first
    start_either(choice, own_sep_ref, other_sep_ref, sep_ref, semaphore)
    slots = arrived_ref.shape[0]
    even_ref[...] = jnp.zeros_like(even_ref)
    odd_ref[...] = jnp.zeros_like(odd_ref)
    places = []
    for slot in range(slots):
        place = jnp.where(choice == 0, own_offsets_ref[slot], other_offsets_ref[slot])
        places.append(place)
        total_ref = odd_ref if slot % 2 else even_ref
        total_ref[place] = total_ref[place] + arrived_ref[slot]
    rhs, rhs_turned = unpack_both(even_ref[:QB] + odd_ref[:QB])
    wait_for(own_sep_ref, sep_ref, semaphore)
    solved = narrow_product(sep_ref[0], rhs) + narrow_product(sep_ref[1], rhs_turned)
    solved_ref[:QB] = pack(solved)
    solved_ref[QB] = jnp.zeros((8, LANES), f32)
    for slot in range(slots):
        reply_ref[slot] = solved_ref[places[slot]]


def leaf_finish(choice, own_slots_ref, other_slots_ref, returned_ref, back_ref, wait, base):
    blocks = []
    for block in range(NB):
        slot = jnp.where(choice == 0, own_slots_ref[block], other_slots_ref[block])
        blocks.append(returned_ref[slot])
    mine, mine_turned = unpack_both(jnp.stack(blocks, axis=0))
    wait()
    return base + narrow_product(back_ref[0], mine) + narrow_product(back_ref[1], mine_turned)


def leaf_begin(sweep, choice, trace, trace_turned, forward, u_refs, y_refs, slots_refs, send_ref, base_ref):
    driven = narrow_product(forward, jnp.concatenate([trace, trace_turned], axis=0))
    packed = pack(driven[: NB * RB]) + jnp.where(choice == 0, u_refs[0][sweep], u_refs[1][sweep])
    send_blocks(choice, slots_refs[0], slots_refs[1], packed, send_ref)
    base_ref[...] = driven[NB * RB :] + jnp.where(choice == 0, y_refs[0][sweep], y_refs[1][sweep])


def middle_kernel(
    stage,
    place_ref,
    own_slots_ref,
    other_slots_ref,
    returned_ref,
    base_refs,
    own_u_ref,
    other_u_ref,
    own_y_ref,
    other_y_ref,
    own_back_ref,
    other_back_ref,
    own_forward_ref,
    other_forward_ref,
    field_ref,
    send_ref,
    next_base_ref,
    back_ref,
    forward_ref,
    semaphores,
):
    sweep, first = stage_place(place_ref, stage)
    second = 1 - first
    start_either(first, own_back_ref, other_back_ref, back_ref, semaphores.at[0])
    start_either(
        second, own_forward_ref.at[sweep], other_forward_ref.at[sweep], forward_ref, semaphores.at[1]
    )
    if len(base_refs) == 1:
        base = base_refs[0][...]
    else:
        base = jnp.where(first == 0, own_y_ref[sweep], other_y_ref[sweep])
    field_ref[...] = leaf_finish(
        first,
        own_slots_ref,
        other_slots_ref,
        returned_ref,
        back_ref,
        lambda: wait_for(own_back_ref, back_ref, semaphores.at[0]),
        base,
    )
    trace = field_ref[pl.ds(pl.multiple_of((1 - sweep) * TR, TR), TR), :]
    wait_for(own_forward_ref.at[0], forward_ref, semaphores.at[1])
    leaf_begin(
        sweep,
        second,
        trace,
        turned(trace),
        forward_ref[...],
        (own_u_ref, other_u_ref),
        (own_y_ref, other_y_ref),
        (own_slots_ref, other_slots_ref),
        send_ref,
        next_base_ref,
    )


def last_kernel(
    stage,
    place_ref,
    own_slots_ref,
    other_slots_ref,
    returned_ref,
    base_ref,
    own_back_ref,
    other_back_ref,
    field_ref,
    trace_ref,
    back_ref,
    semaphore,
):
    sweep, first = stage_place(place_ref, stage)
    second = 1 - first
    start_either(second, own_back_ref, other_back_ref, back_ref, semaphore)
    field_ref[...] = leaf_finish(
        second,
        own_slots_ref,
        other_slots_ref,
        returned_ref,
        back_ref,
        lambda: wait_for(own_back_ref, back_ref, semaphore),
        base_ref[...],
    )
    trace_ref[...] = pack(field_ref[pl.ds(pl.multiple_of((1 - sweep) * TR, TR), TR), :])


def enter_kernel(
    stage,
    place_ref,
    own_slots_ref,
    other_slots_ref,
    trace_ref,
    own_u_ref,
    other_u_ref,
    own_y_ref,
    other_y_ref,
    own_forward_ref,
    other_forward_ref,
    send_ref,
    next_base_ref,
    forward_ref,
    semaphore,
):
    sweep, first = stage_place(place_ref, stage)
    start_either(
        first, own_forward_ref.at[sweep], other_forward_ref.at[sweep], forward_ref, semaphore
    )
    trace, trace_turned = unpack_both(trace_ref[...])
    wait_for(own_forward_ref.at[0], forward_ref, semaphore)
    leaf_begin(
        sweep,
        first,
        trace,
        trace_turned,
        forward_ref[...],
        (own_u_ref, other_u_ref),
        (own_y_ref, other_y_ref),
        (own_slots_ref, other_slots_ref),
        send_ref,
        next_base_ref,
    )


def collect_kernel(place_ref, field_refs, own_ref, other_ref, parts_ref, semaphores):
    row = place_ref[0] // 2
    core = place_ref[0] % 2
    for sweep in range(2):
        for position in range(2):
            layer = position if sweep == 0 else 1 - position
            side = jnp.where(core == layer, 0, 1)
            for stage in range(4):
                active = row == stage if sweep == 0 else row == 3 - stage

                @pl.when(active)
                def _():
                    pltpu.make_async_copy(
                        field_refs[2 * stage + position],
                        parts_ref.at[2 * sweep + side],
                        semaphores.at[2 * sweep + position],
                    ).start()

    for index in range(4):
        wait_for(field_refs[0], parts_ref.at[0], semaphores.at[index])
    group = lane_ids(P_SIZE) // GROUP
    joined = pick(group, [parts_ref[index] for index in range(4)])
    rows = joined.T.reshape(2, 2, 2, HALF, P_SIZE)
    own_ref[...] = rows[:, 0]
    other_ref[...] = rows[:, 1]


def output_kernel(place_ref, own_ref, other_ref, down_ref, up_ref):
    core = place_ref[0] % 2
    for sweep, field_ref in enumerate((down_ref, up_ref)):
        for part in range(2):
            field_ref[part, pl.ds(pl.multiple_of(core * HALF, HALF), HALF), :] = own_ref[sweep, part]
            field_ref[part, pl.ds(pl.multiple_of((1 - core) * HALF, HALF), HALF), :] = other_ref[
                sweep, part
            ]


def call(kernel, outs, in_specs, out_specs, scratch=(), cost=None):
    return pl.pallas_call(
        kernel,
        out_shape=outs,
        in_specs=in_specs,
        out_specs=out_specs,
        scratch_shapes=list(scratch),
        compiler_params=pltpu.CompilerParams(vmem_limit_bytes=VMEM_LIMIT),
        cost_estimate=cost,
    )


def shape(*dims, dtype=f32):
    return jax.ShapeDtypeStruct(dims, dtype)


def cost_of(flops, size):
    return pl.CostEstimate(flops=flops, bytes_accessed=size, transcendentals=0)


def across_cores(value):
    layers = lax.axis_size("layer")
    return lax.ppermute(value, "layer", [(index, index ^ 1) for index in range(layers)])


def exchange(value):
    return lax.all_to_all(value, "front", split_axis=0, concat_axis=0, tiled=True)


def to_next_stage(value, stage):
    moves = [(stage, stage + 1), (3 - stage, 2 - stage)]
    pairs = [(2 * a + core, 2 * b + core) for a, b in moves for core in range(2)]
    return lax.ppermute(value, "layer", pairs)


def body(
    sources_down,
    sources_up,
    leaf_inverse,
    coupling,
    sep_inverse,
    inject_top,
    inject_bottom,
    targets,
    offsets,
):
    leaves = lax.axis_size("front")
    slots = leaves * CAP
    place = lax.axis_index("layer").reshape(1).astype(jnp.int32)
    leaf = leaf_inverse[0, 0]
    rows = coupling[0, 0]
    sep = sep_inverse[0, 0]

    own_slots, slot_offsets = call(
        slots_kernel,
        (shape(NB, dtype=jnp.int32), shape(slots, dtype=jnp.int32)),
        [smem, smem],
        (smem, smem),
        [pltpu.SMEM((leaves,), jnp.int32)],
    )(targets[0, 0, :, 0], offsets[0, 0])
    own_offsets = exchange(slot_offsets.reshape(leaves, CAP)).reshape(slots)
    other_slots = across_cores(own_slots)
    other_offsets = across_cores(own_offsets)

    u_shape = shape(2, NB, 8, LANES)
    y_shape = shape(2, P_SIZE, LANES)
    own_u, to_other_u, own_y, to_other_y = call(
        source_kernel,
        (u_shape, u_shape, y_shape, y_shape),
        [smem] + [vmem] * 4,
        (vmem,) * 4,
        cost=cost_of(600_000_000, 2_500_000),
    )(place, sources_down[0, 0], sources_up[0, 0], leaf, rows)
    other_u = across_cores(to_other_u)
    other_y = across_cores(to_other_y)

    own_forward, own_back = call(
        operator_kernel,
        (shape(2, NB * RB + P_SIZE, 2 * TR), shape(2, P_SIZE, NB * RB)),
        [vmem] * 4,
        (vmem,) * 2,
        cost=cost_of(4_000_000_000, 5_000_000),
    )(leaf, rows, inject_top[0, 0], inject_bottom[0, 0])
    other_forward = across_cores(own_forward)
    other_back = across_cores(own_back)
    other_sep = across_cores(sep)

    slot_shape = shape(slots, 8, LANES)
    field_shape = shape(P_SIZE, LANES)
    back_scratch = pltpu.VMEM((2, P_SIZE, NB * RB), f32)
    forward_scratch = pltpu.VMEM((NB * RB + P_SIZE, 2 * TR), f32)

    def separator(stage, step, arrived):
        return call(
            functools.partial(separator_kernel, stage, step),
            slot_shape,
            [smem] * 3 + [vmem] + [hbm] * 2,
            vmem,
            [
                pltpu.VMEM((2, Q, Q), f32),
                pltpu.VMEM((QB + 1, 8, LANES), f32),
                pltpu.VMEM((QB + 1, 8, LANES), f32),
                pltpu.VMEM((QB + 1, 8, LANES), f32),
                pltpu.SemaphoreType.DMA,
            ],
            cost_of(100_000_000, 1_100_000),
        )(place, own_offsets, other_offsets, arrived, sep, other_sep)

    fields = []
    base = None
    trace = None
    for stage in range(4):
        if stage == 0:
            send = call(first_kernel, slot_shape, [smem] * 3 + [vmem] * 2, vmem)(
                place, own_slots, other_slots, own_u, other_u
            )
        else:
            send, base = call(
                functools.partial(enter_kernel, stage),
                (slot_shape, field_shape),
                [smem] * 3 + [vmem] * 5 + [hbm] * 2,
                (vmem, vmem),
                [forward_scratch, pltpu.SemaphoreType.DMA],
                cost_of(100_000_000, 2_000_000),
            )(
                place,
                own_slots,
                other_slots,
                trace,
                own_u,
                other_u,
                own_y,
                other_y,
                own_forward,
                other_forward,
            )
        returned = exchange(separator(stage, 0, exchange(send)))
        bases = [] if base is None else [base]

        def middle(*refs, stage=stage, count=len(bases)):
            head, rest = refs[:4], refs[4:]
            middle_kernel(stage, *head, rest[:count], *rest[count:])

        field, send, base = call(
            middle,
            (field_shape, slot_shape, field_shape),
            [smem] * 3 + [vmem] * (1 + len(bases)) + [vmem] * 4 + [hbm] * 4,
            (vmem,) * 3,
            [back_scratch, forward_scratch, pltpu.SemaphoreType.DMA((2,))],
            cost_of(300_000_000, 3_000_000),
        )(
            place,
            own_slots,
            other_slots,
            returned,
            *bases,
            own_u,
            other_u,
            own_y,
            other_y,
            own_back,
            other_back,
            own_forward,
            other_forward,
        )
        fields.append(field)
        returned = exchange(separator(stage, 1, exchange(send)))
        field, trace = call(
            functools.partial(last_kernel, stage),
            (field_shape, shape(TR // RB, 8, LANES)),
            [smem] * 3 + [vmem] * 2 + [hbm] * 2,
            (vmem, vmem),
            [back_scratch, pltpu.SemaphoreType.DMA],
            cost_of(200_000_000, 2_000_000),
        )(place, own_slots, other_slots, returned, base, own_back, other_back)
        fields.append(field)
        if stage < 3:
            trace = to_next_stage(trace, stage)

    half_shape = shape(2, 2, HALF, P_SIZE)

    def collect(place_ref, *refs):
        collect_kernel(place_ref, refs[:8], *refs[8:])

    own, to_other = call(
        collect,
        (half_shape, half_shape),
        [smem] + [hbm] * 8,
        (vmem, vmem),
        [pltpu.VMEM((4, P_SIZE, LANES), f32), pltpu.SemaphoreType.DMA((4,))],
    )(place, *fields)
    down, up = call(
        output_kernel,
        (shape(2, S, P_SIZE), shape(2, S, P_SIZE)),
        [smem, vmem, vmem],
        (vmem, vmem),
    )(place, own, across_cores(to_other))
    return down[None, None], up[None, None]


def solution(mesh):
    whole = P("layer", "front", None, None, None)
    return jax.shard_map(
        body,
        mesh=mesh,
        in_specs=(whole,) * 7 + (P("layer", "front", None, None), P("layer", "front", None)),
        out_specs=(whole, whole),
        check_vma=False,
    )
```

```python
import functools

import jax
import jax.numpy as jnp
from jax import lax
from jax.experimental import pallas as pl
from jax.experimental.pallas import tpu as pltpu
from jax.sharding import PartitionSpec as P


P_SIZE = 256
Q = 256
TR = 128
RB = 32
S = 32
NB = 16
QB = 8
CAP = 2
HALF = 16
GROUP = 32
LANES = 128

f32 = jnp.float32
bf16 = jnp.bfloat16
VMEM_LIMIT = 48 * 1024 * 1024
ALMOST_ALL_VMEM = 60 * 1024 * 1024
smem = pl.BlockSpec(memory_space=pltpu.SMEM)
vmem = pl.BlockSpec(memory_space=pltpu.VMEM)
hbm = pl.BlockSpec(memory_space=pl.ANY)
NN = (((1,), (0,)), ((), ()))
NT = (((1,), (1,)), ((), ()))


def halves(value):
    high = value.astype(bf16)
    return high, (value - high.astype(f32)).astype(bf16)


def dot(first, second, dims=NN):
    return lax.dot_general(first, second, dims, preferred_element_type=f32)


def product(first, second, dims=NN):
    first_high, first_low = halves(first)
    second_high, second_low = halves(second)
    return (
        dot(first_high, second_high, dims)
        + dot(first_high, second_low, dims)
        + dot(first_low, second_high, dims)
    )


def narrow_product(first, second):
    first_high, first_low = halves(first)
    second_high, second_low = halves(second)
    both = dot(first_high, jnp.concatenate([second_high, second_low], axis=1))
    return both[:, :LANES] + both[:, LANES:] + dot(first_low, second_high)


def complex_pair(first, second, dims=NN):
    real = product(first[0], second[0], dims) - product(first[1], second[1], dims)
    imag = product(first[0], second[1], dims) + product(first[1], second[0], dims)
    return real, imag


def lane_ids(rows):
    return lax.broadcasted_iota(jnp.int32, (rows, LANES), 1)


def turned(value):
    lanes = lane_ids(value.shape[0])
    ahead = pltpu.roll(value, LANES - HALF, 1)
    behind = pltpu.roll(value, HALF, 1)
    return jnp.where(lanes % GROUP < HALF, -ahead, behind)


def pick(group, choices):
    return jnp.where(
        group == 0,
        choices[0],
        jnp.where(group == 1, choices[1], jnp.where(group == 2, choices[2], choices[3])),
    )


def rotations(value):
    return [value] + [pltpu.roll(value, GROUP * turn, 1) for turn in (1, 2, 3)]


def spread_group(rolled, group, source):
    return pick(group, [rolled[(place - source) % 4] for place in range(4)])


def unpack(packed):
    count = packed.shape[0]
    flat = packed.reshape(count * 8, LANES)
    group = lane_ids(count * 8) // GROUP
    rolled = rotations(flat)
    parts = [spread_group(rolled, group, k).reshape(count, 8, LANES) for k in range(4)]
    return jnp.stack(parts, axis=1).reshape(count * RB, LANES)


def unpack_both(packed):
    count = packed.shape[0]
    flat = packed.reshape(count * 8, LANES)
    return unpack(packed), unpack(turned(flat).reshape(count, 8, LANES))


def pack(spread):
    count = spread.shape[0] // RB
    parts = spread.reshape(count, 4, 8, LANES)
    group = lax.broadcasted_iota(jnp.int32, (count, 8, LANES), 2) // GROUP
    return pick(group, [parts[:, k] for k in range(4)])


def source_kernel(
    place_ref,
    down_hbm,
    up_hbm,
    leaf_hbm,
    coupling_hbm,
    own_u_ref,
    other_u_ref,
    own_y_ref,
    other_y_ref,
    down_ref,
    up_ref,
    leaf_ref,
    coupling_ref,
    semaphores,
):
    copies = [
        pltpu.make_async_copy(source, target, semaphores.at[index])
        for index, (source, target) in enumerate(
            (
                (down_hbm, down_ref),
                (up_hbm, up_ref),
                (leaf_hbm, leaf_ref),
                (coupling_hbm, coupling_ref),
            )
        )
    ]
    for copy in copies:
        copy.start()
    core = place_ref[0] % 2
    own_row = pl.multiple_of(core * HALF, HALF)
    other_row = pl.multiple_of((1 - core) * HALF, HALF)
    copies[0].wait()
    copies[1].wait()
    rows, turned_rows = [], []
    for source in (down_ref, up_ref):
        for start in (own_row, other_row):
            real = source[0, pl.ds(start, HALF), :]
            imag = source[1, pl.ds(start, HALF), :]
            rows += [real, imag]
            turned_rows += [-imag, real]
    copies[2].wait()
    y = product(leaf_ref[0], jnp.concatenate(rows, axis=0), NT) + product(
        leaf_ref[1], jnp.concatenate(turned_rows, axis=0), NT
    )
    rolled = rotations(y)
    y_group = lane_ids(P_SIZE) // GROUP
    for sweep in range(2):
        for side, y_ref in enumerate((own_y_ref, other_y_ref)):
            y_ref[sweep] = spread_group(rolled, y_group, 2 * sweep + side)
    copies[3].wait()
    u = narrow_product(coupling_ref[0], y) + narrow_product(coupling_ref[1], turned(y))
    parts = u.reshape(NB, 4, 8, LANES)
    u_group = lane_ids(NB * 8) // GROUP
    for sweep in range(2):
        for side, u_ref in enumerate((own_u_ref, other_u_ref)):
            choices = []
            for k in range(4):
                part = parts[:, k].reshape(NB * 8, LANES)
                turn = (k - 2 * sweep - side) % 4
                choices.append(pltpu.roll(part, GROUP * turn, 1) if turn else part)
            u_ref[sweep] = pick(u_group, choices).reshape(NB, 8, LANES)


def operator_kernel(
    after_ref,
    leaf_hbm,
    coupling_hbm,
    top_hbm,
    bottom_hbm,
    forward_ref,
    back_ref,
    leaf_ref,
    coupling_ref,
    top_ref,
    bottom_ref,
    semaphores,
):
    copies = [
        pltpu.make_async_copy(source, target, semaphores.at[index])
        for index, (source, target) in enumerate(
            (
                (leaf_hbm, leaf_ref),
                (top_hbm, top_ref),
                (bottom_hbm, bottom_ref),
                (coupling_hbm, coupling_ref),
            )
        )
    ]
    for copy in copies:
        copy.start()
    for copy in copies[:3]:
        copy.wait()
    leaf = (leaf_ref[0], leaf_ref[1])
    inject = tuple(
        jnp.concatenate([top_ref[part], bottom_ref[part]], axis=0) for part in range(2)
    )
    local = complex_pair(leaf, inject, NT)
    copies[3].wait()
    coupling = (coupling_ref[0], coupling_ref[1])
    update = complex_pair(coupling, local)
    for sweep in range(2):
        for part in range(2):
            columns = slice(sweep * TR, sweep * TR + TR)
            place = slice(part * TR, part * TR + TR)
            forward_ref[sweep, : NB * RB, place] = update[part][:, columns]
            forward_ref[sweep, NB * RB :, place] = local[part][:, columns]
    back = complex_pair(leaf, coupling, NT)
    back_ref[0] = back[0]
    back_ref[1] = back[1]


def stage_place(place_ref, stage):
    row = place_ref[0] // 2
    core = place_ref[0] % 2
    sweep = jnp.where(row == stage, 0, 1)
    first = jnp.where(sweep == core, 0, 1)
    return sweep, first


def start_either(choice, first_ref, second_ref, target_ref, semaphore):
    @pl.when(choice == 0)
    def _():
        pltpu.make_async_copy(first_ref, target_ref, semaphore).start()

    @pl.when(choice != 0)
    def _():
        pltpu.make_async_copy(second_ref, target_ref, semaphore).start()


def wait_for(source_ref, target_ref, semaphore):
    pltpu.make_async_copy(source_ref, target_ref, semaphore).wait()


def send_blocks(choice, own_slots_ref, other_slots_ref, packed, send_ref):
    for block in range(NB):
        slot = jnp.where(choice == 0, own_slots_ref[block], other_slots_ref[block])
        send_ref[slot] = packed[block]


def first_kernel(
    place_ref,
    own_targets_ref,
    other_targets_ref,
    own_offsets_ref,
    other_offsets_ref,
    own_u_ref,
    other_u_ref,
    own_slots_ref,
    other_slots_ref,
    send_ref,
):
    leaves = send_ref.shape[0]
    sweep, first = stage_place(place_ref, 0)
    lanes = lane_ids(leaves)
    rows = lax.broadcasted_iota(jnp.int32, (leaves, LANES), 0)
    notes = jnp.full((leaves, LANES), QB, jnp.int32)
    all_slots = []
    for side, (targets_ref, offsets_ref, slots_ref) in enumerate(
        (
            (own_targets_ref, own_offsets_ref, own_slots_ref),
            (other_targets_ref, other_offsets_ref, other_slots_ref),
        )
    ):
        targets = [targets_ref[block] for block in range(NB)]
        slots = []
        for block in range(NB):
            rank = jnp.int32(0)
            for earlier in range(block):
                rank = rank + jnp.where(targets[earlier] == targets[block], 1, 0)
            slot = targets[block] * CAP + rank
            slots_ref[block] = slot
            slots.append(slot)
            here = (rows == targets[block]) & (lanes == CAP * side + rank)
            notes = jnp.where(here, offsets_ref[block], notes)
        all_slots.append(slots)
    send_ref[:, CAP * 8 :, :] = jnp.broadcast_to(
        notes.astype(f32)[:, None, :], (leaves, 8, LANES)
    )
    packed = jnp.where(first == 0, own_u_ref[sweep], other_u_ref[sweep])
    for block in range(NB):
        slot = jnp.where(first == 0, all_slots[0][block], all_slots[1][block])
        row = pl.multiple_of((slot % CAP) * 8, 8)
        send_ref[slot // CAP, pl.ds(row, 8), :] = packed[block]


def separator_solve(choice, offsets_ref, arrived, reply_ref, sep, even_ref, odd_ref, solved_ref):
    leaves = reply_ref.shape[0] // CAP
    even_ref[...] = jnp.zeros_like(even_ref)
    odd_ref[...] = jnp.zeros_like(odd_ref)
    places = []
    for leaf in range(leaves):
        for rank, total_ref in enumerate((even_ref, odd_ref)):
            place = offsets_ref[CAP * choice + rank, leaf]
            places.append(place)
            total_ref[place] = total_ref[place] + arrived(leaf, rank)
    rhs, rhs_turned = unpack_both(even_ref[:QB] + odd_ref[:QB])
    sep_ref = sep()
    solved = narrow_product(sep_ref[0], rhs) + narrow_product(sep_ref[1], rhs_turned)
    solved_ref[:QB] = pack(solved)
    solved_ref[QB] = jnp.zeros((8, LANES), f32)
    for slot, place in enumerate(places):
        reply_ref[slot] = solved_ref[place]


def separator_kernel(
    stage,
    step,
    place_ref,
    offsets_ref,
    arrived_ref,
    own_sep_ref,
    other_sep_ref,
    reply_ref,
    sep_ref,
    even_ref,
    odd_ref,
    solved_ref,
    semaphore,
):
    sweep, first = stage_place(place_ref, stage)
    choice = first if step == 0 else 1 - first
    start_either(choice, own_sep_ref, other_sep_ref, sep_ref, semaphore)

    def sep():
        wait_for(own_sep_ref, sep_ref, semaphore)
        return sep_ref

    separator_solve(
        choice,
        offsets_ref,
        lambda leaf, rank: arrived_ref[CAP * leaf + rank],
        reply_ref,
        sep,
        even_ref,
        odd_ref,
        solved_ref,
    )


def first_separator_kernel(
    place_ref,
    arrived_ref,
    own_sep_ref,
    other_sep_ref,
    offsets_ref,
    reply_ref,
    sep_ref,
    even_ref,
    odd_ref,
    solved_ref,
    notes_ref,
    semaphores,
):
    sweep, first = stage_place(place_ref, 0)
    start_either(first, own_sep_ref, other_sep_ref, sep_ref, semaphores.at[0])
    leaves = arrived_ref.shape[0]
    notes = arrived_ref[:, CAP * 8, :]
    whole = jnp.concatenate([notes, jnp.zeros((LANES - leaves, LANES), f32)], axis=0)
    notes_ref[...] = whole.T[:8].astype(jnp.int32)
    copy = pltpu.make_async_copy(notes_ref, offsets_ref, semaphores.at[1])
    copy.start()
    copy.wait()

    def sep():
        wait_for(own_sep_ref, sep_ref, semaphores.at[0])
        return sep_ref

    separator_solve(
        first,
        offsets_ref,
        lambda leaf, rank: arrived_ref[leaf, 8 * rank : 8 * rank + 8, :],
        reply_ref,
        sep,
        even_ref,
        odd_ref,
        solved_ref,
    )


def leaf_finish(choice, own_slots_ref, other_slots_ref, returned_ref, back_ref, wait, base):
    blocks = []
    for block in range(NB):
        slot = jnp.where(choice == 0, own_slots_ref[block], other_slots_ref[block])
        blocks.append(returned_ref[slot])
    mine, mine_turned = unpack_both(jnp.stack(blocks, axis=0))
    wait()
    return base + narrow_product(back_ref[0], mine) + narrow_product(back_ref[1], mine_turned)


def leaf_begin(sweep, choice, trace, trace_turned, forward, u_refs, y_refs, slots_refs, send_ref, base_ref):
    driven = narrow_product(forward, jnp.concatenate([trace, trace_turned], axis=0))
    packed = pack(driven[: NB * RB]) + jnp.where(choice == 0, u_refs[0][sweep], u_refs[1][sweep])
    send_blocks(choice, slots_refs[0], slots_refs[1], packed, send_ref)
    base_ref[...] = driven[NB * RB :] + jnp.where(choice == 0, y_refs[0][sweep], y_refs[1][sweep])


def middle_kernel(
    stage,
    place_ref,
    own_slots_ref,
    other_slots_ref,
    returned_ref,
    base_refs,
    own_u_ref,
    other_u_ref,
    own_y_ref,
    other_y_ref,
    own_back_ref,
    other_back_ref,
    own_forward_ref,
    other_forward_ref,
    field_ref,
    send_ref,
    next_base_ref,
    back_ref,
    forward_ref,
    semaphores,
):
    sweep, first = stage_place(place_ref, stage)
    second = 1 - first
    start_either(first, own_back_ref, other_back_ref, back_ref, semaphores.at[0])
    start_either(
        second, own_forward_ref.at[sweep], other_forward_ref.at[sweep], forward_ref, semaphores.at[1]
    )
    if len(base_refs) == 1:
        base = base_refs[0][...]
    else:
        base = jnp.where(first == 0, own_y_ref[sweep], other_y_ref[sweep])
    field_ref[...] = leaf_finish(
        first,
        own_slots_ref,
        other_slots_ref,
        returned_ref,
        back_ref,
        lambda: wait_for(own_back_ref, back_ref, semaphores.at[0]),
        base,
    )
    trace = field_ref[pl.ds(pl.multiple_of((1 - sweep) * TR, TR), TR), :]
    wait_for(own_forward_ref.at[0], forward_ref, semaphores.at[1])
    leaf_begin(
        sweep,
        second,
        trace,
        turned(trace),
        forward_ref[...],
        (own_u_ref, other_u_ref),
        (own_y_ref, other_y_ref),
        (own_slots_ref, other_slots_ref),
        send_ref,
        next_base_ref,
    )


def last_kernel(
    stage,
    place_ref,
    own_slots_ref,
    other_slots_ref,
    returned_ref,
    base_ref,
    own_back_ref,
    other_back_ref,
    field_ref,
    trace_ref,
    back_ref,
    semaphore,
):
    sweep, first = stage_place(place_ref, stage)
    second = 1 - first
    start_either(second, own_back_ref, other_back_ref, back_ref, semaphore)
    field_ref[...] = leaf_finish(
        second,
        own_slots_ref,
        other_slots_ref,
        returned_ref,
        back_ref,
        lambda: wait_for(own_back_ref, back_ref, semaphore),
        base_ref[...],
    )
    trace_ref[...] = pack(field_ref[pl.ds(pl.multiple_of((1 - sweep) * TR, TR), TR), :])


def enter_kernel(
    stage,
    place_ref,
    own_slots_ref,
    other_slots_ref,
    trace_ref,
    own_u_ref,
    other_u_ref,
    own_y_ref,
    other_y_ref,
    own_forward_ref,
    other_forward_ref,
    send_ref,
    next_base_ref,
    forward_ref,
    semaphore,
):
    sweep, first = stage_place(place_ref, stage)
    start_either(
        first, own_forward_ref.at[sweep], other_forward_ref.at[sweep], forward_ref, semaphore
    )
    trace, trace_turned = unpack_both(trace_ref[...])
    wait_for(own_forward_ref.at[0], forward_ref, semaphore)
    leaf_begin(
        sweep,
        first,
        trace,
        trace_turned,
        forward_ref[...],
        (own_u_ref, other_u_ref),
        (own_y_ref, other_y_ref),
        (own_slots_ref, other_slots_ref),
        send_ref,
        next_base_ref,
    )


def collect_kernel(place_ref, field_refs, own_ref, other_ref, parts_ref, semaphores):
    row = place_ref[0] // 2
    core = place_ref[0] % 2
    for sweep in range(2):
        for position in range(2):
            layer = position if sweep == 0 else 1 - position
            side = jnp.where(core == layer, 0, 1)
            for stage in range(4):
                active = row == stage if sweep == 0 else row == 3 - stage

                @pl.when(active)
                def _():
                    pltpu.make_async_copy(
                        field_refs[2 * stage + position],
                        parts_ref.at[2 * sweep + side],
                        semaphores.at[2 * sweep + position],
                    ).start()

    for index in range(4):
        wait_for(field_refs[0], parts_ref.at[0], semaphores.at[index])
    group = lane_ids(P_SIZE) // GROUP
    joined = pick(group, [parts_ref[index] for index in range(4)])
    rows = joined.T.reshape(2, 2, 2, HALF, P_SIZE)
    own_ref[...] = rows[:, 0]
    other_ref[...] = rows[:, 1]


def output_kernel(place_ref, own_ref, other_ref, down_ref, up_ref):
    core = place_ref[0] % 2
    for sweep, field_ref in enumerate((down_ref, up_ref)):
        for part in range(2):
            field_ref[part, pl.ds(pl.multiple_of(core * HALF, HALF), HALF), :] = own_ref[sweep, part]
            field_ref[part, pl.ds(pl.multiple_of((1 - core) * HALF, HALF), HALF), :] = other_ref[
                sweep, part
            ]


def call(kernel, outs, in_specs, out_specs, scratch=(), cost=None, limit=VMEM_LIMIT):
    return pl.pallas_call(
        kernel,
        out_shape=outs,
        in_specs=in_specs,
        out_specs=out_specs,
        scratch_shapes=list(scratch),
        compiler_params=pltpu.CompilerParams(vmem_limit_bytes=limit),
        cost_estimate=cost,
    )


def shape(*dims, dtype=f32):
    return jax.ShapeDtypeStruct(dims, dtype)


def cost_of(flops, size):
    return pl.CostEstimate(flops=flops, bytes_accessed=size, transcendentals=0)


def across_cores(value):
    layers = lax.axis_size("layer")
    return lax.ppermute(value, "layer", [(index, index ^ 1) for index in range(layers)])


def exchange(value):
    return lax.all_to_all(value, "front", split_axis=0, concat_axis=0, tiled=True)


def to_next_stage(value, stage):
    moves = [(stage, stage + 1), (3 - stage, 2 - stage)]
    pairs = [(2 * a + core, 2 * b + core) for a, b in moves for core in range(2)]
    return lax.ppermute(value, "layer", pairs)


def body(
    sources_down,
    sources_up,
    leaf_inverse,
    coupling,
    sep_inverse,
    inject_top,
    inject_bottom,
    targets,
    offsets,
):
    leaves = lax.axis_size("front")
    slots = leaves * CAP
    place = lax.axis_index("layer").reshape(1).astype(jnp.int32)
    leaf = leaf_inverse[0, 0]
    rows = coupling[0, 0]
    sep = sep_inverse[0, 0]
    own_targets = targets[0, 0, :, 0]
    other_targets = across_cores(own_targets)
    other_offsets = across_cores(offsets[0, 0])
    other_sep = across_cores(sep)

    source_scratch = pltpu.VMEM((2, S, P_SIZE), f32)
    leaf_scratch = pltpu.VMEM((2, P_SIZE, P_SIZE), f32)
    rows_scratch = pltpu.VMEM((2, NB * RB, P_SIZE), f32)
    inject_scratch = pltpu.VMEM((2, TR, P_SIZE), f32)
    u_shape = shape(2, NB, 8, LANES)
    y_shape = shape(2, P_SIZE, LANES)
    own_u, to_other_u, own_y, to_other_y = call(
        source_kernel,
        (u_shape, u_shape, y_shape, y_shape),
        [smem] + [hbm] * 4,
        (vmem,) * 4,
        [
            source_scratch,
            source_scratch,
            leaf_scratch,
            rows_scratch,
            pltpu.SemaphoreType.DMA((4,)),
        ],
        cost_of(600_000_000, 2_500_000),
        ALMOST_ALL_VMEM,
    )(place, sources_down[0, 0], sources_up[0, 0], leaf, rows)
    other_u = across_cores(to_other_u)

    own_forward, own_back = call(
        operator_kernel,
        (shape(2, NB * RB + P_SIZE, 2 * TR), shape(2, P_SIZE, NB * RB)),
        [hbm] * 5,
        (vmem,) * 2,
        [
            leaf_scratch,
            rows_scratch,
            inject_scratch,
            inject_scratch,
            pltpu.SemaphoreType.DMA((4,)),
        ],
        cost_of(4_000_000_000, 5_000_000),
        ALMOST_ALL_VMEM,
    )(to_other_u, leaf, rows, inject_top[0, 0], inject_bottom[0, 0])
    other_y = across_cores(to_other_y)
    other_back = across_cores(own_back)
    other_forward = across_cores(own_forward)

    slot_shape = shape(slots, 8, LANES)
    field_shape = shape(P_SIZE, LANES)
    slots_shape = shape(NB, dtype=jnp.int32)
    back_scratch = pltpu.VMEM((2, P_SIZE, NB * RB), f32)
    forward_scratch = pltpu.VMEM((NB * RB + P_SIZE, 2 * TR), f32)
    separator_scratch = [
        pltpu.VMEM((2, Q, Q), f32),
        pltpu.VMEM((QB + 1, 8, LANES), f32),
        pltpu.VMEM((QB + 1, 8, LANES), f32),
        pltpu.VMEM((QB + 1, 8, LANES), f32),
    ]

    own_slots, other_slots, send = call(
        first_kernel,
        (slots_shape, slots_shape, shape(leaves, (CAP + 1) * 8, LANES)),
        [smem] * 5 + [vmem] * 2,
        (smem, smem, vmem),
    )(place, own_targets, other_targets, offsets[0, 0], other_offsets, own_u, other_u)
    places, reply = call(
        first_separator_kernel,
        (shape(8, LANES, dtype=jnp.int32), slot_shape),
        [smem, vmem, hbm, hbm],
        (smem, vmem),
        separator_scratch
        + [pltpu.VMEM((8, LANES), jnp.int32), pltpu.SemaphoreType.DMA((2,))],
        cost_of(100_000_000, 1_100_000),
    )(place, exchange(send), sep, other_sep)

    def separator(stage, step, arrived):
        return call(
            functools.partial(separator_kernel, stage, step),
            slot_shape,
            [smem] * 2 + [vmem] + [hbm] * 2,
            vmem,
            separator_scratch + [pltpu.SemaphoreType.DMA],
            cost_of(100_000_000, 1_100_000),
        )(place, places, arrived, sep, other_sep)

    fields = []
    base = None
    trace = None
    for stage in range(4):
        if stage > 0:
            send, base = call(
                functools.partial(enter_kernel, stage),
                (slot_shape, field_shape),
                [smem] * 3 + [vmem] * 5 + [hbm] * 2,
                (vmem, vmem),
                [forward_scratch, pltpu.SemaphoreType.DMA],
                cost_of(100_000_000, 2_000_000),
            )(
                place,
                own_slots,
                other_slots,
                trace,
                own_u,
                other_u,
                own_y,
                other_y,
                own_forward,
                other_forward,
            )
            reply = separator(stage, 0, exchange(send))
        returned = exchange(reply)
        bases = [] if base is None else [base]

        def middle(*refs, stage=stage, count=len(bases)):
            head, rest = refs[:4], refs[4:]
            middle_kernel(stage, *head, rest[:count], *rest[count:])

        field, send, base = call(
            middle,
            (field_shape, slot_shape, field_shape),
            [smem] * 3 + [vmem] * (1 + len(bases)) + [vmem] * 4 + [hbm] * 4,
            (vmem,) * 3,
            [back_scratch, forward_scratch, pltpu.SemaphoreType.DMA((2,))],
            cost_of(300_000_000, 3_000_000),
        )(
            place,
            own_slots,
            other_slots,
            returned,
            *bases,
            own_u,
            other_u,
            own_y,
            other_y,
            own_back,
            other_back,
            own_forward,
            other_forward,
        )
        fields.append(field)
        returned = exchange(separator(stage, 1, exchange(send)))
        field, trace = call(
            functools.partial(last_kernel, stage),
            (field_shape, shape(TR // RB, 8, LANES)),
            [smem] * 3 + [vmem] * 2 + [hbm] * 2,
            (vmem, vmem),
            [back_scratch, pltpu.SemaphoreType.DMA],
            cost_of(200_000_000, 2_000_000),
        )(place, own_slots, other_slots, returned, base, own_back, other_back)
        fields.append(field)
        if stage < 3:
            trace = to_next_stage(trace, stage)

    half_shape = shape(2, 2, HALF, P_SIZE)

    def collect(place_ref, *refs):
        collect_kernel(place_ref, refs[:8], *refs[8:])

    own, to_other = call(
        collect,
        (half_shape, half_shape),
        [smem] + [hbm] * 8,
        (vmem, vmem),
        [pltpu.VMEM((4, P_SIZE, LANES), f32), pltpu.SemaphoreType.DMA((4,))],
    )(place, *fields)
    down, up = call(
        output_kernel,
        (shape(2, S, P_SIZE), shape(2, S, P_SIZE)),
        [smem, vmem, vmem],
        (vmem, vmem),
    )(place, own, across_cores(to_other))
    return down[None, None], up[None, None]


def solution(mesh):
    whole = P("layer", "front", None, None, None)
    return jax.shard_map(
        body,
        mesh=mesh,
        in_specs=(whole,) * 7 + (P("layer", "front", None, None), P("layer", "front", None)),
        out_specs=(whole, whole),
        check_vma=False,
    )
```

```python
import functools

import jax
import jax.numpy as jnp
from jax import lax
from jax.experimental import pallas as pl
from jax.experimental.pallas import tpu as pltpu
from jax.sharding import PartitionSpec as P


P_SIZE = 256
Q = 256
TR = 128
RB = 32
S = 32
NB = 16
QB = 8
CAP = 2
HALF = 16
GROUP = 32
LANES = 128

f32 = jnp.float32
bf16 = jnp.bfloat16
VMEM_LIMIT = 48 * 1024 * 1024
ALMOST_ALL_VMEM = 60 * 1024 * 1024
smem = pl.BlockSpec(memory_space=pltpu.SMEM)
vmem = pl.BlockSpec(memory_space=pltpu.VMEM)
hbm = pl.BlockSpec(memory_space=pl.ANY)
NN = (((1,), (0,)), ((), ()))
NT = (((1,), (1,)), ((), ()))


def halves(value):
    high = value.astype(bf16)
    return high, (value - high.astype(f32)).astype(bf16)


def dot(first, second, dims=NN):
    return lax.dot_general(first, second, dims, preferred_element_type=f32)


def product(first, second, dims=NN):
    first_high, first_low = halves(first)
    second_high, second_low = halves(second)
    return (
        dot(first_high, second_high, dims)
        + dot(first_high, second_low, dims)
        + dot(first_low, second_high, dims)
    )


def narrow_product(first, second):
    first_high, first_low = halves(first)
    second_high, second_low = halves(second)
    both = dot(first_high, jnp.concatenate([second_high, second_low], axis=1))
    return both[:, :LANES] + both[:, LANES:] + dot(first_low, second_high)


def stacked(value):
    return jnp.concatenate(halves(value), axis=0)


def stacked_product(first, second):
    rows = first.shape[0] // 2
    both = dot(first, jnp.concatenate(halves(second), axis=1))
    return (both[:rows, :LANES] + both[:rows, LANES:]) + (both[rows:, :LANES] + both[rows:, LANES:])


def complex_pair(first, second, dims=NN):
    real = product(first[0], second[0], dims) - product(first[1], second[1], dims)
    imag = product(first[0], second[1], dims) + product(first[1], second[0], dims)
    return real, imag


def lane_ids(rows):
    return lax.broadcasted_iota(jnp.int32, (rows, LANES), 1)


def turned(value):
    lanes = lane_ids(value.shape[0])
    ahead = pltpu.roll(value, LANES - HALF, 1)
    behind = pltpu.roll(value, HALF, 1)
    return jnp.where(lanes % GROUP < HALF, -ahead, behind)


def pick(group, choices):
    return jnp.where(
        group == 0,
        choices[0],
        jnp.where(group == 1, choices[1], jnp.where(group == 2, choices[2], choices[3])),
    )


def rotations(value):
    return [value] + [pltpu.roll(value, GROUP * turn, 1) for turn in (1, 2, 3)]


def spread_group(rolled, group, source):
    return pick(group, [rolled[(place - source) % 4] for place in range(4)])


def unpack(packed):
    count = packed.shape[0]
    flat = packed.reshape(count * 8, LANES)
    group = lane_ids(count * 8) // GROUP
    rolled = rotations(flat)
    parts = [spread_group(rolled, group, k).reshape(count, 8, LANES) for k in range(4)]
    return jnp.stack(parts, axis=1).reshape(count * RB, LANES)


def unpack_both(packed):
    count = packed.shape[0]
    flat = packed.reshape(count * 8, LANES)
    return unpack(packed), unpack(turned(flat).reshape(count, 8, LANES))


def pack(spread):
    count = spread.shape[0] // RB
    parts = spread.reshape(count, 4, 8, LANES)
    group = lax.broadcasted_iota(jnp.int32, (count, 8, LANES), 2) // GROUP
    return pick(group, [parts[:, k] for k in range(4)])


def source_kernel(
    place_ref,
    down_hbm,
    up_hbm,
    leaf_hbm,
    coupling_hbm,
    own_u_ref,
    other_u_ref,
    own_y_ref,
    other_y_ref,
    down_ref,
    up_ref,
    leaf_ref,
    coupling_ref,
    semaphores,
):
    copies = [
        pltpu.make_async_copy(source, target, semaphores.at[index])
        for index, (source, target) in enumerate(
            (
                (down_hbm, down_ref),
                (up_hbm, up_ref),
                (leaf_hbm, leaf_ref),
                (coupling_hbm, coupling_ref),
            )
        )
    ]
    for copy in copies:
        copy.start()
    core = place_ref[0] % 2
    own_row = pl.multiple_of(core * HALF, HALF)
    other_row = pl.multiple_of((1 - core) * HALF, HALF)
    copies[0].wait()
    copies[1].wait()
    rows, turned_rows = [], []
    for source in (down_ref, up_ref):
        for start in (own_row, other_row):
            real = source[0, pl.ds(start, HALF), :]
            imag = source[1, pl.ds(start, HALF), :]
            rows += [real, imag]
            turned_rows += [-imag, real]
    copies[2].wait()
    y = product(leaf_ref[0], jnp.concatenate(rows, axis=0), NT) + product(
        leaf_ref[1], jnp.concatenate(turned_rows, axis=0), NT
    )
    rolled = rotations(y)
    y_group = lane_ids(P_SIZE) // GROUP
    for sweep in range(2):
        for side, y_ref in enumerate((own_y_ref, other_y_ref)):
            y_ref[sweep] = spread_group(rolled, y_group, 2 * sweep + side)
    copies[3].wait()
    u = narrow_product(coupling_ref[0], y) + narrow_product(coupling_ref[1], turned(y))
    parts = u.reshape(NB, 4, 8, LANES)
    u_group = lane_ids(NB * 8) // GROUP
    for sweep in range(2):
        for side, u_ref in enumerate((own_u_ref, other_u_ref)):
            choices = []
            for k in range(4):
                part = parts[:, k].reshape(NB * 8, LANES)
                turn = (k - 2 * sweep - side) % 4
                choices.append(pltpu.roll(part, GROUP * turn, 1) if turn else part)
            u_ref[sweep] = pick(u_group, choices).reshape(NB, 8, LANES)


def operator_kernel(
    after_ref,
    leaf_hbm,
    coupling_hbm,
    top_hbm,
    bottom_hbm,
    own_sep_hbm,
    other_sep_hbm,
    forward_ref,
    back_ref,
    seps_ref,
    leaf_ref,
    coupling_ref,
    top_ref,
    bottom_ref,
    sep_ref,
    semaphores,
):
    copies = [
        pltpu.make_async_copy(source, target, semaphores.at[index])
        for index, (source, target) in enumerate(
            (
                (leaf_hbm, leaf_ref),
                (top_hbm, top_ref),
                (bottom_hbm, bottom_ref),
                (coupling_hbm, coupling_ref),
                (own_sep_hbm, sep_ref.at[0]),
                (other_sep_hbm, sep_ref.at[1]),
            )
        )
    ]
    for copy in copies:
        copy.start()
    for copy in copies[:3]:
        copy.wait()
    leaf = (leaf_ref[0], leaf_ref[1])
    inject = tuple(
        jnp.concatenate([top_ref[part], bottom_ref[part]], axis=0) for part in range(2)
    )
    local = complex_pair(leaf, inject, NT)
    copies[3].wait()
    coupling = (coupling_ref[0], coupling_ref[1])
    update = complex_pair(coupling, local)
    for sweep in range(2):
        for part in range(2):
            columns = slice(sweep * TR, sweep * TR + TR)
            place = slice(part * TR, part * TR + TR)
            forward_ref[sweep, : NB * RB, place] = update[part][:, columns]
            forward_ref[sweep, NB * RB :, place] = local[part][:, columns]
    back = complex_pair(leaf, coupling, NT)
    back_ref[0] = back[0]
    back_ref[1] = back[1]
    for side in range(2):
        copies[4 + side].wait()
        for part in range(2):
            seps_ref[side, part] = stacked(sep_ref[side, part])


def gather_kernel(
    own_u_hbm,
    other_u_hbm,
    own_y_hbm,
    other_y_hbm,
    own_back_hbm,
    other_back_hbm,
    own_forward_hbm,
    other_forward_hbm,
    u_ref,
    y_ref,
    backs_ref,
    forwards_ref,
    back_ref,
    forward_ref,
    semaphores,
):
    copies = [
        pltpu.make_async_copy(source, target, semaphores.at[index])
        for index, (source, target) in enumerate(
            (
                (own_back_hbm, back_ref.at[0]),
                (own_forward_hbm, forward_ref.at[0]),
                (other_back_hbm, back_ref.at[1]),
                (other_forward_hbm, forward_ref.at[1]),
                (own_u_hbm, u_ref.at[0]),
                (other_u_hbm, u_ref.at[1]),
                (own_y_hbm, y_ref.at[0]),
                (other_y_hbm, y_ref.at[1]),
            )
        )
    ]
    for copy in copies:
        copy.start()
    for side in range(2):
        copies[2 * side].wait()
        for part in range(2):
            backs_ref[side, part] = stacked(back_ref[side, part])
        copies[2 * side + 1].wait()
        for sweep in range(2):
            forwards_ref[side, sweep] = stacked(forward_ref[side, sweep])
    for copy in copies[4:]:
        copy.wait()


def stage_place(place_ref, stage):
    row = place_ref[0] // 2
    core = place_ref[0] % 2
    sweep = jnp.where(row == stage, 0, 1)
    first = jnp.where(sweep == core, 0, 1)
    return sweep, first


def wait_for(source_ref, target_ref, semaphore):
    pltpu.make_async_copy(source_ref, target_ref, semaphore).wait()


def send_blocks(choice, own_slots_ref, other_slots_ref, packed, send_ref):
    for block in range(NB):
        slot = jnp.where(choice == 0, own_slots_ref[block], other_slots_ref[block])
        send_ref[slot] = packed[block]


def first_kernel(
    place_ref,
    own_targets_ref,
    other_targets_ref,
    own_offsets_ref,
    other_offsets_ref,
    own_u_ref,
    other_u_ref,
    own_slots_ref,
    other_slots_ref,
    send_ref,
):
    leaves = send_ref.shape[0]
    sweep, first = stage_place(place_ref, 0)
    lanes = lane_ids(leaves)
    rows = lax.broadcasted_iota(jnp.int32, (leaves, LANES), 0)
    notes = jnp.full((leaves, LANES), QB, jnp.int32)
    all_slots = []
    for side, (targets_ref, offsets_ref, slots_ref) in enumerate(
        (
            (own_targets_ref, own_offsets_ref, own_slots_ref),
            (other_targets_ref, other_offsets_ref, other_slots_ref),
        )
    ):
        targets = [targets_ref[block] for block in range(NB)]
        slots = []
        for block in range(NB):
            rank = jnp.int32(0)
            for earlier in range(block):
                rank = rank + jnp.where(targets[earlier] == targets[block], 1, 0)
            slot = targets[block] * CAP + rank
            slots_ref[block] = slot
            slots.append(slot)
            here = (rows == targets[block]) & (lanes == CAP * side + rank)
            notes = jnp.where(here, offsets_ref[block], notes)
        all_slots.append(slots)
    send_ref[:, CAP * 8 :, :] = jnp.broadcast_to(
        notes.astype(f32)[:, None, :], (leaves, 8, LANES)
    )
    packed = jnp.where(first == 0, own_u_ref[sweep], other_u_ref[sweep])
    for block in range(NB):
        slot = jnp.where(first == 0, all_slots[0][block], all_slots[1][block])
        row = pl.multiple_of((slot % CAP) * 8, 8)
        send_ref[slot // CAP, pl.ds(row, 8), :] = packed[block]


def separator_solve(choice, offsets_ref, arrived, seps_ref, reply_ref, even_ref, odd_ref, solved_ref):
    leaves = reply_ref.shape[0] // CAP
    even_ref[...] = jnp.zeros_like(even_ref)
    odd_ref[...] = jnp.zeros_like(odd_ref)
    places = []
    for leaf in range(leaves):
        for rank, total_ref in enumerate((even_ref, odd_ref)):
            place = offsets_ref[CAP * choice + rank, leaf]
            places.append(place)
            total_ref[place] = total_ref[place] + arrived(leaf, rank)
    rhs, rhs_turned = unpack_both(even_ref[:QB] + odd_ref[:QB])
    solved = stacked_product(seps_ref[choice, 0], rhs) + stacked_product(
        seps_ref[choice, 1], rhs_turned
    )
    solved_ref[:QB] = pack(solved)
    solved_ref[QB] = jnp.zeros((8, LANES), f32)
    for slot, place in enumerate(places):
        reply_ref[slot] = solved_ref[place]


def separator_kernel(
    stage, step, place_ref, offsets_ref, arrived_ref, seps_ref, reply_ref, *scratch
):
    sweep, first = stage_place(place_ref, stage)
    separator_solve(
        first if step == 0 else 1 - first,
        offsets_ref,
        lambda leaf, rank: arrived_ref[CAP * leaf + rank],
        seps_ref,
        reply_ref,
        *scratch,
    )


def first_separator_kernel(
    place_ref,
    arrived_ref,
    seps_ref,
    forward_in_hbm,
    back_in_hbm,
    offsets_ref,
    reply_ref,
    forward_out_hbm,
    back_out_hbm,
    notes_ref,
    semaphore,
    *scratch,
):
    sweep, first = stage_place(place_ref, 0)
    leaves = arrived_ref.shape[0]
    notes = arrived_ref[:, CAP * 8, :]
    whole = jnp.concatenate([notes, jnp.zeros((LANES - leaves, LANES), f32)], axis=0)
    notes_ref[...] = whole.T[:8].astype(jnp.int32)
    copy = pltpu.make_async_copy(notes_ref, offsets_ref, semaphore)
    copy.start()
    copy.wait()
    separator_solve(
        first,
        offsets_ref,
        lambda leaf, rank: arrived_ref[leaf, 8 * rank : 8 * rank + 8, :],
        seps_ref,
        reply_ref,
        *scratch,
    )


def leaf_finish(choice, own_slots_ref, other_slots_ref, returned_ref, backs_ref, base):
    blocks = []
    for block in range(NB):
        slot = jnp.where(choice == 0, own_slots_ref[block], other_slots_ref[block])
        blocks.append(returned_ref[slot])
    mine, mine_turned = unpack_both(jnp.stack(blocks, axis=0))
    return (
        base
        + stacked_product(backs_ref[choice, 0], mine)
        + stacked_product(backs_ref[choice, 1], mine_turned)
    )


def leaf_begin(
    sweep,
    choice,
    trace,
    trace_turned,
    own_slots_ref,
    other_slots_ref,
    u_ref,
    y_ref,
    forwards_ref,
    send_ref,
    base_ref,
):
    driven = stacked_product(
        forwards_ref[choice, sweep], jnp.concatenate([trace, trace_turned], axis=0)
    )
    packed = pack(driven[: NB * RB]) + u_ref[choice, sweep]
    send_blocks(choice, own_slots_ref, other_slots_ref, packed, send_ref)
    base_ref[...] = driven[NB * RB :] + y_ref[choice, sweep]


def trace_rows(sweep, field_ref):
    return field_ref[pl.ds(pl.multiple_of((1 - sweep) * TR, TR), TR), :]


def middle_kernel(
    stage,
    place_ref,
    own_slots_ref,
    other_slots_ref,
    u_ref,
    y_ref,
    forwards_ref,
    backs_ref,
    returned_ref,
    base_refs,
    field_ref,
    send_ref,
    next_base_ref,
):
    sweep, first = stage_place(place_ref, stage)
    base = base_refs[0][...] if base_refs else y_ref[first, sweep]
    field_ref[...] = leaf_finish(
        first, own_slots_ref, other_slots_ref, returned_ref, backs_ref, base
    )
    trace = trace_rows(sweep, field_ref)
    leaf_begin(
        sweep,
        1 - first,
        trace,
        turned(trace),
        own_slots_ref,
        other_slots_ref,
        u_ref,
        y_ref,
        forwards_ref,
        send_ref,
        next_base_ref,
    )


def last_kernel(
    stage,
    place_ref,
    own_slots_ref,
    other_slots_ref,
    backs_ref,
    returned_ref,
    base_ref,
    field_ref,
    trace_ref,
):
    sweep, first = stage_place(place_ref, stage)
    field_ref[...] = leaf_finish(
        1 - first, own_slots_ref, other_slots_ref, returned_ref, backs_ref, base_ref[...]
    )
    trace_ref[...] = pack(trace_rows(sweep, field_ref))


def enter_kernel(
    stage,
    place_ref,
    own_slots_ref,
    other_slots_ref,
    u_ref,
    y_ref,
    forwards_ref,
    trace_ref,
    send_ref,
    next_base_ref,
):
    sweep, first = stage_place(place_ref, stage)
    trace, trace_turned = unpack_both(trace_ref[...])
    leaf_begin(
        sweep,
        first,
        trace,
        trace_turned,
        own_slots_ref,
        other_slots_ref,
        u_ref,
        y_ref,
        forwards_ref,
        send_ref,
        next_base_ref,
    )


def collect_kernel(place_ref, field_refs, own_ref, other_ref, parts_ref, semaphores):
    row = place_ref[0] // 2
    core = place_ref[0] % 2
    for sweep in range(2):
        for position in range(2):
            layer = position if sweep == 0 else 1 - position
            side = jnp.where(core == layer, 0, 1)
            for stage in range(4):
                active = row == stage if sweep == 0 else row == 3 - stage

                @pl.when(active)
                def _():
                    pltpu.make_async_copy(
                        field_refs[2 * stage + position],
                        parts_ref.at[2 * sweep + side],
                        semaphores.at[2 * sweep + position],
                    ).start()

    for index in range(4):
        wait_for(field_refs[0], parts_ref.at[0], semaphores.at[index])
    group = lane_ids(P_SIZE) // GROUP
    joined = pick(group, [parts_ref[index] for index in range(4)])
    rows = joined.T.reshape(2, 2, 2, HALF, P_SIZE)
    own_ref[...] = rows[:, 0]
    other_ref[...] = rows[:, 1]


def output_kernel(place_ref, own_ref, other_ref, down_ref, up_ref):
    core = place_ref[0] % 2
    for sweep, field_ref in enumerate((down_ref, up_ref)):
        for part in range(2):
            field_ref[part, pl.ds(pl.multiple_of(core * HALF, HALF), HALF), :] = own_ref[sweep, part]
            field_ref[part, pl.ds(pl.multiple_of((1 - core) * HALF, HALF), HALF), :] = other_ref[
                sweep, part
            ]


def call(
    kernel, outs, in_specs, out_specs, scratch=(), cost=None, limit=VMEM_LIMIT, aliases=None
):
    return pl.pallas_call(
        kernel,
        out_shape=outs,
        in_specs=in_specs,
        out_specs=out_specs,
        scratch_shapes=list(scratch),
        compiler_params=pltpu.CompilerParams(vmem_limit_bytes=limit),
        cost_estimate=cost,
        input_output_aliases=aliases or {},
    )


def shape(*dims, dtype=f32):
    return jax.ShapeDtypeStruct(dims, dtype)


def cost_of(flops, size):
    return pl.CostEstimate(flops=flops, bytes_accessed=size, transcendentals=0)


def across_cores(value):
    layers = lax.axis_size("layer")
    return lax.ppermute(value, "layer", [(index, index ^ 1) for index in range(layers)])


def exchange(value):
    return lax.all_to_all(value, "front", split_axis=0, concat_axis=0, tiled=True)


def to_next_stage(value, stage):
    moves = [(stage, stage + 1), (3 - stage, 2 - stage)]
    pairs = [(2 * a + core, 2 * b + core) for a, b in moves for core in range(2)]
    return lax.ppermute(value, "layer", pairs)


def body(
    sources_down,
    sources_up,
    leaf_inverse,
    coupling,
    sep_inverse,
    inject_top,
    inject_bottom,
    targets,
    offsets,
):
    leaves = lax.axis_size("front")
    slots = leaves * CAP
    place = lax.axis_index("layer").reshape(1).astype(jnp.int32)
    leaf = leaf_inverse[0, 0]
    rows = coupling[0, 0]
    sep = sep_inverse[0, 0]
    own_targets = targets[0, 0, :, 0]
    other_targets = across_cores(own_targets)
    other_offsets = across_cores(offsets[0, 0])
    other_sep = across_cores(sep)

    source_scratch = pltpu.VMEM((2, S, P_SIZE), f32)
    leaf_scratch = pltpu.VMEM((2, P_SIZE, P_SIZE), f32)
    rows_scratch = pltpu.VMEM((2, NB * RB, P_SIZE), f32)
    inject_scratch = pltpu.VMEM((2, TR, P_SIZE), f32)
    u_shape = shape(2, NB, 8, LANES)
    y_shape = shape(2, P_SIZE, LANES)
    own_u, to_other_u, own_y, to_other_y = call(
        source_kernel,
        (u_shape, u_shape, y_shape, y_shape),
        [smem] + [hbm] * 4,
        (vmem,) * 4,
        [
            source_scratch,
            source_scratch,
            leaf_scratch,
            rows_scratch,
            pltpu.SemaphoreType.DMA((4,)),
        ],
        cost_of(600_000_000, 2_500_000),
        ALMOST_ALL_VMEM,
    )(place, sources_down[0, 0], sources_up[0, 0], leaf, rows)
    other_u = across_cores(to_other_u)

    slot_shape = shape(slots, 8, LANES)
    field_shape = shape(P_SIZE, LANES)
    slots_shape = shape(NB, dtype=jnp.int32)
    own_slots, other_slots, send = call(
        first_kernel,
        (slots_shape, slots_shape, shape(leaves, (CAP + 1) * 8, LANES)),
        [smem] * 5 + [vmem] * 2,
        (smem, smem, vmem),
    )(place, own_targets, other_targets, offsets[0, 0], other_offsets, own_u, other_u)
    arrived = exchange(send)

    own_forward, own_back, seps = call(
        operator_kernel,
        (
            shape(2, NB * RB + P_SIZE, 2 * TR),
            shape(2, P_SIZE, NB * RB),
            shape(2, 2, 2 * Q, Q, dtype=bf16),
        ),
        [hbm] * 7,
        (vmem,) * 3,
        [
            leaf_scratch,
            rows_scratch,
            inject_scratch,
            inject_scratch,
            pltpu.VMEM((2, 2, Q, Q), f32),
            pltpu.SemaphoreType.DMA((6,)),
        ],
        cost_of(4_000_000_000, 5_000_000),
    )(send, leaf, rows, inject_top[0, 0], inject_bottom[0, 0], sep, other_sep)
    separator_scratch = [pltpu.VMEM((QB + 1, 8, LANES), f32)] * 3
    places, reply, own_forward, own_back = call(
        first_separator_kernel,
        (
            shape(8, LANES, dtype=jnp.int32),
            slot_shape,
            shape(*own_forward.shape),
            shape(*own_back.shape),
        ),
        [smem, vmem, vmem, hbm, hbm],
        (smem, vmem, hbm, hbm),
        [pltpu.VMEM((8, LANES), jnp.int32), pltpu.SemaphoreType.DMA] + separator_scratch,
        cost_of(100_000_000, 1_100_000),
        aliases={3: 2, 4: 3},
    )(place, arrived, seps, own_forward, own_back)
    other_y = across_cores(to_other_y)
    other_back = across_cores(own_back)
    other_forward = across_cores(own_forward)

    u, y, backs, forwards = call(
        gather_kernel,
        (
            shape(2, 2, NB, 8, LANES),
            shape(2, 2, P_SIZE, LANES),
            shape(2, 2, 2 * P_SIZE, NB * RB, dtype=bf16),
            shape(2, 2, 2 * (NB * RB + P_SIZE), 2 * TR, dtype=bf16),
        ),
        [hbm] * 8,
        (vmem,) * 4,
        [
            pltpu.VMEM((2, 2, P_SIZE, NB * RB), f32),
            pltpu.VMEM((2, 2, NB * RB + P_SIZE, 2 * TR), f32),
            pltpu.SemaphoreType.DMA((8,)),
        ],
        cost_of(10_000_000, 12_000_000),
    )(own_u, other_u, own_y, other_y, own_back, other_back, own_forward, other_forward)

    def separator(stage, step, arrived):
        return call(
            functools.partial(separator_kernel, stage, step),
            slot_shape,
            [smem] * 2 + [vmem] * 2,
            vmem,
            separator_scratch,
            cost_of(100_000_000, 1_100_000),
        )(place, places, arrived, seps)

    fields = []
    base = None
    trace = None
    for stage in range(4):
        if stage > 0:
            send, base = call(
                functools.partial(enter_kernel, stage),
                (slot_shape, field_shape),
                [smem] * 3 + [vmem] * 4,
                (vmem, vmem),
                cost=cost_of(100_000_000, 2_000_000),
            )(place, own_slots, other_slots, u, y, forwards, trace)
            reply = separator(stage, 0, exchange(send))
        returned = exchange(reply)
        bases = [] if base is None else [base]

        def middle(*refs, stage=stage, count=len(bases)):
            head, rest = refs[:8], refs[8:]
            middle_kernel(stage, *head, rest[:count], *rest[count:])

        field, send, base = call(
            middle,
            (field_shape, slot_shape, field_shape),
            [smem] * 3 + [vmem] * (5 + len(bases)),
            (vmem,) * 3,
            cost=cost_of(300_000_000, 3_000_000),
        )(place, own_slots, other_slots, u, y, forwards, backs, returned, *bases)
        fields.append(field)
        returned = exchange(separator(stage, 1, exchange(send)))
        field, trace = call(
            functools.partial(last_kernel, stage),
            (field_shape, shape(TR // RB, 8, LANES)),
            [smem] * 3 + [vmem] * 3,
            (vmem, vmem),
            cost=cost_of(200_000_000, 2_000_000),
        )(place, own_slots, other_slots, backs, returned, base)
        fields.append(field)
        if stage < 3:
            trace = to_next_stage(trace, stage)

    half_shape = shape(2, 2, HALF, P_SIZE)

    def collect(place_ref, *refs):
        collect_kernel(place_ref, refs[:8], *refs[8:])

    own, to_other = call(
        collect,
        (half_shape, half_shape),
        [smem] + [hbm] * 8,
        (vmem, vmem),
        [pltpu.VMEM((4, P_SIZE, LANES), f32), pltpu.SemaphoreType.DMA((4,))],
    )(place, *fields)
    down, up = call(
        output_kernel,
        (shape(2, S, P_SIZE), shape(2, S, P_SIZE)),
        [smem, vmem, vmem],
        (vmem, vmem),
    )(place, own, across_cores(to_other))
    return down[None, None], up[None, None]


def solution(mesh):
    whole = P("layer", "front", None, None, None)
    return jax.shard_map(
        body,
        mesh=mesh,
        in_specs=(whole,) * 7 + (P("layer", "front", None, None), P("layer", "front", None)),
        out_specs=(whole, whole),
        check_vma=False,
    )
```

```python
import functools

import jax
import jax.numpy as jnp
from jax import lax
from jax.experimental import pallas as pl
from jax.experimental.pallas import tpu as pltpu
from jax.sharding import PartitionSpec as P


P_SIZE = 256
Q = 256
TR = 128
RB = 32
S = 32
NB = 16
QB = 8
CAP = 2
HALF = 16
GROUP = 32
LANES = 128

f32 = jnp.float32
bf16 = jnp.bfloat16
VMEM_LIMIT = 52 * 1024 * 1024
ALMOST_ALL_VMEM = 60 * 1024 * 1024
smem = pl.BlockSpec(memory_space=pltpu.SMEM)
vmem = pl.BlockSpec(memory_space=pltpu.VMEM)
hbm = pl.BlockSpec(memory_space=pl.ANY)
NN = (((1,), (0,)), ((), ()))
NT = (((1,), (1,)), ((), ()))


def halves(value):
    high = value.astype(bf16)
    return high, (value - high.astype(f32)).astype(bf16)


def dot(first, second, dims=NN):
    return lax.dot_general(first, second, dims, preferred_element_type=f32)


def product(first, second, dims=NN):
    first_high, first_low = halves(first)
    second_high, second_low = halves(second)
    return (
        dot(first_high, second_high, dims)
        + dot(first_high, second_low, dims)
        + dot(first_low, second_high, dims)
    )


def narrow_product(first, second):
    first_high, first_low = halves(first)
    second_high, second_low = halves(second)
    both = dot(first_high, jnp.concatenate([second_high, second_low], axis=1))
    return both[:, :LANES] + both[:, LANES:] + dot(first_low, second_high)


def stacked(value):
    return jnp.concatenate(halves(value), axis=0)


def shared(value):
    low = value - value.astype(bf16).astype(f32)
    return jnp.where(lane_ids(value.shape[0]) < LANES // 2, value, low).astype(bf16)


def stacked_product(pairs):
    total = None
    for first, second in pairs:
        both = dot(first, shared(second))
        total = both if total is None else total + both
    rows = total.shape[0] // 2
    total = total[:rows] + total[rows:]
    return total + pltpu.roll(total, LANES // 2, 1)


def complex_pair(first, second, dims=NN):
    real = product(first[0], second[0], dims) - product(first[1], second[1], dims)
    imag = product(first[0], second[1], dims) + product(first[1], second[0], dims)
    return real, imag


def lane_ids(rows):
    return lax.broadcasted_iota(jnp.int32, (rows, LANES), 1)


def turned(value):
    lanes = lane_ids(value.shape[0])
    ahead = pltpu.roll(value, LANES - HALF, 1)
    behind = pltpu.roll(value, HALF, 1)
    return jnp.where(lanes % GROUP < HALF, -ahead, behind)


def pick(group, choices):
    return jnp.where(
        group == 0,
        choices[0],
        jnp.where(group == 1, choices[1], jnp.where(group == 2, choices[2], choices[3])),
    )


def rotations(value):
    return [value] + [pltpu.roll(value, GROUP * turn, 1) for turn in (1, 2, 3)]


def spread_group(rolled, group, source):
    return pick(group, [rolled[(place - source) % 4] for place in range(4)])


def unpack(packed):
    count = packed.shape[0]
    flat = packed.reshape(count * 8, LANES)
    group = lane_ids(count * 8) // GROUP
    rolled = rotations(flat)
    parts = [spread_group(rolled, group, k).reshape(count, 8, LANES) for k in range(4)]
    return jnp.stack(parts, axis=1).reshape(count * RB, LANES)


def unpack_both(packed):
    count = packed.shape[0]
    flat = packed.reshape(count * 8, LANES)
    return unpack(packed), unpack(turned(flat).reshape(count, 8, LANES))


def pack(spread):
    count = spread.shape[0] // RB
    parts = spread.reshape(count, 4, 8, LANES)
    group = lax.broadcasted_iota(jnp.int32, (count, 8, LANES), 2) // GROUP
    return pick(group, [parts[:, k] for k in range(4)])


def source_kernel(
    place_ref,
    down_hbm,
    up_hbm,
    leaf_hbm,
    coupling_hbm,
    own_u_ref,
    other_u_ref,
    own_y_ref,
    other_y_ref,
    down_ref,
    up_ref,
    leaf_ref,
    coupling_ref,
    semaphores,
):
    copies = [
        pltpu.make_async_copy(source, target, semaphores.at[index])
        for index, (source, target) in enumerate(
            (
                (down_hbm, down_ref),
                (up_hbm, up_ref),
                (leaf_hbm, leaf_ref),
                (coupling_hbm, coupling_ref),
            )
        )
    ]
    for copy in copies:
        copy.start()
    core = place_ref[0] % 2
    own_row = pl.multiple_of(core * HALF, HALF)
    other_row = pl.multiple_of((1 - core) * HALF, HALF)
    copies[0].wait()
    copies[1].wait()
    rows, turned_rows = [], []
    for source in (down_ref, up_ref):
        for start in (own_row, other_row):
            real = source[0, pl.ds(start, HALF), :]
            imag = source[1, pl.ds(start, HALF), :]
            rows += [real, imag]
            turned_rows += [-imag, real]
    copies[2].wait()
    y = product(leaf_ref[0], jnp.concatenate(rows, axis=0), NT) + product(
        leaf_ref[1], jnp.concatenate(turned_rows, axis=0), NT
    )
    rolled = rotations(y)
    y_group = lane_ids(P_SIZE) // GROUP
    for sweep in range(2):
        for side, y_ref in enumerate((own_y_ref, other_y_ref)):
            y_ref[sweep] = spread_group(rolled, y_group, 2 * sweep + side)
    copies[3].wait()
    u = narrow_product(coupling_ref[0], y) + narrow_product(coupling_ref[1], turned(y))
    parts = u.reshape(NB, 4, 8, LANES)
    u_group = lane_ids(NB * 8) // GROUP
    for sweep in range(2):
        for side, u_ref in enumerate((own_u_ref, other_u_ref)):
            choices = []
            for k in range(4):
                part = parts[:, k].reshape(NB * 8, LANES)
                turn = (k - 2 * sweep - side) % 4
                choices.append(pltpu.roll(part, GROUP * turn, 1) if turn else part)
            u_ref[sweep] = pick(u_group, choices).reshape(NB, 8, LANES)


def operator_kernel(
    after_ref,
    leaf_hbm,
    coupling_hbm,
    top_hbm,
    bottom_hbm,
    own_sep_hbm,
    other_sep_hbm,
    forward_ref,
    back_ref,
    seps_ref,
    leaf_ref,
    coupling_ref,
    top_ref,
    bottom_ref,
    sep_ref,
    semaphores,
):
    copies = [
        pltpu.make_async_copy(source, target, semaphores.at[index])
        for index, (source, target) in enumerate(
            (
                (leaf_hbm, leaf_ref),
                (top_hbm, top_ref),
                (bottom_hbm, bottom_ref),
                (coupling_hbm, coupling_ref),
                (own_sep_hbm, sep_ref.at[0]),
                (other_sep_hbm, sep_ref.at[1]),
            )
        )
    ]
    for copy in copies:
        copy.start()
    for copy in copies[:3]:
        copy.wait()
    leaf = (leaf_ref[0], leaf_ref[1])
    inject = tuple(
        jnp.concatenate([top_ref[part], bottom_ref[part]], axis=0) for part in range(2)
    )
    local = complex_pair(leaf, inject, NT)
    copies[3].wait()
    coupling = (coupling_ref[0], coupling_ref[1])
    update = complex_pair(coupling, local)
    for sweep in range(2):
        for part in range(2):
            columns = slice(sweep * TR, sweep * TR + TR)
            place = slice(part * TR, part * TR + TR)
            forward_ref[sweep, : NB * RB, place] = update[part][:, columns]
            forward_ref[sweep, NB * RB :, place] = local[part][:, columns]
    back = complex_pair(leaf, coupling, NT)
    back_ref[0] = back[0]
    back_ref[1] = back[1]
    for side in range(2):
        copies[4 + side].wait()
        for part in range(2):
            seps_ref[side, part] = stacked(sep_ref[side, part])


def gather_kernel(
    own_u_hbm,
    other_u_hbm,
    own_y_hbm,
    other_y_hbm,
    own_back_hbm,
    other_back_hbm,
    own_forward_hbm,
    other_forward_hbm,
    u_ref,
    y_ref,
    backs_ref,
    forwards_ref,
    back_ref,
    forward_ref,
    semaphores,
):
    copies = [
        pltpu.make_async_copy(source, target, semaphores.at[index])
        for index, (source, target) in enumerate(
            (
                (own_back_hbm, back_ref.at[0]),
                (own_forward_hbm, forward_ref.at[0]),
                (other_back_hbm, back_ref.at[1]),
                (other_forward_hbm, forward_ref.at[1]),
                (own_u_hbm, u_ref.at[0]),
                (other_u_hbm, u_ref.at[1]),
                (own_y_hbm, y_ref.at[0]),
                (other_y_hbm, y_ref.at[1]),
            )
        )
    ]
    for copy in copies:
        copy.start()
    for side in range(2):
        copies[2 * side].wait()
        for part in range(2):
            backs_ref[side, part] = stacked(back_ref[side, part])
        copies[2 * side + 1].wait()
        for sweep in range(2):
            forwards_ref[side, sweep] = stacked(forward_ref[side, sweep])
    for copy in copies[4:]:
        copy.wait()


def stage_place(place_ref, stage):
    row = place_ref[0] // 2
    core = place_ref[0] % 2
    sweep = jnp.where(row == stage, 0, 1)
    first = jnp.where(sweep == core, 0, 1)
    return sweep, first


def wait_for(source_ref, target_ref, semaphore):
    pltpu.make_async_copy(source_ref, target_ref, semaphore).wait()


def send_blocks(choice, own_slots_ref, other_slots_ref, packed, send_ref):
    for block in range(NB):
        slot = jnp.where(choice == 0, own_slots_ref[block], other_slots_ref[block])
        send_ref[slot] = packed[block]


def first_kernel(
    place_ref,
    own_targets_ref,
    other_targets_ref,
    own_offsets_ref,
    other_offsets_ref,
    own_u_ref,
    other_u_ref,
    own_slots_ref,
    other_slots_ref,
    send_ref,
):
    leaves = send_ref.shape[0]
    sweep, first = stage_place(place_ref, 0)
    lanes = lane_ids(leaves)
    rows = lax.broadcasted_iota(jnp.int32, (leaves, LANES), 0)
    notes = jnp.full((leaves, LANES), QB, jnp.int32)
    all_slots = []
    for side, (targets_ref, offsets_ref, slots_ref) in enumerate(
        (
            (own_targets_ref, own_offsets_ref, own_slots_ref),
            (other_targets_ref, other_offsets_ref, other_slots_ref),
        )
    ):
        targets = [targets_ref[block] for block in range(NB)]
        slots = []
        for block in range(NB):
            rank = jnp.int32(0)
            for earlier in range(block):
                rank = rank + jnp.where(targets[earlier] == targets[block], 1, 0)
            slot = targets[block] * CAP + rank
            slots_ref[block] = slot
            slots.append(slot)
            here = (rows == targets[block]) & (lanes == CAP * side + rank)
            notes = jnp.where(here, offsets_ref[block], notes)
        all_slots.append(slots)
    send_ref[:, CAP * 8 :, :] = jnp.broadcast_to(
        notes.astype(f32)[:, None, :], (leaves, 8, LANES)
    )
    packed = jnp.where(first == 0, own_u_ref[sweep], other_u_ref[sweep])
    for block in range(NB):
        slot = jnp.where(first == 0, all_slots[0][block], all_slots[1][block])
        row = pl.multiple_of((slot % CAP) * 8, 8)
        send_ref[slot // CAP, pl.ds(row, 8), :] = packed[block]


def separator_solve(choice, offsets_ref, arrived, seps_ref, reply_ref, solved_ref, *total_refs):
    leaves = reply_ref.shape[0] // CAP
    for total_ref in total_refs:
        total_ref[...] = jnp.zeros_like(total_ref)
    places = []
    for leaf in range(leaves):
        for rank in range(CAP):
            place = offsets_ref[CAP * choice + rank, leaf]
            total_ref = total_refs[len(places) % len(total_refs)]
            places.append(place)
            total_ref[place] = total_ref[place] + arrived(leaf, rank)
    total = total_refs[0][:QB]
    for total_ref in total_refs[1:]:
        total = total + total_ref[:QB]
    rhs, rhs_turned = unpack_both(total)
    solved = stacked_product(
        ((seps_ref[choice, 0], rhs), (seps_ref[choice, 1], rhs_turned))
    )
    solved_ref[:QB] = pack(solved)
    solved_ref[QB] = jnp.zeros((8, LANES), f32)
    for slot, place in enumerate(places):
        reply_ref[slot] = solved_ref[place]


def separator_kernel(
    stage, step, place_ref, offsets_ref, arrived_ref, seps_ref, reply_ref, *scratch
):
    sweep, first = stage_place(place_ref, stage)
    separator_solve(
        first if step == 0 else 1 - first,
        offsets_ref,
        lambda leaf, rank: arrived_ref[CAP * leaf + rank],
        seps_ref,
        reply_ref,
        *scratch,
    )


def first_separator_kernel(
    place_ref,
    arrived_ref,
    seps_ref,
    forward_in_hbm,
    back_in_hbm,
    offsets_ref,
    reply_ref,
    forward_out_hbm,
    back_out_hbm,
    notes_ref,
    semaphore,
    *scratch,
):
    sweep, first = stage_place(place_ref, 0)
    leaves = arrived_ref.shape[0]
    notes = arrived_ref[:, CAP * 8, :]
    whole = jnp.concatenate([notes, jnp.zeros((LANES - leaves, LANES), f32)], axis=0)
    notes_ref[...] = whole.T[:8].astype(jnp.int32)
    copy = pltpu.make_async_copy(notes_ref, offsets_ref, semaphore)
    copy.start()
    copy.wait()
    separator_solve(
        first,
        offsets_ref,
        lambda leaf, rank: arrived_ref[leaf, 8 * rank : 8 * rank + 8, :],
        seps_ref,
        reply_ref,
        *scratch,
    )


def leaf_finish(choice, own_slots_ref, other_slots_ref, returned_ref, backs_ref, base):
    blocks = []
    for block in range(NB):
        slot = jnp.where(choice == 0, own_slots_ref[block], other_slots_ref[block])
        blocks.append(returned_ref[slot])
    mine, mine_turned = unpack_both(jnp.stack(blocks, axis=0))
    return base + stacked_product(
        ((backs_ref[choice, 0], mine), (backs_ref[choice, 1], mine_turned))
    )


def leaf_begin(
    sweep,
    choice,
    trace,
    trace_turned,
    own_slots_ref,
    other_slots_ref,
    u_ref,
    y_ref,
    forwards_ref,
    send_ref,
    base_ref,
):
    driven = stacked_product(
        ((forwards_ref[choice, sweep], jnp.concatenate([trace, trace_turned], axis=0)),)
    )
    packed = pack(driven[: NB * RB]) + u_ref[choice, sweep]
    send_blocks(choice, own_slots_ref, other_slots_ref, packed, send_ref)
    base_ref[...] = driven[NB * RB :] + y_ref[choice, sweep]


def trace_rows(sweep, field_ref):
    return field_ref[pl.ds(pl.multiple_of((1 - sweep) * TR, TR), TR), :]


def middle_kernel(
    stage,
    place_ref,
    own_slots_ref,
    other_slots_ref,
    u_ref,
    y_ref,
    forwards_ref,
    backs_ref,
    returned_ref,
    base_refs,
    field_ref,
    send_ref,
    next_base_ref,
):
    sweep, first = stage_place(place_ref, stage)
    base = base_refs[0][...] if base_refs else y_ref[first, sweep]
    field_ref[...] = leaf_finish(
        first, own_slots_ref, other_slots_ref, returned_ref, backs_ref, base
    )
    trace = trace_rows(sweep, field_ref)
    leaf_begin(
        sweep,
        1 - first,
        trace,
        turned(trace),
        own_slots_ref,
        other_slots_ref,
        u_ref,
        y_ref,
        forwards_ref,
        send_ref,
        next_base_ref,
    )


def last_kernel(
    stage,
    place_ref,
    own_slots_ref,
    other_slots_ref,
    backs_ref,
    returned_ref,
    base_ref,
    field_ref,
    trace_ref,
):
    sweep, first = stage_place(place_ref, stage)
    field_ref[...] = leaf_finish(
        1 - first, own_slots_ref, other_slots_ref, returned_ref, backs_ref, base_ref[...]
    )
    trace_ref[...] = pack(trace_rows(sweep, field_ref))


def enter_kernel(
    stage,
    place_ref,
    own_slots_ref,
    other_slots_ref,
    u_ref,
    y_ref,
    forwards_ref,
    trace_ref,
    send_ref,
    next_base_ref,
):
    sweep, first = stage_place(place_ref, stage)
    trace, trace_turned = unpack_both(trace_ref[...])
    leaf_begin(
        sweep,
        first,
        trace,
        trace_turned,
        own_slots_ref,
        other_slots_ref,
        u_ref,
        y_ref,
        forwards_ref,
        send_ref,
        next_base_ref,
    )


def collect_kernel(place_ref, field_refs, own_ref, other_ref, parts_ref, semaphores):
    row = place_ref[0] // 2
    core = place_ref[0] % 2
    for sweep in range(2):
        for position in range(2):
            layer = position if sweep == 0 else 1 - position
            side = jnp.where(core == layer, 0, 1)
            for stage in range(4):
                active = row == stage if sweep == 0 else row == 3 - stage

                @pl.when(active)
                def _():
                    pltpu.make_async_copy(
                        field_refs[2 * stage + position],
                        parts_ref.at[2 * sweep + side],
                        semaphores.at[2 * sweep + position],
                    ).start()

    for index in range(4):
        wait_for(field_refs[0], parts_ref.at[0], semaphores.at[index])
    group = lane_ids(P_SIZE) // GROUP
    joined = pick(group, [parts_ref[index] for index in range(4)])
    rows = joined.T.reshape(2, 2, 2, HALF, P_SIZE)
    own_ref[...] = rows[:, 0]
    other_ref[...] = rows[:, 1]


def output_kernel(place_ref, own_ref, other_ref, down_ref, up_ref):
    core = place_ref[0] % 2
    for sweep, field_ref in enumerate((down_ref, up_ref)):
        for part in range(2):
            field_ref[part, pl.ds(pl.multiple_of(core * HALF, HALF), HALF), :] = own_ref[sweep, part]
            field_ref[part, pl.ds(pl.multiple_of((1 - core) * HALF, HALF), HALF), :] = other_ref[
                sweep, part
            ]


def call(
    kernel, outs, in_specs, out_specs, scratch=(), cost=None, limit=VMEM_LIMIT, aliases=None
):
    return pl.pallas_call(
        kernel,
        out_shape=outs,
        in_specs=in_specs,
        out_specs=out_specs,
        scratch_shapes=list(scratch),
        compiler_params=pltpu.CompilerParams(vmem_limit_bytes=limit),
        cost_estimate=cost,
        input_output_aliases=aliases or {},
    )


def shape(*dims, dtype=f32):
    return jax.ShapeDtypeStruct(dims, dtype)


def cost_of(flops, size):
    return pl.CostEstimate(flops=flops, bytes_accessed=size, transcendentals=0)


def across_cores(value):
    layers = lax.axis_size("layer")
    return lax.ppermute(value, "layer", [(index, index ^ 1) for index in range(layers)])


def exchange(value):
    return lax.all_to_all(value, "front", split_axis=0, concat_axis=0, tiled=True)


def to_next_stage(value, stage):
    moves = [(stage, stage + 1), (3 - stage, 2 - stage)]
    pairs = [(2 * a + core, 2 * b + core) for a, b in moves for core in range(2)]
    return lax.ppermute(value, "layer", pairs)


def body(
    sources_down,
    sources_up,
    leaf_inverse,
    coupling,
    sep_inverse,
    inject_top,
    inject_bottom,
    targets,
    offsets,
):
    leaves = lax.axis_size("front")
    slots = leaves * CAP
    place = lax.axis_index("layer").reshape(1).astype(jnp.int32)
    leaf = leaf_inverse[0, 0]
    rows = coupling[0, 0]
    sep = sep_inverse[0, 0]
    own_targets = targets[0, 0, :, 0]
    other_targets = across_cores(own_targets)
    other_offsets = across_cores(offsets[0, 0])
    other_sep = across_cores(sep)

    source_scratch = pltpu.VMEM((2, S, P_SIZE), f32)
    leaf_scratch = pltpu.VMEM((2, P_SIZE, P_SIZE), f32)
    rows_scratch = pltpu.VMEM((2, NB * RB, P_SIZE), f32)
    inject_scratch = pltpu.VMEM((2, TR, P_SIZE), f32)
    u_shape = shape(2, NB, 8, LANES)
    y_shape = shape(2, P_SIZE, LANES)
    own_u, to_other_u, own_y, to_other_y = call(
        source_kernel,
        (u_shape, u_shape, y_shape, y_shape),
        [smem] + [hbm] * 4,
        (vmem,) * 4,
        [
            source_scratch,
            source_scratch,
            leaf_scratch,
            rows_scratch,
            pltpu.SemaphoreType.DMA((4,)),
        ],
        cost_of(600_000_000, 2_500_000),
        ALMOST_ALL_VMEM,
    )(place, sources_down[0, 0], sources_up[0, 0], leaf, rows)
    other_u = across_cores(to_other_u)

    slot_shape = shape(slots, 8, LANES)
    field_shape = shape(P_SIZE, LANES)
    slots_shape = shape(NB, dtype=jnp.int32)
    own_slots, other_slots, send = call(
        first_kernel,
        (slots_shape, slots_shape, shape(leaves, (CAP + 1) * 8, LANES)),
        [smem] * 5 + [vmem] * 2,
        (smem, smem, vmem),
    )(place, own_targets, other_targets, offsets[0, 0], other_offsets, own_u, other_u)
    arrived = exchange(send)

    own_forward, own_back, seps = call(
        operator_kernel,
        (
            shape(2, NB * RB + P_SIZE, 2 * TR),
            shape(2, P_SIZE, NB * RB),
            shape(2, 2, 2 * Q, Q, dtype=bf16),
        ),
        [hbm] * 7,
        (vmem,) * 3,
        [
            leaf_scratch,
            rows_scratch,
            inject_scratch,
            inject_scratch,
            pltpu.VMEM((2, 2, Q, Q), f32),
            pltpu.SemaphoreType.DMA((6,)),
        ],
        cost_of(4_000_000_000, 5_000_000),
    )(send, leaf, rows, inject_top[0, 0], inject_bottom[0, 0], sep, other_sep)
    separator_scratch = [pltpu.VMEM((QB + 1, 8, LANES), f32)] * 5
    places, reply, own_forward, own_back = call(
        first_separator_kernel,
        (
            shape(8, LANES, dtype=jnp.int32),
            slot_shape,
            shape(*own_forward.shape),
            shape(*own_back.shape),
        ),
        [smem, vmem, vmem, hbm, hbm],
        (smem, vmem, hbm, hbm),
        [pltpu.VMEM((8, LANES), jnp.int32), pltpu.SemaphoreType.DMA] + separator_scratch,
        cost_of(100_000_000, 1_100_000),
        aliases={3: 2, 4: 3},
    )(place, arrived, seps, own_forward, own_back)
    other_y = across_cores(to_other_y)
    other_back = across_cores(own_back)
    other_forward = across_cores(own_forward)

    u, y, backs, forwards = call(
        gather_kernel,
        (
            shape(2, 2, NB, 8, LANES),
            shape(2, 2, P_SIZE, LANES),
            shape(2, 2, 2 * P_SIZE, NB * RB, dtype=bf16),
            shape(2, 2, 2 * (NB * RB + P_SIZE), 2 * TR, dtype=bf16),
        ),
        [hbm] * 8,
        (vmem,) * 4,
        [
            pltpu.VMEM((2, 2, P_SIZE, NB * RB), f32),
            pltpu.VMEM((2, 2, NB * RB + P_SIZE, 2 * TR), f32),
            pltpu.SemaphoreType.DMA((8,)),
        ],
        cost_of(10_000_000, 12_000_000),
    )(own_u, other_u, own_y, other_y, own_back, other_back, own_forward, other_forward)

    def separator(stage, step, arrived):
        return call(
            functools.partial(separator_kernel, stage, step),
            slot_shape,
            [smem] * 2 + [vmem] * 2,
            vmem,
            separator_scratch,
            cost_of(100_000_000, 1_100_000),
        )(place, places, arrived, seps)

    fields = []
    base = None
    trace = None
    for stage in range(4):
        if stage > 0:
            send, base = call(
                functools.partial(enter_kernel, stage),
                (slot_shape, field_shape),
                [smem] * 3 + [vmem] * 4,
                (vmem, vmem),
                cost=cost_of(100_000_000, 2_000_000),
            )(place, own_slots, other_slots, u, y, forwards, trace)
            reply = separator(stage, 0, exchange(send))
        returned = exchange(reply)
        bases = [] if base is None else [base]

        def middle(*refs, stage=stage, count=len(bases)):
            head, rest = refs[:8], refs[8:]
            middle_kernel(stage, *head, rest[:count], *rest[count:])

        field, send, base = call(
            middle,
            (field_shape, slot_shape, field_shape),
            [smem] * 3 + [vmem] * (5 + len(bases)),
            (vmem,) * 3,
            cost=cost_of(300_000_000, 3_000_000),
        )(place, own_slots, other_slots, u, y, forwards, backs, returned, *bases)
        fields.append(field)
        returned = exchange(separator(stage, 1, exchange(send)))
        field, trace = call(
            functools.partial(last_kernel, stage),
            (field_shape, shape(TR // RB, 8, LANES)),
            [smem] * 3 + [vmem] * 3,
            (vmem, vmem),
            cost=cost_of(200_000_000, 2_000_000),
        )(place, own_slots, other_slots, backs, returned, base)
        fields.append(field)
        if stage < 3:
            trace = to_next_stage(trace, stage)

    half_shape = shape(2, 2, HALF, P_SIZE)

    def collect(place_ref, *refs):
        collect_kernel(place_ref, refs[:8], *refs[8:])

    own, to_other = call(
        collect,
        (half_shape, half_shape),
        [smem] + [hbm] * 8,
        (vmem, vmem),
        [pltpu.VMEM((4, P_SIZE, LANES), f32), pltpu.SemaphoreType.DMA((4,))],
    )(place, *fields)
    down, up = call(
        output_kernel,
        (shape(2, S, P_SIZE), shape(2, S, P_SIZE)),
        [smem, vmem, vmem],
        (vmem, vmem),
    )(place, own, across_cores(to_other))
    return down[None, None], up[None, None]


def solution(mesh):
    whole = P("layer", "front", None, None, None)
    return jax.shard_map(
        body,
        mesh=mesh,
        in_specs=(whole,) * 7 + (P("layer", "front", None, None), P("layer", "front", None)),
        out_specs=(whole, whole),
        check_vma=False,
    )
```

```python
import functools

import jax
import jax.numpy as jnp
from jax import lax
from jax.experimental import pallas as pl
from jax.experimental.pallas import tpu as pltpu
from jax.sharding import PartitionSpec as P


P_SIZE = 256
Q = 256
TR = 128
RB = 32
S = 32
NB = 16
QB = 8
CAP = 2
HALF = 16
GROUP = 32
LANES = 128

f32 = jnp.float32
bf16 = jnp.bfloat16
VMEM_LIMIT = 48 * 1024 * 1024
ALMOST_ALL_VMEM = 60 * 1024 * 1024
smem = pl.BlockSpec(memory_space=pltpu.SMEM)
vmem = pl.BlockSpec(memory_space=pltpu.VMEM)
hbm = pl.BlockSpec(memory_space=pl.ANY)
NN = (((1,), (0,)), ((), ()))
NT = (((1,), (1,)), ((), ()))


def halves(value):
    high = value.astype(bf16)
    return high, (value - high.astype(f32)).astype(bf16)


def dot(first, second, dims=NN):
    return lax.dot_general(first, second, dims, preferred_element_type=f32)


def product(first, second, dims=NN):
    first_high, first_low = halves(first)
    second_high, second_low = halves(second)
    return (
        dot(first_high, second_high, dims)
        + dot(first_high, second_low, dims)
        + dot(first_low, second_high, dims)
    )


def narrow_product(first, second):
    first_high, first_low = halves(first)
    second_high, second_low = halves(second)
    both = dot(first_high, jnp.concatenate([second_high, second_low], axis=1))
    return both[:, :LANES] + both[:, LANES:] + dot(first_low, second_high)


def stacked(value):
    return jnp.concatenate(halves(value), axis=0)


def shared(value):
    low = value - value.astype(bf16).astype(f32)
    return jnp.where(lane_ids(value.shape[0]) < LANES // 2, value, low).astype(bf16)


def stacked_product(pairs):
    total = None
    for first, second in pairs:
        both = dot(first, shared(second))
        total = both if total is None else total + both
    rows = total.shape[0] // 2
    total = total[:rows] + total[rows:]
    return total + pltpu.roll(total, LANES // 2, 1)


def complex_pair(first, second, dims=NN):
    real = product(first[0], second[0], dims) - product(first[1], second[1], dims)
    imag = product(first[0], second[1], dims) + product(first[1], second[0], dims)
    return real, imag


def lane_ids(rows):
    return lax.broadcasted_iota(jnp.int32, (rows, LANES), 1)


def turned(value):
    lanes = lane_ids(value.shape[0])
    ahead = pltpu.roll(value, LANES - HALF, 1)
    behind = pltpu.roll(value, HALF, 1)
    return jnp.where(lanes % GROUP < HALF, -ahead, behind)


def pick(group, choices):
    return jnp.where(
        group == 0,
        choices[0],
        jnp.where(group == 1, choices[1], jnp.where(group == 2, choices[2], choices[3])),
    )


def rotations(value):
    return [value] + [pltpu.roll(value, GROUP * turn, 1) for turn in (1, 2, 3)]


def spread_group(rolled, group, source):
    return pick(group, [rolled[(place - source) % 4] for place in range(4)])


def unpack(packed):
    count = packed.shape[0]
    flat = packed.reshape(count * 8, LANES)
    group = lane_ids(count * 8) // GROUP
    rolled = rotations(flat)
    parts = [spread_group(rolled, group, k).reshape(count, 8, LANES) for k in range(4)]
    return jnp.stack(parts, axis=1).reshape(count * RB, LANES)


def unpack_both(packed):
    count = packed.shape[0]
    flat = packed.reshape(count * 8, LANES)
    return unpack(packed), unpack(turned(flat).reshape(count, 8, LANES))


def pack(spread):
    count = spread.shape[0] // RB
    parts = spread.reshape(count, 4, 8, LANES)
    group = lax.broadcasted_iota(jnp.int32, (count, 8, LANES), 2) // GROUP
    return pick(group, [parts[:, k] for k in range(4)])


def source_kernel(
    place_ref,
    down_hbm,
    up_hbm,
    leaf_hbm,
    coupling_hbm,
    own_u_ref,
    other_u_ref,
    own_y_ref,
    other_y_ref,
    down_ref,
    up_ref,
    leaf_ref,
    coupling_ref,
    semaphores,
):
    copies = [
        pltpu.make_async_copy(source, target, semaphores.at[index])
        for index, (source, target) in enumerate(
            (
                (down_hbm, down_ref),
                (up_hbm, up_ref),
                (leaf_hbm, leaf_ref),
                (coupling_hbm, coupling_ref),
            )
        )
    ]
    for copy in copies:
        copy.start()
    core = place_ref[0] % 2
    own_row = pl.multiple_of(core * HALF, HALF)
    other_row = pl.multiple_of((1 - core) * HALF, HALF)
    copies[0].wait()
    copies[1].wait()
    rows, turned_rows = [], []
    for source in (down_ref, up_ref):
        for start in (own_row, other_row):
            real = source[0, pl.ds(start, HALF), :]
            imag = source[1, pl.ds(start, HALF), :]
            rows += [real, imag]
            turned_rows += [-imag, real]
    copies[2].wait()
    y = product(leaf_ref[0], jnp.concatenate(rows, axis=0), NT) + product(
        leaf_ref[1], jnp.concatenate(turned_rows, axis=0), NT
    )
    rolled = rotations(y)
    y_group = lane_ids(P_SIZE) // GROUP
    for sweep in range(2):
        for side, y_ref in enumerate((own_y_ref, other_y_ref)):
            y_ref[sweep] = spread_group(rolled, y_group, 2 * sweep + side)
    copies[3].wait()
    u = narrow_product(coupling_ref[0], y) + narrow_product(coupling_ref[1], turned(y))
    parts = u.reshape(NB, 4, 8, LANES)
    u_group = lane_ids(NB * 8) // GROUP
    for sweep in range(2):
        for side, u_ref in enumerate((own_u_ref, other_u_ref)):
            choices = []
            for k in range(4):
                part = parts[:, k].reshape(NB * 8, LANES)
                turn = (k - 2 * sweep - side) % 4
                choices.append(pltpu.roll(part, GROUP * turn, 1) if turn else part)
            u_ref[sweep] = pick(u_group, choices).reshape(NB, 8, LANES)


def operator_kernel(
    after_ref,
    leaf_hbm,
    coupling_hbm,
    top_hbm,
    bottom_hbm,
    own_sep_hbm,
    other_sep_hbm,
    forward_ref,
    back_ref,
    seps_ref,
    leaf_ref,
    coupling_ref,
    top_ref,
    bottom_ref,
    sep_ref,
    semaphores,
):
    copies = [
        pltpu.make_async_copy(source, target, semaphores.at[index])
        for index, (source, target) in enumerate(
            (
                (leaf_hbm, leaf_ref),
                (top_hbm, top_ref),
                (bottom_hbm, bottom_ref),
                (coupling_hbm, coupling_ref),
                (own_sep_hbm, sep_ref.at[0]),
                (other_sep_hbm, sep_ref.at[1]),
            )
        )
    ]
    for copy in copies:
        copy.start()
    for copy in copies[:3]:
        copy.wait()
    leaf = (leaf_ref[0], leaf_ref[1])
    inject = tuple(
        jnp.concatenate([top_ref[part], bottom_ref[part]], axis=0) for part in range(2)
    )
    local = complex_pair(leaf, inject, NT)
    copies[3].wait()
    coupling = (coupling_ref[0], coupling_ref[1])
    update = complex_pair(coupling, local)
    for sweep in range(2):
        for part in range(2):
            columns = slice(sweep * TR, sweep * TR + TR)
            place = slice(part * TR, part * TR + TR)
            forward_ref[sweep, : NB * RB, place] = update[part][:, columns]
            forward_ref[sweep, NB * RB :, place] = local[part][:, columns]
    back = complex_pair(leaf, coupling, NT)
    back_ref[0] = back[0]
    back_ref[1] = back[1]
    for side in range(2):
        copies[4 + side].wait()
        for part in range(2):
            seps_ref[side, part] = stacked(sep_ref[side, part])


def gather_kernel(
    own_u_hbm,
    other_u_hbm,
    own_y_hbm,
    other_y_hbm,
    own_back_hbm,
    other_back_hbm,
    own_forward_hbm,
    other_forward_hbm,
    u_ref,
    y_ref,
    backs_ref,
    forwards_ref,
    back_ref,
    forward_ref,
    semaphores,
):
    copies = [
        pltpu.make_async_copy(source, target, semaphores.at[index])
        for index, (source, target) in enumerate(
            (
                (own_back_hbm, back_ref.at[0]),
                (own_forward_hbm, forward_ref.at[0]),
                (other_back_hbm, back_ref.at[1]),
                (other_forward_hbm, forward_ref.at[1]),
                (own_u_hbm, u_ref.at[0]),
                (other_u_hbm, u_ref.at[1]),
                (own_y_hbm, y_ref.at[0]),
                (other_y_hbm, y_ref.at[1]),
            )
        )
    ]
    for copy in copies:
        copy.start()
    for side in range(2):
        copies[2 * side].wait()
        for part in range(2):
            backs_ref[side, part] = stacked(back_ref[side, part])
        copies[2 * side + 1].wait()
        for sweep in range(2):
            forwards_ref[side, sweep] = stacked(forward_ref[side, sweep])
    for copy in copies[4:]:
        copy.wait()


def stage_place(place_ref, stage):
    row = place_ref[0] // 2
    core = place_ref[0] % 2
    sweep = jnp.where(row == stage, 0, 1)
    first = jnp.where(sweep == core, 0, 1)
    return sweep, first


def wait_for(source_ref, target_ref, semaphore):
    pltpu.make_async_copy(source_ref, target_ref, semaphore).wait()


def send_blocks(choice, own_slots_ref, other_slots_ref, packed, send_ref):
    for block in range(NB):
        slot = jnp.where(choice == 0, own_slots_ref[block], other_slots_ref[block])
        send_ref[slot] = packed[block]


def first_kernel(
    place_ref,
    own_targets_ref,
    other_targets_ref,
    own_offsets_ref,
    other_offsets_ref,
    own_u_ref,
    other_u_ref,
    own_slots_ref,
    other_slots_ref,
    send_ref,
):
    leaves = send_ref.shape[0]
    sweep, first = stage_place(place_ref, 0)
    lanes = lane_ids(leaves)
    rows = lax.broadcasted_iota(jnp.int32, (leaves, LANES), 0)
    notes = jnp.full((leaves, LANES), QB, jnp.int32)
    all_slots = []
    for side, (targets_ref, offsets_ref, slots_ref) in enumerate(
        (
            (own_targets_ref, own_offsets_ref, own_slots_ref),
            (other_targets_ref, other_offsets_ref, other_slots_ref),
        )
    ):
        targets = [targets_ref[block] for block in range(NB)]
        slots = []
        for block in range(NB):
            rank = jnp.int32(0)
            for earlier in range(block):
                rank = rank + jnp.where(targets[earlier] == targets[block], 1, 0)
            slot = targets[block] * CAP + rank
            slots_ref[block] = slot
            slots.append(slot)
            here = (rows == targets[block]) & (lanes == CAP * side + rank)
            notes = jnp.where(here, offsets_ref[block], notes)
        all_slots.append(slots)
    send_ref[:, CAP * 8 :, :] = jnp.broadcast_to(
        notes.astype(f32)[:, None, :], (leaves, 8, LANES)
    )
    packed = jnp.where(first == 0, own_u_ref[sweep], other_u_ref[sweep])
    for block in range(NB):
        slot = jnp.where(first == 0, all_slots[0][block], all_slots[1][block])
        row = pl.multiple_of((slot % CAP) * 8, 8)
        send_ref[slot // CAP, pl.ds(row, 8), :] = packed[block]


def separator_solve(choice, offsets_ref, arrived, seps_ref, reply_ref, solved_ref, *total_refs):
    leaves = reply_ref.shape[0] // CAP
    for total_ref in total_refs:
        total_ref[...] = jnp.zeros_like(total_ref)
    places = []
    for leaf in range(leaves):
        for rank in range(CAP):
            place = offsets_ref[CAP * choice + rank, leaf]
            total_ref = total_refs[len(places) % len(total_refs)]
            places.append(place)
            total_ref[place] = total_ref[place] + arrived(leaf, rank)
    total = total_refs[0][:QB]
    for total_ref in total_refs[1:]:
        total = total + total_ref[:QB]
    rhs, rhs_turned = unpack_both(total)
    solved = stacked_product(
        ((seps_ref[choice, 0], rhs), (seps_ref[choice, 1], rhs_turned))
    )
    solved_ref[:QB] = pack(solved)
    solved_ref[QB] = jnp.zeros((8, LANES), f32)
    for slot, place in enumerate(places):
        reply_ref[slot] = solved_ref[place]


def separator_kernel(
    stage, step, place_ref, offsets_ref, arrived_ref, seps_ref, reply_ref, *scratch
):
    sweep, first = stage_place(place_ref, stage)
    separator_solve(
        first if step == 0 else 1 - first,
        offsets_ref,
        lambda leaf, rank: arrived_ref[CAP * leaf + rank],
        seps_ref,
        reply_ref,
        *scratch,
    )


def first_separator_kernel(
    place_ref,
    arrived_ref,
    seps_ref,
    forward_in_hbm,
    back_in_hbm,
    offsets_ref,
    reply_ref,
    forward_out_hbm,
    back_out_hbm,
    notes_ref,
    semaphore,
    *scratch,
):
    sweep, first = stage_place(place_ref, 0)
    leaves = arrived_ref.shape[0]
    notes = arrived_ref[:, CAP * 8, :]
    whole = jnp.concatenate([notes, jnp.zeros((LANES - leaves, LANES), f32)], axis=0)
    notes_ref[...] = whole.T[:8].astype(jnp.int32)
    copy = pltpu.make_async_copy(notes_ref, offsets_ref, semaphore)
    copy.start()
    copy.wait()
    separator_solve(
        first,
        offsets_ref,
        lambda leaf, rank: arrived_ref[leaf, 8 * rank : 8 * rank + 8, :],
        seps_ref,
        reply_ref,
        *scratch,
    )


def leaf_finish(choice, own_slots_ref, other_slots_ref, returned_ref, backs_ref, base):
    blocks = []
    for block in range(NB):
        slot = jnp.where(choice == 0, own_slots_ref[block], other_slots_ref[block])
        blocks.append(returned_ref[slot])
    mine, mine_turned = unpack_both(jnp.stack(blocks, axis=0))
    return base + stacked_product(
        ((backs_ref[choice, 0], mine), (backs_ref[choice, 1], mine_turned))
    )


def leaf_begin(
    sweep,
    choice,
    trace,
    trace_turned,
    own_slots_ref,
    other_slots_ref,
    u_ref,
    y_ref,
    forwards_ref,
    send_ref,
    base_ref,
):
    driven = stacked_product(
        ((forwards_ref[choice, sweep], jnp.concatenate([trace, trace_turned], axis=0)),)
    )
    packed = pack(driven[: NB * RB]) + u_ref[choice, sweep]
    send_blocks(choice, own_slots_ref, other_slots_ref, packed, send_ref)
    base_ref[...] = driven[NB * RB :] + y_ref[choice, sweep]


def trace_rows(sweep, field_ref):
    return field_ref[pl.ds(pl.multiple_of((1 - sweep) * TR, TR), TR), :]


def middle_kernel(
    stage,
    place_ref,
    own_slots_ref,
    other_slots_ref,
    u_ref,
    y_ref,
    forwards_ref,
    backs_ref,
    returned_ref,
    base_refs,
    field_ref,
    send_ref,
    next_base_ref,
):
    sweep, first = stage_place(place_ref, stage)
    base = base_refs[0][...] if base_refs else y_ref[first, sweep]
    field_ref[...] = leaf_finish(
        first, own_slots_ref, other_slots_ref, returned_ref, backs_ref, base
    )
    trace = trace_rows(sweep, field_ref)
    leaf_begin(
        sweep,
        1 - first,
        trace,
        turned(trace),
        own_slots_ref,
        other_slots_ref,
        u_ref,
        y_ref,
        forwards_ref,
        send_ref,
        next_base_ref,
    )


def last_kernel(
    stage,
    place_ref,
    own_slots_ref,
    other_slots_ref,
    backs_ref,
    returned_ref,
    base_ref,
    field_ref,
    trace_ref,
):
    sweep, first = stage_place(place_ref, stage)
    field_ref[...] = leaf_finish(
        1 - first, own_slots_ref, other_slots_ref, returned_ref, backs_ref, base_ref[...]
    )
    trace_ref[...] = pack(trace_rows(sweep, field_ref))


def enter_kernel(
    stage,
    place_ref,
    own_slots_ref,
    other_slots_ref,
    u_ref,
    y_ref,
    forwards_ref,
    trace_ref,
    send_ref,
    next_base_ref,
):
    sweep, first = stage_place(place_ref, stage)
    trace, trace_turned = unpack_both(trace_ref[...])
    leaf_begin(
        sweep,
        first,
        trace,
        trace_turned,
        own_slots_ref,
        other_slots_ref,
        u_ref,
        y_ref,
        forwards_ref,
        send_ref,
        next_base_ref,
    )


def collect_kernel(place_ref, field_refs, own_ref, other_ref, parts_ref, semaphores):
    row = place_ref[0] // 2
    core = place_ref[0] % 2
    for sweep in range(2):
        for position in range(2):
            layer = position if sweep == 0 else 1 - position
            side = jnp.where(core == layer, 0, 1)
            for stage in range(4):
                active = row == stage if sweep == 0 else row == 3 - stage

                @pl.when(active)
                def _():
                    pltpu.make_async_copy(
                        field_refs[2 * stage + position],
                        parts_ref.at[2 * sweep + side],
                        semaphores.at[2 * sweep + position],
                    ).start()

    for index in range(4):
        wait_for(field_refs[0], parts_ref.at[0], semaphores.at[index])
    group = lane_ids(P_SIZE) // GROUP
    joined = pick(group, [parts_ref[index] for index in range(4)])
    rows = joined.T.reshape(2, 2, 2, HALF, P_SIZE)
    own_ref[...] = rows[:, 0]
    other_ref[...] = rows[:, 1]


def output_kernel(place_ref, own_ref, other_ref, down_ref, up_ref):
    core = place_ref[0] % 2
    for sweep, field_ref in enumerate((down_ref, up_ref)):
        for part in range(2):
            field_ref[part, pl.ds(pl.multiple_of(core * HALF, HALF), HALF), :] = own_ref[sweep, part]
            field_ref[part, pl.ds(pl.multiple_of((1 - core) * HALF, HALF), HALF), :] = other_ref[
                sweep, part
            ]


def call(
    kernel, outs, in_specs, out_specs, scratch=(), cost=None, limit=VMEM_LIMIT, aliases=None
):
    return pl.pallas_call(
        kernel,
        out_shape=outs,
        in_specs=in_specs,
        out_specs=out_specs,
        scratch_shapes=list(scratch),
        compiler_params=pltpu.CompilerParams(vmem_limit_bytes=limit),
        cost_estimate=cost,
        input_output_aliases=aliases or {},
    )


def shape(*dims, dtype=f32):
    return jax.ShapeDtypeStruct(dims, dtype)


def cost_of(flops, size):
    return pl.CostEstimate(flops=flops, bytes_accessed=size, transcendentals=0)


def across_cores(value):
    layers = lax.axis_size("layer")
    return lax.ppermute(value, "layer", [(index, index ^ 1) for index in range(layers)])


def exchange(value):
    return lax.all_to_all(value, "front", split_axis=0, concat_axis=0, tiled=True)


def to_next_stage(value, stage):
    moves = [(stage, stage + 1), (3 - stage, 2 - stage)]
    pairs = [(2 * a + core, 2 * b + core) for a, b in moves for core in range(2)]
    return lax.ppermute(value, "layer", pairs)


def body(
    sources_down,
    sources_up,
    leaf_inverse,
    coupling,
    sep_inverse,
    inject_top,
    inject_bottom,
    targets,
    offsets,
):
    leaves = lax.axis_size("front")
    slots = leaves * CAP
    place = lax.axis_index("layer").reshape(1).astype(jnp.int32)
    leaf = leaf_inverse[0, 0]
    rows = coupling[0, 0]
    sep = sep_inverse[0, 0]
    own_targets = targets[0, 0, :, 0]
    other_targets = across_cores(own_targets)
    other_offsets = across_cores(offsets[0, 0])
    other_sep = across_cores(sep)

    source_scratch = pltpu.VMEM((2, S, P_SIZE), f32)
    leaf_scratch = pltpu.VMEM((2, P_SIZE, P_SIZE), f32)
    rows_scratch = pltpu.VMEM((2, NB * RB, P_SIZE), f32)
    inject_scratch = pltpu.VMEM((2, TR, P_SIZE), f32)
    u_shape = shape(2, NB, 8, LANES)
    y_shape = shape(2, P_SIZE, LANES)
    own_u, to_other_u, own_y, to_other_y = call(
        source_kernel,
        (u_shape, u_shape, y_shape, y_shape),
        [smem] + [hbm] * 4,
        (vmem,) * 4,
        [
            source_scratch,
            source_scratch,
            leaf_scratch,
            rows_scratch,
            pltpu.SemaphoreType.DMA((4,)),
        ],
        cost_of(600_000_000, 2_500_000),
        ALMOST_ALL_VMEM,
    )(place, sources_down[0, 0], sources_up[0, 0], leaf, rows)
    other_u = across_cores(to_other_u)

    slot_shape = shape(slots, 8, LANES)
    field_shape = shape(P_SIZE, LANES)
    slots_shape = shape(NB, dtype=jnp.int32)
    own_slots, other_slots, send = call(
        first_kernel,
        (slots_shape, slots_shape, shape(leaves, (CAP + 1) * 8, LANES)),
        [smem] * 5 + [vmem] * 2,
        (smem, smem, vmem),
    )(place, own_targets, other_targets, offsets[0, 0], other_offsets, own_u, other_u)
    arrived = exchange(send)

    own_forward, own_back, seps = call(
        operator_kernel,
        (
            shape(2, NB * RB + P_SIZE, 2 * TR),
            shape(2, P_SIZE, NB * RB),
            shape(2, 2, 2 * Q, Q, dtype=bf16),
        ),
        [hbm] * 7,
        (vmem,) * 3,
        [
            leaf_scratch,
            rows_scratch,
            inject_scratch,
            inject_scratch,
            pltpu.VMEM((2, 2, Q, Q), f32),
            pltpu.SemaphoreType.DMA((6,)),
        ],
        cost_of(4_000_000_000, 5_000_000),
    )(send, leaf, rows, inject_top[0, 0], inject_bottom[0, 0], sep, other_sep)
    separator_scratch = [pltpu.VMEM((QB + 1, 8, LANES), f32)] * 5
    places, reply, own_forward, own_back = call(
        first_separator_kernel,
        (
            shape(8, LANES, dtype=jnp.int32),
            slot_shape,
            shape(*own_forward.shape),
            shape(*own_back.shape),
        ),
        [smem, vmem, vmem, hbm, hbm],
        (smem, vmem, hbm, hbm),
        [pltpu.VMEM((8, LANES), jnp.int32), pltpu.SemaphoreType.DMA] + separator_scratch,
        cost_of(100_000_000, 1_100_000),
        aliases={3: 2, 4: 3},
    )(place, arrived, seps, own_forward, own_back)
    other_y = across_cores(to_other_y)
    other_back = across_cores(own_back)
    other_forward = across_cores(own_forward)

    u, y, backs, forwards = call(
        gather_kernel,
        (
            shape(2, 2, NB, 8, LANES),
            shape(2, 2, P_SIZE, LANES),
            shape(2, 2, 2 * P_SIZE, NB * RB, dtype=bf16),
            shape(2, 2, 2 * (NB * RB + P_SIZE), 2 * TR, dtype=bf16),
        ),
        [hbm] * 8,
        (vmem,) * 4,
        [
            pltpu.VMEM((2, 2, P_SIZE, NB * RB), f32),
            pltpu.VMEM((2, 2, NB * RB + P_SIZE, 2 * TR), f32),
            pltpu.SemaphoreType.DMA((8,)),
        ],
        cost_of(10_000_000, 12_000_000),
    )(own_u, other_u, own_y, other_y, own_back, other_back, own_forward, other_forward)

    def separator(stage, step, arrived):
        return call(
            functools.partial(separator_kernel, stage, step),
            slot_shape,
            [smem] * 2 + [vmem] * 2,
            vmem,
            separator_scratch,
            cost_of(100_000_000, 1_100_000),
        )(place, places, arrived, seps)

    fields = []
    base = None
    trace = None
    for stage in range(4):
        if stage > 0:
            send, base = call(
                functools.partial(enter_kernel, stage),
                (slot_shape, field_shape),
                [smem] * 3 + [vmem] * 4,
                (vmem, vmem),
                cost=cost_of(100_000_000, 2_000_000),
            )(place, own_slots, other_slots, u, y, forwards, trace)
            reply = separator(stage, 0, exchange(send))
        returned = exchange(reply)
        bases = [] if base is None else [base]

        def middle(*refs, stage=stage, count=len(bases)):
            head, rest = refs[:8], refs[8:]
            middle_kernel(stage, *head, rest[:count], *rest[count:])

        field, send, base = call(
            middle,
            (field_shape, slot_shape, field_shape),
            [smem] * 3 + [vmem] * (5 + len(bases)),
            (vmem,) * 3,
            cost=cost_of(300_000_000, 3_000_000),
        )(place, own_slots, other_slots, u, y, forwards, backs, returned, *bases)
        fields.append(field)
        returned = exchange(separator(stage, 1, exchange(send)))
        field, trace = call(
            functools.partial(last_kernel, stage),
            (field_shape, shape(TR // RB, 8, LANES)),
            [smem] * 3 + [vmem] * 3,
            (vmem, vmem),
            cost=cost_of(200_000_000, 2_000_000),
        )(place, own_slots, other_slots, backs, returned, base)
        fields.append(field)
        if stage < 3:
            trace = to_next_stage(trace, stage)

    half_shape = shape(2, 2, HALF, P_SIZE)

    def collect(place_ref, *refs):
        collect_kernel(place_ref, refs[:8], *refs[8:])

    own, to_other = call(
        collect,
        (half_shape, half_shape),
        [smem] + [hbm] * 8,
        (vmem, vmem),
        [pltpu.VMEM((4, P_SIZE, LANES), f32), pltpu.SemaphoreType.DMA((4,))],
    )(place, *fields)
    down, up = call(
        output_kernel,
        (shape(2, S, P_SIZE), shape(2, S, P_SIZE)),
        [smem, vmem, vmem],
        (vmem, vmem),
    )(place, own, across_cores(to_other))
    return down[None, None], up[None, None]


def solution(mesh):
    whole = P("layer", "front", None, None, None)
    return jax.shard_map(
        body,
        mesh=mesh,
        in_specs=(whole,) * 7 + (P("layer", "front", None, None), P("layer", "front", None)),
        out_specs=(whole, whole),
        check_vma=False,
    )
```

```python
import functools

import jax
import jax.numpy as jnp
from jax import lax
from jax.experimental import pallas as pl
from jax.experimental.pallas import tpu as pltpu
from jax.sharding import PartitionSpec as P


P_SIZE = 256
Q = 256
TR = 128
RB = 32
S = 32
NB = 16
QB = 8
CAP = 2
HALF = 16
GROUP = 32
LANES = 128

f32 = jnp.float32
bf16 = jnp.bfloat16
VMEM_LIMIT = 48 * 1024 * 1024
ALMOST_ALL_VMEM = 60 * 1024 * 1024
smem = pl.BlockSpec(memory_space=pltpu.SMEM)
vmem = pl.BlockSpec(memory_space=pltpu.VMEM)
hbm = pl.BlockSpec(memory_space=pl.ANY)
NN = (((1,), (0,)), ((), ()))
NT = (((1,), (1,)), ((), ()))


def halves(value):
    high = value.astype(bf16)
    return high, (value - high.astype(f32)).astype(bf16)


def dot(first, second, dims=NN):
    return lax.dot_general(first, second, dims, preferred_element_type=f32)


def product(first, second, dims=NN):
    first_high, first_low = halves(first)
    second_high, second_low = halves(second)
    return (
        dot(first_high, second_high, dims)
        + dot(first_high, second_low, dims)
        + dot(first_low, second_high, dims)
    )


def narrow_product(first, second):
    first_high, first_low = halves(first)
    second_high, second_low = halves(second)
    both = dot(first_high, jnp.concatenate([second_high, second_low], axis=1))
    return both[:, :LANES] + both[:, LANES:] + dot(first_low, second_high)


def stacked(value):
    return jnp.concatenate(halves(value), axis=0)


def stacked_product(first, second):
    rows = first.shape[0] // 2
    both = dot(first, jnp.concatenate(halves(second), axis=1))
    return (both[:rows, :LANES] + both[:rows, LANES:]) + (both[rows:, :LANES] + both[rows:, LANES:])


def complex_pair(first, second, dims=NN):
    real = product(first[0], second[0], dims) - product(first[1], second[1], dims)
    imag = product(first[0], second[1], dims) + product(first[1], second[0], dims)
    return real, imag


def lane_ids(rows):
    return lax.broadcasted_iota(jnp.int32, (rows, LANES), 1)


def turned(value):
    lanes = lane_ids(value.shape[0])
    ahead = pltpu.roll(value, LANES - HALF, 1)
    behind = pltpu.roll(value, HALF, 1)
    return jnp.where(lanes % GROUP < HALF, -ahead, behind)


def pick(group, choices):
    return jnp.where(
        group == 0,
        choices[0],
        jnp.where(group == 1, choices[1], jnp.where(group == 2, choices[2], choices[3])),
    )


def rotations(value):
    return [value] + [pltpu.roll(value, GROUP * turn, 1) for turn in (1, 2, 3)]


def spread_group(rolled, group, source):
    return pick(group, [rolled[(place - source) % 4] for place in range(4)])


def unpack(packed):
    count = packed.shape[0]
    flat = packed.reshape(count * 8, LANES)
    group = lane_ids(count * 8) // GROUP
    rolled = rotations(flat)
    parts = [spread_group(rolled, group, k).reshape(count, 8, LANES) for k in range(4)]
    return jnp.stack(parts, axis=1).reshape(count * RB, LANES)


def unpack_both(packed):
    count = packed.shape[0]
    flat = packed.reshape(count * 8, LANES)
    return unpack(packed), unpack(turned(flat).reshape(count, 8, LANES))


def pack(spread):
    count = spread.shape[0] // RB
    parts = spread.reshape(count, 4, 8, LANES)
    group = lax.broadcasted_iota(jnp.int32, (count, 8, LANES), 2) // GROUP
    return pick(group, [parts[:, k] for k in range(4)])


def source_kernel(
    place_ref,
    down_hbm,
    up_hbm,
    leaf_hbm,
    coupling_hbm,
    own_u_ref,
    other_u_ref,
    own_y_ref,
    other_y_ref,
    down_ref,
    up_ref,
    leaf_ref,
    coupling_ref,
    semaphores,
):
    copies = [
        pltpu.make_async_copy(source, target, semaphores.at[index])
        for index, (source, target) in enumerate(
            (
                (down_hbm, down_ref),
                (up_hbm, up_ref),
                (leaf_hbm, leaf_ref),
                (coupling_hbm, coupling_ref),
            )
        )
    ]
    for copy in copies:
        copy.start()
    core = place_ref[0] % 2
    own_row = pl.multiple_of(core * HALF, HALF)
    other_row = pl.multiple_of((1 - core) * HALF, HALF)
    copies[0].wait()
    copies[1].wait()
    rows, turned_rows = [], []
    for source in (down_ref, up_ref):
        for start in (own_row, other_row):
            real = source[0, pl.ds(start, HALF), :]
            imag = source[1, pl.ds(start, HALF), :]
            rows += [real, imag]
            turned_rows += [-imag, real]
    copies[2].wait()
    y = product(leaf_ref[0], jnp.concatenate(rows, axis=0), NT) + product(
        leaf_ref[1], jnp.concatenate(turned_rows, axis=0), NT
    )
    rolled = rotations(y)
    y_group = lane_ids(P_SIZE) // GROUP
    for sweep in range(2):
        for side, y_ref in enumerate((own_y_ref, other_y_ref)):
            y_ref[sweep] = spread_group(rolled, y_group, 2 * sweep + side)
    copies[3].wait()
    u = narrow_product(coupling_ref[0], y) + narrow_product(coupling_ref[1], turned(y))
    parts = u.reshape(NB, 4, 8, LANES)
    u_group = lane_ids(NB * 8) // GROUP
    for sweep in range(2):
        for side, u_ref in enumerate((own_u_ref, other_u_ref)):
            choices = []
            for k in range(4):
                part = parts[:, k].reshape(NB * 8, LANES)
                turn = (k - 2 * sweep - side) % 4
                choices.append(pltpu.roll(part, GROUP * turn, 1) if turn else part)
            u_ref[sweep] = pick(u_group, choices).reshape(NB, 8, LANES)


def operator_kernel(
    after_ref,
    leaf_hbm,
    coupling_hbm,
    top_hbm,
    bottom_hbm,
    own_sep_hbm,
    other_sep_hbm,
    forward_ref,
    back_ref,
    seps_ref,
    leaf_ref,
    coupling_ref,
    top_ref,
    bottom_ref,
    sep_ref,
    semaphores,
):
    copies = [
        pltpu.make_async_copy(source, target, semaphores.at[index])
        for index, (source, target) in enumerate(
            (
                (leaf_hbm, leaf_ref),
                (top_hbm, top_ref),
                (bottom_hbm, bottom_ref),
                (coupling_hbm, coupling_ref),
                (own_sep_hbm, sep_ref.at[0]),
                (other_sep_hbm, sep_ref.at[1]),
            )
        )
    ]
    for copy in copies:
        copy.start()
    for copy in copies[:3]:
        copy.wait()
    leaf = (leaf_ref[0], leaf_ref[1])
    inject = tuple(
        jnp.concatenate([top_ref[part], bottom_ref[part]], axis=0) for part in range(2)
    )
    local = complex_pair(leaf, inject, NT)
    copies[3].wait()
    coupling = (coupling_ref[0], coupling_ref[1])
    update = complex_pair(coupling, local)
    for sweep in range(2):
        for part in range(2):
            columns = slice(sweep * TR, sweep * TR + TR)
            place = slice(part * TR, part * TR + TR)
            forward_ref[sweep, : NB * RB, place] = update[part][:, columns]
            forward_ref[sweep, NB * RB :, place] = local[part][:, columns]
    back = complex_pair(leaf, coupling, NT)
    back_ref[0] = back[0]
    back_ref[1] = back[1]
    for side in range(2):
        copies[4 + side].wait()
        for part in range(2):
            seps_ref[side, part] = stacked(sep_ref[side, part])


def gather_kernel(
    own_u_hbm,
    other_u_hbm,
    own_y_hbm,
    other_y_hbm,
    own_back_hbm,
    other_back_hbm,
    own_forward_hbm,
    other_forward_hbm,
    u_ref,
    y_ref,
    backs_ref,
    forwards_ref,
    back_ref,
    forward_ref,
    semaphores,
):
    copies = [
        pltpu.make_async_copy(source, target, semaphores.at[index])
        for index, (source, target) in enumerate(
            (
                (own_back_hbm, back_ref.at[0]),
                (own_forward_hbm, forward_ref.at[0]),
                (other_back_hbm, back_ref.at[1]),
                (other_forward_hbm, forward_ref.at[1]),
                (own_u_hbm, u_ref.at[0]),
                (other_u_hbm, u_ref.at[1]),
                (own_y_hbm, y_ref.at[0]),
                (other_y_hbm, y_ref.at[1]),
            )
        )
    ]
    for copy in copies:
        copy.start()
    for side in range(2):
        copies[2 * side].wait()
        for part in range(2):
            backs_ref[side, part] = stacked(back_ref[side, part])
        copies[2 * side + 1].wait()
        for sweep in range(2):
            forwards_ref[side, sweep] = stacked(forward_ref[side, sweep])
    for copy in copies[4:]:
        copy.wait()


def stage_place(place_ref, stage):
    row = place_ref[0] // 2
    core = place_ref[0] % 2
    sweep = jnp.where(row == stage, 0, 1)
    first = jnp.where(sweep == core, 0, 1)
    return sweep, first


def wait_for(source_ref, target_ref, semaphore):
    pltpu.make_async_copy(source_ref, target_ref, semaphore).wait()


def send_blocks(choice, own_slots_ref, other_slots_ref, packed, send_ref):
    for block in range(NB):
        slot = jnp.where(choice == 0, own_slots_ref[block], other_slots_ref[block])
        send_ref[slot] = packed[block]


def first_kernel(
    place_ref,
    own_targets_ref,
    other_targets_ref,
    own_offsets_ref,
    other_offsets_ref,
    own_u_ref,
    other_u_ref,
    own_slots_ref,
    other_slots_ref,
    send_ref,
):
    leaves = send_ref.shape[0]
    sweep, first = stage_place(place_ref, 0)
    lanes = lane_ids(leaves)
    rows = lax.broadcasted_iota(jnp.int32, (leaves, LANES), 0)
    notes = jnp.full((leaves, LANES), QB, jnp.int32)
    all_slots = []
    for side, (targets_ref, offsets_ref, slots_ref) in enumerate(
        (
            (own_targets_ref, own_offsets_ref, own_slots_ref),
            (other_targets_ref, other_offsets_ref, other_slots_ref),
        )
    ):
        targets = [targets_ref[block] for block in range(NB)]
        slots = []
        for block in range(NB):
            rank = jnp.int32(0)
            for earlier in range(block):
                rank = rank + jnp.where(targets[earlier] == targets[block], 1, 0)
            slot = targets[block] * CAP + rank
            slots_ref[block] = slot
            slots.append(slot)
            here = (rows == targets[block]) & (lanes == CAP * side + rank)
            notes = jnp.where(here, offsets_ref[block], notes)
        all_slots.append(slots)
    send_ref[:, CAP * 8 :, :] = jnp.broadcast_to(
        notes.astype(f32)[:, None, :], (leaves, 8, LANES)
    )
    packed = jnp.where(first == 0, own_u_ref[sweep], other_u_ref[sweep])
    for block in range(NB):
        slot = jnp.where(first == 0, all_slots[0][block], all_slots[1][block])
        row = pl.multiple_of((slot % CAP) * 8, 8)
        send_ref[slot // CAP, pl.ds(row, 8), :] = packed[block]


def separator_solve(choice, offsets_ref, arrived, seps_ref, reply_ref, even_ref, odd_ref, solved_ref):
    leaves = reply_ref.shape[0] // CAP
    even_ref[...] = jnp.zeros_like(even_ref)
    odd_ref[...] = jnp.zeros_like(odd_ref)
    places = []
    for leaf in range(leaves):
        for rank, total_ref in enumerate((even_ref, odd_ref)):
            place = offsets_ref[CAP * choice + rank, leaf]
            places.append(place)
            total_ref[place] = total_ref[place] + arrived(leaf, rank)
    rhs, rhs_turned = unpack_both(even_ref[:QB] + odd_ref[:QB])
    solved = stacked_product(seps_ref[choice, 0], rhs) + stacked_product(
        seps_ref[choice, 1], rhs_turned
    )
    solved_ref[:QB] = pack(solved)
    solved_ref[QB] = jnp.zeros((8, LANES), f32)
    for slot, place in enumerate(places):
        reply_ref[slot] = solved_ref[place]


def separator_kernel(
    stage, step, place_ref, offsets_ref, arrived_ref, seps_ref, reply_ref, *scratch
):
    sweep, first = stage_place(place_ref, stage)
    separator_solve(
        first if step == 0 else 1 - first,
        offsets_ref,
        lambda leaf, rank: arrived_ref[CAP * leaf + rank],
        seps_ref,
        reply_ref,
        *scratch,
    )


def first_separator_kernel(
    place_ref,
    arrived_ref,
    seps_ref,
    forward_in_hbm,
    back_in_hbm,
    offsets_ref,
    reply_ref,
    forward_out_hbm,
    back_out_hbm,
    notes_ref,
    semaphore,
    *scratch,
):
    sweep, first = stage_place(place_ref, 0)
    leaves = arrived_ref.shape[0]
    notes = arrived_ref[:, CAP * 8, :]
    whole = jnp.concatenate([notes, jnp.zeros((LANES - leaves, LANES), f32)], axis=0)
    notes_ref[...] = whole.T[:8].astype(jnp.int32)
    copy = pltpu.make_async_copy(notes_ref, offsets_ref, semaphore)
    copy.start()
    copy.wait()
    separator_solve(
        first,
        offsets_ref,
        lambda leaf, rank: arrived_ref[leaf, 8 * rank : 8 * rank + 8, :],
        seps_ref,
        reply_ref,
        *scratch,
    )


def leaf_finish(choice, own_slots_ref, other_slots_ref, returned_ref, backs_ref, base):
    blocks = []
    for block in range(NB):
        slot = jnp.where(choice == 0, own_slots_ref[block], other_slots_ref[block])
        blocks.append(returned_ref[slot])
    mine, mine_turned = unpack_both(jnp.stack(blocks, axis=0))
    return (
        base
        + stacked_product(backs_ref[choice, 0], mine)
        + stacked_product(backs_ref[choice, 1], mine_turned)
    )


def leaf_begin(
    sweep,
    choice,
    trace,
    trace_turned,
    own_slots_ref,
    other_slots_ref,
    u_ref,
    y_ref,
    forward,
    send_ref,
    base_ref,
):
    driven = stacked_product(forward, jnp.concatenate([trace, trace_turned], axis=0))
    packed = pack(driven[: NB * RB]) + u_ref[choice, sweep]
    send_blocks(choice, own_slots_ref, other_slots_ref, packed, send_ref)
    base_ref[...] = driven[NB * RB :] + y_ref[choice, sweep]


def trace_rows(sweep, field_ref):
    return field_ref[pl.ds(pl.multiple_of((1 - sweep) * TR, TR), TR), :]


def middle_kernel(
    stage,
    place_ref,
    own_slots_ref,
    other_slots_ref,
    u_ref,
    y_ref,
    forwards_hbm,
    backs_ref,
    returned_ref,
    base_refs,
    field_ref,
    send_ref,
    next_base_ref,
    forward_ref,
    semaphore,
):
    sweep, first = stage_place(place_ref, stage)
    copy = pltpu.make_async_copy(forwards_hbm.at[1 - first, sweep], forward_ref, semaphore)
    copy.start()
    base = base_refs[0][...] if base_refs else y_ref[first, sweep]
    field_ref[...] = leaf_finish(
        first, own_slots_ref, other_slots_ref, returned_ref, backs_ref, base
    )
    trace = trace_rows(sweep, field_ref)
    copy.wait()
    leaf_begin(
        sweep,
        1 - first,
        trace,
        turned(trace),
        own_slots_ref,
        other_slots_ref,
        u_ref,
        y_ref,
        forward_ref[...],
        send_ref,
        next_base_ref,
    )


def last_kernel(
    stage,
    place_ref,
    own_slots_ref,
    other_slots_ref,
    backs_ref,
    returned_ref,
    base_ref,
    field_ref,
    trace_ref,
):
    sweep, first = stage_place(place_ref, stage)
    field_ref[...] = leaf_finish(
        1 - first, own_slots_ref, other_slots_ref, returned_ref, backs_ref, base_ref[...]
    )
    trace_ref[...] = pack(trace_rows(sweep, field_ref))


def enter_kernel(
    stage,
    place_ref,
    own_slots_ref,
    other_slots_ref,
    u_ref,
    y_ref,
    forwards_ref,
    trace_ref,
    send_ref,
    next_base_ref,
):
    sweep, first = stage_place(place_ref, stage)
    trace, trace_turned = unpack_both(trace_ref[...])
    leaf_begin(
        sweep,
        first,
        trace,
        trace_turned,
        own_slots_ref,
        other_slots_ref,
        u_ref,
        y_ref,
        forwards_ref[first, sweep],
        send_ref,
        next_base_ref,
    )


def collect_kernel(place_ref, field_refs, own_ref, other_ref, parts_ref, semaphores):
    row = place_ref[0] // 2
    core = place_ref[0] % 2
    for sweep in range(2):
        for position in range(2):
            layer = position if sweep == 0 else 1 - position
            side = jnp.where(core == layer, 0, 1)
            for stage in range(4):
                active = row == stage if sweep == 0 else row == 3 - stage

                @pl.when(active)
                def _():
                    pltpu.make_async_copy(
                        field_refs[2 * stage + position],
                        parts_ref.at[2 * sweep + side],
                        semaphores.at[2 * sweep + position],
                    ).start()

    for index in range(4):
        wait_for(field_refs[0], parts_ref.at[0], semaphores.at[index])
    group = lane_ids(P_SIZE) // GROUP
    joined = pick(group, [parts_ref[index] for index in range(4)])
    rows = joined.T.reshape(2, 2, 2, HALF, P_SIZE)
    own_ref[...] = rows[:, 0]
    other_ref[...] = rows[:, 1]


def output_kernel(place_ref, own_ref, other_ref, down_ref, up_ref):
    core = place_ref[0] % 2
    for sweep, field_ref in enumerate((down_ref, up_ref)):
        for part in range(2):
            field_ref[part, pl.ds(pl.multiple_of(core * HALF, HALF), HALF), :] = own_ref[sweep, part]
            field_ref[part, pl.ds(pl.multiple_of((1 - core) * HALF, HALF), HALF), :] = other_ref[
                sweep, part
            ]


def call(
    kernel, outs, in_specs, out_specs, scratch=(), cost=None, limit=VMEM_LIMIT, aliases=None
):
    return pl.pallas_call(
        kernel,
        out_shape=outs,
        in_specs=in_specs,
        out_specs=out_specs,
        scratch_shapes=list(scratch),
        compiler_params=pltpu.CompilerParams(vmem_limit_bytes=limit),
        cost_estimate=cost,
        input_output_aliases=aliases or {},
    )


def shape(*dims, dtype=f32):
    return jax.ShapeDtypeStruct(dims, dtype)


def cost_of(flops, size):
    return pl.CostEstimate(flops=flops, bytes_accessed=size, transcendentals=0)


def across_cores(value):
    layers = lax.axis_size("layer")
    return lax.ppermute(value, "layer", [(index, index ^ 1) for index in range(layers)])


def exchange(value):
    return lax.all_to_all(value, "front", split_axis=0, concat_axis=0, tiled=True)


def to_next_stage(value, stage):
    moves = [(stage, stage + 1), (3 - stage, 2 - stage)]
    pairs = [(2 * a + core, 2 * b + core) for a, b in moves for core in range(2)]
    return lax.ppermute(value, "layer", pairs)


def body(
    sources_down,
    sources_up,
    leaf_inverse,
    coupling,
    sep_inverse,
    inject_top,
    inject_bottom,
    targets,
    offsets,
):
    leaves = lax.axis_size("front")
    slots = leaves * CAP
    place = lax.axis_index("layer").reshape(1).astype(jnp.int32)
    leaf = leaf_inverse[0, 0]
    rows = coupling[0, 0]
    sep = sep_inverse[0, 0]
    own_targets = targets[0, 0, :, 0]
    other_targets = across_cores(own_targets)
    other_offsets = across_cores(offsets[0, 0])
    other_sep = across_cores(sep)

    source_scratch = pltpu.VMEM((2, S, P_SIZE), f32)
    leaf_scratch = pltpu.VMEM((2, P_SIZE, P_SIZE), f32)
    rows_scratch = pltpu.VMEM((2, NB * RB, P_SIZE), f32)
    inject_scratch = pltpu.VMEM((2, TR, P_SIZE), f32)
    u_shape = shape(2, NB, 8, LANES)
    y_shape = shape(2, P_SIZE, LANES)
    own_u, to_other_u, own_y, to_other_y = call(
        source_kernel,
        (u_shape, u_shape, y_shape, y_shape),
        [smem] + [hbm] * 4,
        (vmem,) * 4,
        [
            source_scratch,
            source_scratch,
            leaf_scratch,
            rows_scratch,
            pltpu.SemaphoreType.DMA((4,)),
        ],
        cost_of(600_000_000, 2_500_000),
        ALMOST_ALL_VMEM,
    )(place, sources_down[0, 0], sources_up[0, 0], leaf, rows)
    other_u = across_cores(to_other_u)

    slot_shape = shape(slots, 8, LANES)
    field_shape = shape(P_SIZE, LANES)
    slots_shape = shape(NB, dtype=jnp.int32)
    own_slots, other_slots, send = call(
        first_kernel,
        (slots_shape, slots_shape, shape(leaves, (CAP + 1) * 8, LANES)),
        [smem] * 5 + [vmem] * 2,
        (smem, smem, vmem),
    )(place, own_targets, other_targets, offsets[0, 0], other_offsets, own_u, other_u)
    arrived = exchange(send)

    own_forward, own_back, seps = call(
        operator_kernel,
        (
            shape(2, NB * RB + P_SIZE, 2 * TR),
            shape(2, P_SIZE, NB * RB),
            shape(2, 2, 2 * Q, Q, dtype=bf16),
        ),
        [hbm] * 7,
        (vmem,) * 3,
        [
            leaf_scratch,
            rows_scratch,
            inject_scratch,
            inject_scratch,
            pltpu.VMEM((2, 2, Q, Q), f32),
            pltpu.SemaphoreType.DMA((6,)),
        ],
        cost_of(4_000_000_000, 5_000_000),
    )(send, leaf, rows, inject_top[0, 0], inject_bottom[0, 0], sep, other_sep)
    separator_scratch = [pltpu.VMEM((QB + 1, 8, LANES), f32)] * 3
    places, reply, own_forward, own_back = call(
        first_separator_kernel,
        (
            shape(8, LANES, dtype=jnp.int32),
            slot_shape,
            shape(*own_forward.shape),
            shape(*own_back.shape),
        ),
        [smem, vmem, vmem, hbm, hbm],
        (smem, vmem, hbm, hbm),
        [pltpu.VMEM((8, LANES), jnp.int32), pltpu.SemaphoreType.DMA] + separator_scratch,
        cost_of(100_000_000, 1_100_000),
        aliases={3: 2, 4: 3},
    )(place, arrived, seps, own_forward, own_back)
    other_y = across_cores(to_other_y)
    other_back = across_cores(own_back)
    other_forward = across_cores(own_forward)

    u, y, backs, forwards = call(
        gather_kernel,
        (
            shape(2, 2, NB, 8, LANES),
            shape(2, 2, P_SIZE, LANES),
            shape(2, 2, 2 * P_SIZE, NB * RB, dtype=bf16),
            shape(2, 2, 2 * (NB * RB + P_SIZE), 2 * TR, dtype=bf16),
        ),
        [hbm] * 8,
        (vmem,) * 4,
        [
            pltpu.VMEM((2, 2, P_SIZE, NB * RB), f32),
            pltpu.VMEM((2, 2, NB * RB + P_SIZE, 2 * TR), f32),
            pltpu.SemaphoreType.DMA((8,)),
        ],
        cost_of(10_000_000, 12_000_000),
    )(own_u, other_u, own_y, other_y, own_back, other_back, own_forward, other_forward)

    def separator(stage, step, arrived):
        return call(
            functools.partial(separator_kernel, stage, step),
            slot_shape,
            [smem] * 2 + [vmem] * 2,
            vmem,
            separator_scratch,
            cost_of(100_000_000, 1_100_000),
        )(place, places, arrived, seps)

    fields = []
    base = None
    trace = None
    for stage in range(4):
        if stage > 0:
            send, base = call(
                functools.partial(enter_kernel, stage),
                (slot_shape, field_shape),
                [smem] * 3 + [vmem] * 4,
                (vmem, vmem),
                cost=cost_of(100_000_000, 2_000_000),
            )(place, own_slots, other_slots, u, y, forwards, trace)
            reply = separator(stage, 0, exchange(send))
        returned = exchange(reply)
        bases = [] if base is None else [base]

        def middle(*refs, stage=stage, count=len(bases)):
            head, rest = refs[:8], refs[8:]
            middle_kernel(stage, *head, rest[:count], *rest[count:])

        field, send, base = call(
            middle,
            (field_shape, slot_shape, field_shape),
            [smem] * 3 + [vmem] * 2 + [hbm] + [vmem] * (2 + len(bases)),
            (vmem,) * 3,
            [
                pltpu.VMEM((2 * (NB * RB + P_SIZE), 2 * TR), bf16),
                pltpu.SemaphoreType.DMA,
            ],
            cost_of(300_000_000, 3_000_000),
        )(place, own_slots, other_slots, u, y, forwards, backs, returned, *bases)
        fields.append(field)
        returned = exchange(separator(stage, 1, exchange(send)))
        field, trace = call(
            functools.partial(last_kernel, stage),
            (field_shape, shape(TR // RB, 8, LANES)),
            [smem] * 3 + [vmem] * 3,
            (vmem, vmem),
            cost=cost_of(200_000_000, 2_000_000),
        )(place, own_slots, other_slots, backs, returned, base)
        fields.append(field)
        if stage < 3:
            trace = to_next_stage(trace, stage)

    half_shape = shape(2, 2, HALF, P_SIZE)

    def collect(place_ref, *refs):
        collect_kernel(place_ref, refs[:8], *refs[8:])

    own, to_other = call(
        collect,
        (half_shape, half_shape),
        [smem] + [hbm] * 8,
        (vmem, vmem),
        [pltpu.VMEM((4, P_SIZE, LANES), f32), pltpu.SemaphoreType.DMA((4,))],
    )(place, *fields)
    down, up = call(
        output_kernel,
        (shape(2, S, P_SIZE), shape(2, S, P_SIZE)),
        [smem, vmem, vmem],
        (vmem, vmem),
    )(place, own, across_cores(to_other))
    return down[None, None], up[None, None]


def solution(mesh):
    whole = P("layer", "front", None, None, None)
    return jax.shard_map(
        body,
        mesh=mesh,
        in_specs=(whole,) * 7 + (P("layer", "front", None, None), P("layer", "front", None)),
        out_specs=(whole, whole),
        check_vma=False,
    )
```

```python
import functools

import jax
import jax.numpy as jnp
from jax import lax
from jax.experimental import pallas as pl
from jax.experimental.pallas import tpu as pltpu
from jax.sharding import PartitionSpec as P


P_SIZE = 256
Q = 256
TR = 128
RB = 32
S = 32
NB = 16
QB = 8
CAP = 2
HALF = 16
GROUP = 32
LANES = 128

f32 = jnp.float32
bf16 = jnp.bfloat16
VMEM_LIMIT = 48 * 1024 * 1024
ALMOST_ALL_VMEM = 60 * 1024 * 1024
FIRST_MIDDLE_VMEM = 58 * 1024 * 1024
smem = pl.BlockSpec(memory_space=pltpu.SMEM)
vmem = pl.BlockSpec(memory_space=pltpu.VMEM)
hbm = pl.BlockSpec(memory_space=pl.ANY)
NN = (((1,), (0,)), ((), ()))
NT = (((1,), (1,)), ((), ()))


def halves(value):
    high = value.astype(bf16)
    return high, (value - high.astype(f32)).astype(bf16)


def dot(first, second, dims=NN):
    return lax.dot_general(first, second, dims, preferred_element_type=f32)


def product(first, second, dims=NN):
    first_high, first_low = halves(first)
    second_high, second_low = halves(second)
    return (
        dot(first_high, second_high, dims)
        + dot(first_high, second_low, dims)
        + dot(first_low, second_high, dims)
    )


def narrow_product(first, second):
    first_high, first_low = halves(first)
    second_high, second_low = halves(second)
    both = dot(first_high, jnp.concatenate([second_high, second_low], axis=1))
    return both[:, :LANES] + both[:, LANES:] + dot(first_low, second_high)


def stacked(value):
    return jnp.concatenate(halves(value), axis=0)


def stacked_product(first, second):
    rows = first.shape[0] // 2
    both = dot(first, jnp.concatenate(halves(second), axis=1))
    return (both[:rows, :LANES] + both[:rows, LANES:]) + (both[rows:, :LANES] + both[rows:, LANES:])


def complex_pair(first, second, dims=NN):
    real = product(first[0], second[0], dims) - product(first[1], second[1], dims)
    imag = product(first[0], second[1], dims) + product(first[1], second[0], dims)
    return real, imag


def lane_ids(rows):
    return lax.broadcasted_iota(jnp.int32, (rows, LANES), 1)


def turned(value):
    lanes = lane_ids(value.shape[0])
    ahead = pltpu.roll(value, LANES - HALF, 1)
    behind = pltpu.roll(value, HALF, 1)
    return jnp.where(lanes % GROUP < HALF, -ahead, behind)


def pick(group, choices):
    return jnp.where(
        group == 0,
        choices[0],
        jnp.where(group == 1, choices[1], jnp.where(group == 2, choices[2], choices[3])),
    )


def rotations(value):
    return [value] + [pltpu.roll(value, GROUP * turn, 1) for turn in (1, 2, 3)]


def spread_group(rolled, group, source):
    return pick(group, [rolled[(place - source) % 4] for place in range(4)])


def unpack(packed):
    count = packed.shape[0]
    flat = packed.reshape(count * 8, LANES)
    group = lane_ids(count * 8) // GROUP
    rolled = rotations(flat)
    parts = [spread_group(rolled, group, k).reshape(count, 8, LANES) for k in range(4)]
    return jnp.stack(parts, axis=1).reshape(count * RB, LANES)


def unpack_both(packed):
    count = packed.shape[0]
    flat = packed.reshape(count * 8, LANES)
    return unpack(packed), unpack(turned(flat).reshape(count, 8, LANES))


def pack(spread):
    count = spread.shape[0] // RB
    parts = spread.reshape(count, 4, 8, LANES)
    group = lax.broadcasted_iota(jnp.int32, (count, 8, LANES), 2) // GROUP
    return pick(group, [parts[:, k] for k in range(4)])


def source_kernel(
    place_ref,
    down_hbm,
    up_hbm,
    leaf_hbm,
    coupling_hbm,
    own_u_ref,
    other_u_ref,
    own_y_ref,
    other_y_ref,
    down_ref,
    up_ref,
    leaf_ref,
    coupling_ref,
    semaphores,
):
    copies = [
        pltpu.make_async_copy(source, target, semaphores.at[index])
        for index, (source, target) in enumerate(
            (
                (down_hbm, down_ref),
                (up_hbm, up_ref),
                (leaf_hbm, leaf_ref),
                (coupling_hbm, coupling_ref),
            )
        )
    ]
    for copy in copies:
        copy.start()
    core = place_ref[0] % 2
    own_row = pl.multiple_of(core * HALF, HALF)
    other_row = pl.multiple_of((1 - core) * HALF, HALF)
    copies[0].wait()
    copies[1].wait()
    rows, turned_rows = [], []
    for source in (down_ref, up_ref):
        for start in (own_row, other_row):
            real = source[0, pl.ds(start, HALF), :]
            imag = source[1, pl.ds(start, HALF), :]
            rows += [real, imag]
            turned_rows += [-imag, real]
    copies[2].wait()
    y = product(leaf_ref[0], jnp.concatenate(rows, axis=0), NT) + product(
        leaf_ref[1], jnp.concatenate(turned_rows, axis=0), NT
    )
    rolled = rotations(y)
    y_group = lane_ids(P_SIZE) // GROUP
    for sweep in range(2):
        for side, y_ref in enumerate((own_y_ref, other_y_ref)):
            y_ref[sweep] = spread_group(rolled, y_group, 2 * sweep + side)
    copies[3].wait()
    u = narrow_product(coupling_ref[0], y) + narrow_product(coupling_ref[1], turned(y))
    parts = u.reshape(NB, 4, 8, LANES)
    u_group = lane_ids(NB * 8) // GROUP
    for sweep in range(2):
        for side, u_ref in enumerate((own_u_ref, other_u_ref)):
            choices = []
            for k in range(4):
                part = parts[:, k].reshape(NB * 8, LANES)
                turn = (k - 2 * sweep - side) % 4
                choices.append(pltpu.roll(part, GROUP * turn, 1) if turn else part)
            u_ref[sweep] = pick(u_group, choices).reshape(NB, 8, LANES)


def operator_kernel(
    after_ref,
    leaf_hbm,
    coupling_hbm,
    top_hbm,
    bottom_hbm,
    own_sep_hbm,
    other_sep_hbm,
    forward_ref,
    back_ref,
    seps_ref,
    leaf_ref,
    coupling_ref,
    top_ref,
    bottom_ref,
    sep_ref,
    semaphores,
):
    copies = [
        pltpu.make_async_copy(source, target, semaphores.at[index])
        for index, (source, target) in enumerate(
            (
                (leaf_hbm, leaf_ref),
                (top_hbm, top_ref),
                (bottom_hbm, bottom_ref),
                (coupling_hbm, coupling_ref),
                (own_sep_hbm, sep_ref.at[0]),
                (other_sep_hbm, sep_ref.at[1]),
            )
        )
    ]
    for copy in copies:
        copy.start()
    for copy in copies[:3]:
        copy.wait()
    leaf = (leaf_ref[0], leaf_ref[1])
    inject = tuple(
        jnp.concatenate([top_ref[part], bottom_ref[part]], axis=0) for part in range(2)
    )
    local = complex_pair(leaf, inject, NT)
    copies[3].wait()
    coupling = (coupling_ref[0], coupling_ref[1])
    update = complex_pair(coupling, local)
    for sweep in range(2):
        for part in range(2):
            columns = slice(sweep * TR, sweep * TR + TR)
            place = slice(part * TR, part * TR + TR)
            forward_ref[sweep, : NB * RB, place] = update[part][:, columns]
            forward_ref[sweep, NB * RB :, place] = local[part][:, columns]
    back = complex_pair(leaf, coupling, NT)
    back_ref[0] = back[0]
    back_ref[1] = back[1]
    for side in range(2):
        copies[4 + side].wait()
        for part in range(2):
            seps_ref[side, part] = stacked(sep_ref[side, part])


def gather_kernel(
    own_u_hbm,
    other_u_hbm,
    own_y_hbm,
    other_y_hbm,
    own_back_hbm,
    other_back_hbm,
    own_forward_hbm,
    other_forward_hbm,
    u_ref,
    y_ref,
    backs_ref,
    forwards_ref,
    back_ref,
    forward_ref,
    semaphores,
):
    copies = [
        pltpu.make_async_copy(source, target, semaphores.at[index])
        for index, (source, target) in enumerate(
            (
                (own_back_hbm, back_ref.at[0]),
                (own_forward_hbm, forward_ref.at[0]),
                (other_back_hbm, back_ref.at[1]),
                (other_forward_hbm, forward_ref.at[1]),
                (own_u_hbm, u_ref.at[0]),
                (other_u_hbm, u_ref.at[1]),
                (own_y_hbm, y_ref.at[0]),
                (other_y_hbm, y_ref.at[1]),
            )
        )
    ]
    for copy in copies:
        copy.start()
    for side in range(2):
        copies[2 * side].wait()
        for part in range(2):
            backs_ref[side, part] = stacked(back_ref[side, part])
        copies[2 * side + 1].wait()
        for sweep in range(2):
            forwards_ref[side, sweep] = stacked(forward_ref[side, sweep])
    for copy in copies[4:]:
        copy.wait()


def stage_place(place_ref, stage):
    row = place_ref[0] // 2
    core = place_ref[0] % 2
    sweep = jnp.where(row == stage, 0, 1)
    first = jnp.where(sweep == core, 0, 1)
    return sweep, first


def wait_for(source_ref, target_ref, semaphore):
    pltpu.make_async_copy(source_ref, target_ref, semaphore).wait()


def send_blocks(choice, own_slots_ref, other_slots_ref, packed, send_ref):
    for block in range(NB):
        slot = jnp.where(choice == 0, own_slots_ref[block], other_slots_ref[block])
        send_ref[slot] = packed[block]


def first_kernel(
    place_ref,
    own_targets_ref,
    other_targets_ref,
    own_offsets_ref,
    other_offsets_ref,
    own_u_ref,
    other_u_ref,
    own_slots_ref,
    other_slots_ref,
    send_ref,
):
    leaves = send_ref.shape[0]
    sweep, first = stage_place(place_ref, 0)
    lanes = lane_ids(leaves)
    rows = lax.broadcasted_iota(jnp.int32, (leaves, LANES), 0)
    notes = jnp.full((leaves, LANES), QB, jnp.int32)
    all_slots = []
    for side, (targets_ref, offsets_ref, slots_ref) in enumerate(
        (
            (own_targets_ref, own_offsets_ref, own_slots_ref),
            (other_targets_ref, other_offsets_ref, other_slots_ref),
        )
    ):
        targets = [targets_ref[block] for block in range(NB)]
        slots = []
        for block in range(NB):
            rank = jnp.int32(0)
            for earlier in range(block):
                rank = rank + jnp.where(targets[earlier] == targets[block], 1, 0)
            slot = targets[block] * CAP + rank
            slots_ref[block] = slot
            slots.append(slot)
            here = (rows == targets[block]) & (lanes == CAP * side + rank)
            notes = jnp.where(here, offsets_ref[block], notes)
        all_slots.append(slots)
    send_ref[:, CAP * 8 :, :] = jnp.broadcast_to(
        notes.astype(f32)[:, None, :], (leaves, 8, LANES)
    )
    packed = jnp.where(first == 0, own_u_ref[sweep], other_u_ref[sweep])
    for block in range(NB):
        slot = jnp.where(first == 0, all_slots[0][block], all_slots[1][block])
        row = pl.multiple_of((slot % CAP) * 8, 8)
        send_ref[slot // CAP, pl.ds(row, 8), :] = packed[block]


def separator_solve(choice, offsets_ref, arrived, seps_ref, reply_ref, even_ref, odd_ref, solved_ref):
    leaves = reply_ref.shape[0] // CAP
    even_ref[...] = jnp.zeros_like(even_ref)
    odd_ref[...] = jnp.zeros_like(odd_ref)
    places = []
    for leaf in range(leaves):
        for rank, total_ref in enumerate((even_ref, odd_ref)):
            place = offsets_ref[CAP * choice + rank, leaf]
            places.append(place)
            total_ref[place] = total_ref[place] + arrived(leaf, rank)
    rhs, rhs_turned = unpack_both(even_ref[:QB] + odd_ref[:QB])
    solved = stacked_product(seps_ref[choice, 0], rhs) + stacked_product(
        seps_ref[choice, 1], rhs_turned
    )
    solved_ref[:QB] = pack(solved)
    solved_ref[QB] = jnp.zeros((8, LANES), f32)
    for slot, place in enumerate(places):
        reply_ref[slot] = solved_ref[place]


def separator_kernel(
    stage, step, place_ref, offsets_ref, arrived_ref, seps_ref, reply_ref, *scratch
):
    sweep, first = stage_place(place_ref, stage)
    separator_solve(
        first if step == 0 else 1 - first,
        offsets_ref,
        lambda leaf, rank: arrived_ref[CAP * leaf + rank],
        seps_ref,
        reply_ref,
        *scratch,
    )


def first_separator_kernel(
    place_ref,
    arrived_ref,
    seps_ref,
    forward_in_hbm,
    back_in_hbm,
    offsets_ref,
    reply_ref,
    forward_out_hbm,
    back_out_hbm,
    notes_ref,
    semaphore,
    *scratch,
):
    sweep, first = stage_place(place_ref, 0)
    leaves = arrived_ref.shape[0]
    notes = arrived_ref[:, CAP * 8, :]
    whole = jnp.concatenate([notes, jnp.zeros((LANES - leaves, LANES), f32)], axis=0)
    notes_ref[...] = whole.T[:8].astype(jnp.int32)
    copy = pltpu.make_async_copy(notes_ref, offsets_ref, semaphore)
    copy.start()
    copy.wait()
    separator_solve(
        first,
        offsets_ref,
        lambda leaf, rank: arrived_ref[leaf, 8 * rank : 8 * rank + 8, :],
        seps_ref,
        reply_ref,
        *scratch,
    )


def leaf_finish(choice, own_slots_ref, other_slots_ref, returned_ref, back, base):
    blocks = []
    for block in range(NB):
        slot = jnp.where(choice == 0, own_slots_ref[block], other_slots_ref[block])
        blocks.append(returned_ref[slot])
    mine, mine_turned = unpack_both(jnp.stack(blocks, axis=0))
    real, imag = back()
    return (
        base
        + stacked_product(real, mine)
        + stacked_product(imag, mine_turned)
    )


def leaf_begin(
    sweep,
    choice,
    trace,
    trace_turned,
    own_slots_ref,
    other_slots_ref,
    u_ref,
    y_ref,
    forward,
    send_ref,
    base_ref,
):
    driven = stacked_product(forward, jnp.concatenate([trace, trace_turned], axis=0))
    packed = pack(driven[: NB * RB]) + u_ref[choice, sweep]
    send_blocks(choice, own_slots_ref, other_slots_ref, packed, send_ref)
    base_ref[...] = driven[NB * RB :] + y_ref[choice, sweep]


def trace_rows(sweep, field_ref):
    return field_ref[pl.ds(pl.multiple_of((1 - sweep) * TR, TR), TR), :]


def middle_kernel(
    stage,
    place_ref,
    own_slots_ref,
    other_slots_ref,
    u_ref,
    y_ref,
    forwards_hbm,
    backs_ref,
    returned_ref,
    base_refs,
    field_ref,
    send_ref,
    next_base_ref,
    forward_ref,
    semaphore,
    *back_scratch,
):
    sweep, first = stage_place(place_ref, stage)
    copy = pltpu.make_async_copy(forwards_hbm.at[1 - first, sweep], forward_ref, semaphore)
    if back_scratch:
        back_ref, back_semaphore = back_scratch
        back_copy = pltpu.make_async_copy(backs_ref.at[first], back_ref, back_semaphore)
        back_copy.start()
    copy.start()

    def back():
        if not back_scratch:
            return backs_ref[first, 0], backs_ref[first, 1]
        back_copy.wait()
        return back_ref[0], back_ref[1]

    base = base_refs[0][...] if base_refs else y_ref[first, sweep]
    field_ref[...] = leaf_finish(
        first, own_slots_ref, other_slots_ref, returned_ref, back, base
    )
    trace = trace_rows(sweep, field_ref)
    copy.wait()
    leaf_begin(
        sweep,
        1 - first,
        trace,
        turned(trace),
        own_slots_ref,
        other_slots_ref,
        u_ref,
        y_ref,
        forward_ref[...],
        send_ref,
        next_base_ref,
    )


def last_kernel(
    stage,
    place_ref,
    own_slots_ref,
    other_slots_ref,
    backs_ref,
    returned_ref,
    base_ref,
    field_ref,
    trace_ref,
):
    sweep, first = stage_place(place_ref, stage)
    field_ref[...] = leaf_finish(
        1 - first,
        own_slots_ref,
        other_slots_ref,
        returned_ref,
        lambda: (backs_ref[1 - first, 0], backs_ref[1 - first, 1]),
        base_ref[...],
    )
    trace_ref[...] = pack(trace_rows(sweep, field_ref))


def enter_kernel(
    stage,
    place_ref,
    own_slots_ref,
    other_slots_ref,
    u_ref,
    y_ref,
    forwards_ref,
    trace_ref,
    send_ref,
    next_base_ref,
):
    sweep, first = stage_place(place_ref, stage)
    trace, trace_turned = unpack_both(trace_ref[...])
    leaf_begin(
        sweep,
        first,
        trace,
        trace_turned,
        own_slots_ref,
        other_slots_ref,
        u_ref,
        y_ref,
        forwards_ref[first, sweep],
        send_ref,
        next_base_ref,
    )


def final_kernel(
    place_ref,
    own_slots_ref,
    other_slots_ref,
    backs_ref,
    returned_ref,
    base_ref,
    field_refs,
    own_ref,
    other_ref,
    parts_ref,
    semaphores,
):
    row = place_ref[0] // 2
    core = place_ref[0] % 2
    sweep_now, first = stage_place(place_ref, 3)
    spots, finals = [], []
    for sweep in range(2):
        for position in range(2):
            layer = position if sweep == 0 else 1 - position
            spot = 2 * sweep + jnp.where(core == layer, 0, 1)
            spots.append(spot)
            for stage in range(4):
                active = row == stage if sweep == 0 else row == 3 - stage
                if 2 * stage + position == len(field_refs):
                    finals.append(active)
                    continue

                @pl.when(active)
                def _():
                    pltpu.make_async_copy(
                        field_refs[2 * stage + position],
                        parts_ref.at[spot],
                        semaphores.at[2 * sweep + position],
                    ).start()

    field = leaf_finish(
        1 - first,
        own_slots_ref,
        other_slots_ref,
        returned_ref,
        lambda: (backs_ref[1 - first, 0], backs_ref[1 - first, 1]),
        base_ref[...],
    )
    for sweep in range(2):

        @pl.when(finals[sweep])
        def _():
            parts_ref[spots[2 * sweep + 1]] = field

        @pl.when(jnp.logical_not(finals[sweep]))
        def _():
            wait_for(field_refs[0], parts_ref.at[0], semaphores.at[2 * sweep + 1])

        wait_for(field_refs[0], parts_ref.at[0], semaphores.at[2 * sweep])
    group = lane_ids(P_SIZE) // GROUP
    joined = pick(group, [parts_ref[index] for index in range(4)])
    rows = joined.T.reshape(2, 2, 2, HALF, P_SIZE)
    own_ref[...] = rows[:, 0]
    other_ref[...] = rows[:, 1]


def output_kernel(place_ref, own_ref, other_ref, down_ref, up_ref):
    core = place_ref[0] % 2
    for sweep, field_ref in enumerate((down_ref, up_ref)):
        for part in range(2):
            field_ref[part, pl.ds(pl.multiple_of(core * HALF, HALF), HALF), :] = own_ref[sweep, part]
            field_ref[part, pl.ds(pl.multiple_of((1 - core) * HALF, HALF), HALF), :] = other_ref[
                sweep, part
            ]


def call(
    kernel, outs, in_specs, out_specs, scratch=(), cost=None, limit=VMEM_LIMIT, aliases=None
):
    return pl.pallas_call(
        kernel,
        out_shape=outs,
        in_specs=in_specs,
        out_specs=out_specs,
        scratch_shapes=list(scratch),
        compiler_params=pltpu.CompilerParams(vmem_limit_bytes=limit),
        cost_estimate=cost,
        input_output_aliases=aliases or {},
    )


def shape(*dims, dtype=f32):
    return jax.ShapeDtypeStruct(dims, dtype)


def cost_of(flops, size):
    return pl.CostEstimate(flops=flops, bytes_accessed=size, transcendentals=0)


def across_cores(value):
    layers = lax.axis_size("layer")
    return lax.ppermute(value, "layer", [(index, index ^ 1) for index in range(layers)])


def exchange(value):
    return lax.all_to_all(value, "front", split_axis=0, concat_axis=0, tiled=True)


def to_next_stage(value, stage):
    moves = [(stage, stage + 1), (3 - stage, 2 - stage)]
    pairs = [(2 * a + core, 2 * b + core) for a, b in moves for core in range(2)]
    return lax.ppermute(value, "layer", pairs)


def body(
    sources_down,
    sources_up,
    leaf_inverse,
    coupling,
    sep_inverse,
    inject_top,
    inject_bottom,
    targets,
    offsets,
):
    leaves = lax.axis_size("front")
    slots = leaves * CAP
    place = lax.axis_index("layer").reshape(1).astype(jnp.int32)
    leaf = leaf_inverse[0, 0]
    rows = coupling[0, 0]
    sep = sep_inverse[0, 0]
    own_targets = targets[0, 0, :, 0]
    other_targets = across_cores(own_targets)
    other_offsets = across_cores(offsets[0, 0])
    other_sep = across_cores(sep)

    source_scratch = pltpu.VMEM((2, S, P_SIZE), f32)
    leaf_scratch = pltpu.VMEM((2, P_SIZE, P_SIZE), f32)
    rows_scratch = pltpu.VMEM((2, NB * RB, P_SIZE), f32)
    inject_scratch = pltpu.VMEM((2, TR, P_SIZE), f32)
    u_shape = shape(2, NB, 8, LANES)
    y_shape = shape(2, P_SIZE, LANES)
    own_u, to_other_u, own_y, to_other_y = call(
        source_kernel,
        (u_shape, u_shape, y_shape, y_shape),
        [smem] + [hbm] * 4,
        (vmem,) * 4,
        [
            source_scratch,
            source_scratch,
            leaf_scratch,
            rows_scratch,
            pltpu.SemaphoreType.DMA((4,)),
        ],
        cost_of(600_000_000, 2_500_000),
        ALMOST_ALL_VMEM,
    )(place, sources_down[0, 0], sources_up[0, 0], leaf, rows)
    other_u = across_cores(to_other_u)

    slot_shape = shape(slots, 8, LANES)
    field_shape = shape(P_SIZE, LANES)
    slots_shape = shape(NB, dtype=jnp.int32)
    own_slots, other_slots, send = call(
        first_kernel,
        (slots_shape, slots_shape, shape(leaves, (CAP + 1) * 8, LANES)),
        [smem] * 5 + [vmem] * 2,
        (smem, smem, vmem),
    )(place, own_targets, other_targets, offsets[0, 0], other_offsets, own_u, other_u)
    arrived = exchange(send)

    own_forward, own_back, seps = call(
        operator_kernel,
        (
            shape(2, NB * RB + P_SIZE, 2 * TR),
            shape(2, P_SIZE, NB * RB),
            shape(2, 2, 2 * Q, Q, dtype=bf16),
        ),
        [hbm] * 7,
        (vmem,) * 3,
        [
            leaf_scratch,
            rows_scratch,
            inject_scratch,
            inject_scratch,
            pltpu.VMEM((2, 2, Q, Q), f32),
            pltpu.SemaphoreType.DMA((6,)),
        ],
        cost_of(4_000_000_000, 5_000_000),
    )(send, leaf, rows, inject_top[0, 0], inject_bottom[0, 0], sep, other_sep)
    separator_scratch = [pltpu.VMEM((QB + 1, 8, LANES), f32)] * 3
    places, reply, own_forward, own_back = call(
        first_separator_kernel,
        (
            shape(8, LANES, dtype=jnp.int32),
            slot_shape,
            shape(*own_forward.shape),
            shape(*own_back.shape),
        ),
        [smem, vmem, vmem, hbm, hbm],
        (smem, vmem, hbm, hbm),
        [pltpu.VMEM((8, LANES), jnp.int32), pltpu.SemaphoreType.DMA] + separator_scratch,
        cost_of(100_000_000, 1_100_000),
        aliases={3: 2, 4: 3},
    )(place, arrived, seps, own_forward, own_back)
    other_y = across_cores(to_other_y)
    other_back = across_cores(own_back)
    other_forward = across_cores(own_forward)

    u, y, backs, forwards = call(
        gather_kernel,
        (
            shape(2, 2, NB, 8, LANES),
            shape(2, 2, P_SIZE, LANES),
            shape(2, 2, 2 * P_SIZE, NB * RB, dtype=bf16),
            shape(2, 2, 2 * (NB * RB + P_SIZE), 2 * TR, dtype=bf16),
        ),
        [hbm] * 8,
        (vmem,) * 4,
        [
            pltpu.VMEM((2, 2, P_SIZE, NB * RB), f32),
            pltpu.VMEM((2, 2, NB * RB + P_SIZE, 2 * TR), f32),
            pltpu.SemaphoreType.DMA((8,)),
        ],
        cost_of(10_000_000, 12_000_000),
    )(own_u, other_u, own_y, other_y, own_back, other_back, own_forward, other_forward)

    def separator(stage, step, arrived):
        return call(
            functools.partial(separator_kernel, stage, step),
            slot_shape,
            [smem] * 2 + [vmem] * 2,
            vmem,
            separator_scratch,
            cost_of(100_000_000, 1_100_000),
        )(place, places, arrived, seps)

    fields = []
    base = None
    trace = None
    for stage in range(4):
        if stage > 0:
            send, base = call(
                functools.partial(enter_kernel, stage),
                (slot_shape, field_shape),
                [smem] * 3 + [vmem] * 4,
                (vmem, vmem),
                cost=cost_of(100_000_000, 2_000_000),
            )(place, own_slots, other_slots, u, y, forwards, trace)
            reply = separator(stage, 0, exchange(send))
        returned = exchange(reply)
        bases = [] if base is None else [base]

        def middle(*refs, stage=stage, count=len(bases)):
            head, rest = refs[:8], refs[8:]
            middle_kernel(stage, *head, rest[:count], *rest[count:])

        field, send, base = call(
            middle,
            (field_shape, slot_shape, field_shape),
            [smem] * 3
            + [vmem] * 2
            + [hbm]
            + ([vmem] if bases else [hbm])
            + [vmem] * (1 + len(bases)),
            (vmem,) * 3,
            [
                pltpu.VMEM((2 * (NB * RB + P_SIZE), 2 * TR), bf16),
                pltpu.SemaphoreType.DMA,
            ]
            + (
                []
                if bases
                else [pltpu.VMEM((2, 2 * P_SIZE, NB * RB), bf16), pltpu.SemaphoreType.DMA]
            ),
            cost_of(300_000_000, 3_000_000),
            VMEM_LIMIT if bases else FIRST_MIDDLE_VMEM,
        )(place, own_slots, other_slots, u, y, forwards, backs, returned, *bases)
        fields.append(field)
        returned = exchange(separator(stage, 1, exchange(send)))
        if stage == 3:
            break
        field, trace = call(
            functools.partial(last_kernel, stage),
            (field_shape, shape(TR // RB, 8, LANES)),
            [smem] * 3 + [vmem] * 3,
            (vmem, vmem),
            cost=cost_of(200_000_000, 2_000_000),
        )(place, own_slots, other_slots, backs, returned, base)
        fields.append(field)
        trace = to_next_stage(trace, stage)

    half_shape = shape(2, 2, HALF, P_SIZE)

    def final(*refs):
        final_kernel(*refs[:6], refs[6 : 6 + len(fields)], *refs[6 + len(fields) :])

    own, to_other = call(
        final,
        (half_shape, half_shape),
        [smem] * 3 + [vmem] * 3 + [hbm] * len(fields),
        (vmem, vmem),
        [pltpu.VMEM((4, P_SIZE, LANES), f32), pltpu.SemaphoreType.DMA((4,))],
    )(place, own_slots, other_slots, backs, returned, base, *fields)
    down, up = call(
        output_kernel,
        (shape(2, S, P_SIZE), shape(2, S, P_SIZE)),
        [smem, vmem, vmem],
        (vmem, vmem),
    )(place, own, across_cores(to_other))
    return down[None, None], up[None, None]


def solution(mesh):
    whole = P("layer", "front", None, None, None)
    return jax.shard_map(
        body,
        mesh=mesh,
        in_specs=(whole,) * 7 + (P("layer", "front", None, None), P("layer", "front", None)),
        out_specs=(whole, whole),
        check_vma=False,
    )
```

```python
import functools

import jax
import jax.numpy as jnp
from jax import lax
from jax.experimental import pallas as pl
from jax.experimental.pallas import tpu as pltpu
from jax.sharding import PartitionSpec as P


P_SIZE = 256
Q = 256
TR = 128
RB = 32
S = 32
NB = 16
QB = 8
CAP = 2
HALF = 16
GROUP = 32
LANES = 128

f32 = jnp.float32
bf16 = jnp.bfloat16
VMEM_LIMIT = 48 * 1024 * 1024
ALMOST_ALL_VMEM = 60 * 1024 * 1024
smem = pl.BlockSpec(memory_space=pltpu.SMEM)
vmem = pl.BlockSpec(memory_space=pltpu.VMEM)
hbm = pl.BlockSpec(memory_space=pl.ANY)
NN = (((1,), (0,)), ((), ()))
NT = (((1,), (1,)), ((), ()))


def halves(value):
    high = value.astype(bf16)
    return high, (value - high.astype(f32)).astype(bf16)


def dot(first, second, dims=NN):
    return lax.dot_general(first, second, dims, preferred_element_type=f32)


def product(first, second, dims=NN):
    first_high, first_low = halves(first)
    second_high, second_low = halves(second)
    return (
        dot(first_high, second_high, dims)
        + dot(first_high, second_low, dims)
        + dot(first_low, second_high, dims)
    )


def narrow_product(first, second):
    first_high, first_low = halves(first)
    second_high, second_low = halves(second)
    both = dot(first_high, jnp.concatenate([second_high, second_low], axis=1))
    return both[:, :LANES] + both[:, LANES:] + dot(first_low, second_high)


def stacked(value):
    return jnp.concatenate(halves(value), axis=0)


def stacked_product(first, second):
    rows = first.shape[0] // 2
    both = dot(first, jnp.concatenate(halves(second), axis=1))
    return (both[:rows, :LANES] + both[:rows, LANES:]) + (both[rows:, :LANES] + both[rows:, LANES:])


def complex_pair(first, second, dims=NN):
    real = product(first[0], second[0], dims) - product(first[1], second[1], dims)
    imag = product(first[0], second[1], dims) + product(first[1], second[0], dims)
    return real, imag


def lane_ids(rows):
    return lax.broadcasted_iota(jnp.int32, (rows, LANES), 1)


def turned(value):
    lanes = lane_ids(value.shape[0])
    ahead = pltpu.roll(value, LANES - HALF, 1)
    behind = pltpu.roll(value, HALF, 1)
    return jnp.where(lanes % GROUP < HALF, -ahead, behind)


def pick(group, choices):
    return jnp.where(
        group == 0,
        choices[0],
        jnp.where(group == 1, choices[1], jnp.where(group == 2, choices[2], choices[3])),
    )


def rotations(value):
    return [value] + [pltpu.roll(value, GROUP * turn, 1) for turn in (1, 2, 3)]


def spread_group(rolled, group, source):
    return pick(group, [rolled[(place - source) % 4] for place in range(4)])


def unpack(packed):
    count = packed.shape[0]
    flat = packed.reshape(count * 8, LANES)
    group = lane_ids(count * 8) // GROUP
    rolled = rotations(flat)
    parts = [spread_group(rolled, group, k).reshape(count, 8, LANES) for k in range(4)]
    return jnp.stack(parts, axis=1).reshape(count * RB, LANES)


def unpack_both(packed):
    count = packed.shape[0]
    flat = packed.reshape(count * 8, LANES)
    return unpack(packed), unpack(turned(flat).reshape(count, 8, LANES))


def pack(spread):
    count = spread.shape[0] // RB
    parts = spread.reshape(count, 4, 8, LANES)
    group = lax.broadcasted_iota(jnp.int32, (count, 8, LANES), 2) // GROUP
    return pick(group, [parts[:, k] for k in range(4)])


def source_kernel(
    place_ref,
    down_hbm,
    up_hbm,
    leaf_hbm,
    coupling_hbm,
    own_u_ref,
    other_u_ref,
    own_y_ref,
    other_y_ref,
    down_ref,
    up_ref,
    leaf_ref,
    coupling_ref,
    semaphores,
):
    copies = [
        pltpu.make_async_copy(source, target, semaphores.at[index])
        for index, (source, target) in enumerate(
            (
                (down_hbm, down_ref),
                (up_hbm, up_ref),
                (leaf_hbm, leaf_ref),
                (coupling_hbm, coupling_ref),
            )
        )
    ]
    for copy in copies:
        copy.start()
    core = place_ref[0] % 2
    own_row = pl.multiple_of(core * HALF, HALF)
    other_row = pl.multiple_of((1 - core) * HALF, HALF)
    copies[0].wait()
    copies[1].wait()
    rows, turned_rows = [], []
    for source in (down_ref, up_ref):
        for start in (own_row, other_row):
            real = source[0, pl.ds(start, HALF), :]
            imag = source[1, pl.ds(start, HALF), :]
            rows += [real, imag]
            turned_rows += [-imag, real]
    copies[2].wait()
    y = product(leaf_ref[0], jnp.concatenate(rows, axis=0), NT) + product(
        leaf_ref[1], jnp.concatenate(turned_rows, axis=0), NT
    )
    rolled = rotations(y)
    y_group = lane_ids(P_SIZE) // GROUP
    for sweep in range(2):
        for side, y_ref in enumerate((own_y_ref, other_y_ref)):
            y_ref[sweep] = spread_group(rolled, y_group, 2 * sweep + side)
    copies[3].wait()
    u = narrow_product(coupling_ref[0], y) + narrow_product(coupling_ref[1], turned(y))
    parts = u.reshape(NB, 4, 8, LANES)
    u_group = lane_ids(NB * 8) // GROUP
    for sweep in range(2):
        for side, u_ref in enumerate((own_u_ref, other_u_ref)):
            choices = []
            for k in range(4):
                part = parts[:, k].reshape(NB * 8, LANES)
                turn = (k - 2 * sweep - side) % 4
                choices.append(pltpu.roll(part, GROUP * turn, 1) if turn else part)
            u_ref[sweep] = pick(u_group, choices).reshape(NB, 8, LANES)


def operator_kernel(
    after_ref,
    leaf_hbm,
    coupling_hbm,
    top_hbm,
    bottom_hbm,
    own_sep_hbm,
    other_sep_hbm,
    forward_ref,
    back_ref,
    seps_ref,
    leaf_ref,
    coupling_ref,
    top_ref,
    bottom_ref,
    sep_ref,
    semaphores,
):
    copies = [
        pltpu.make_async_copy(source, target, semaphores.at[index])
        for index, (source, target) in enumerate(
            (
                (leaf_hbm, leaf_ref),
                (top_hbm, top_ref),
                (bottom_hbm, bottom_ref),
                (coupling_hbm, coupling_ref),
                (own_sep_hbm, sep_ref.at[0]),
                (other_sep_hbm, sep_ref.at[1]),
            )
        )
    ]
    for copy in copies:
        copy.start()
    for copy in copies[:3]:
        copy.wait()
    leaf = (leaf_ref[0], leaf_ref[1])
    inject = tuple(
        jnp.concatenate([top_ref[part], bottom_ref[part]], axis=0) for part in range(2)
    )
    local = complex_pair(leaf, inject, NT)
    copies[3].wait()
    coupling = (coupling_ref[0], coupling_ref[1])
    update = complex_pair(coupling, local)
    for sweep in range(2):
        for part in range(2):
            columns = slice(sweep * TR, sweep * TR + TR)
            place = slice(part * TR, part * TR + TR)
            forward_ref[sweep, : NB * RB, place] = update[part][:, columns]
            forward_ref[sweep, NB * RB :, place] = local[part][:, columns]
    back = complex_pair(leaf, coupling, NT)
    back_ref[0] = back[0]
    back_ref[1] = back[1]
    for side in range(2):
        copies[4 + side].wait()
        for part in range(2):
            seps_ref[side, part] = stacked(sep_ref[side, part])


def gather_kernel(
    own_u_hbm,
    other_u_hbm,
    own_y_hbm,
    other_y_hbm,
    own_back_hbm,
    other_back_hbm,
    own_forward_hbm,
    other_forward_hbm,
    u_ref,
    y_ref,
    backs_ref,
    forwards_ref,
    back_ref,
    forward_ref,
    semaphores,
):
    copies = [
        pltpu.make_async_copy(source, target, semaphores.at[index])
        for index, (source, target) in enumerate(
            (
                (own_back_hbm, back_ref.at[0]),
                (own_forward_hbm, forward_ref.at[0]),
                (other_back_hbm, back_ref.at[1]),
                (other_forward_hbm, forward_ref.at[1]),
                (own_u_hbm, u_ref.at[0]),
                (other_u_hbm, u_ref.at[1]),
                (own_y_hbm, y_ref.at[0]),
                (other_y_hbm, y_ref.at[1]),
            )
        )
    ]
    for copy in copies:
        copy.start()
    for side in range(2):
        copies[2 * side].wait()
        for part in range(2):
            backs_ref[side, part] = stacked(back_ref[side, part])
        copies[2 * side + 1].wait()
        for sweep in range(2):
            forwards_ref[side, sweep] = stacked(forward_ref[side, sweep])
    for copy in copies[4:]:
        copy.wait()


def stage_place(place_ref, stage):
    row = place_ref[0] // 2
    core = place_ref[0] % 2
    sweep = jnp.where(row == stage, 0, 1)
    first = jnp.where(sweep == core, 0, 1)
    return sweep, first


def wait_for(source_ref, target_ref, semaphore):
    pltpu.make_async_copy(source_ref, target_ref, semaphore).wait()


def send_blocks(choice, own_slots_ref, other_slots_ref, packed, send_ref):
    for block in range(NB):
        slot = jnp.where(choice == 0, own_slots_ref[block], other_slots_ref[block])
        send_ref[slot] = packed[block]


def first_kernel(
    place_ref,
    own_targets_ref,
    other_targets_ref,
    own_offsets_ref,
    other_offsets_ref,
    own_u_ref,
    other_u_ref,
    own_slots_ref,
    other_slots_ref,
    send_ref,
):
    leaves = send_ref.shape[0]
    sweep, first = stage_place(place_ref, 0)
    lanes = lane_ids(leaves)
    rows = lax.broadcasted_iota(jnp.int32, (leaves, LANES), 0)
    notes = jnp.full((leaves, LANES), QB, jnp.int32)
    all_slots = []
    for side, (targets_ref, offsets_ref, slots_ref) in enumerate(
        (
            (own_targets_ref, own_offsets_ref, own_slots_ref),
            (other_targets_ref, other_offsets_ref, other_slots_ref),
        )
    ):
        targets = [targets_ref[block] for block in range(NB)]
        slots = []
        for block in range(NB):
            rank = jnp.int32(0)
            for earlier in range(block):
                rank = rank + jnp.where(targets[earlier] == targets[block], 1, 0)
            slot = targets[block] * CAP + rank
            slots_ref[block] = slot
            slots.append(slot)
            here = (rows == targets[block]) & (lanes == CAP * side + rank)
            notes = jnp.where(here, offsets_ref[block], notes)
        all_slots.append(slots)
    send_ref[:, CAP * 8 :, :] = jnp.broadcast_to(
        notes.astype(f32)[:, None, :], (leaves, 8, LANES)
    )
    packed = jnp.where(first == 0, own_u_ref[sweep], other_u_ref[sweep])
    for block in range(NB):
        slot = jnp.where(first == 0, all_slots[0][block], all_slots[1][block])
        row = pl.multiple_of((slot % CAP) * 8, 8)
        send_ref[slot // CAP, pl.ds(row, 8), :] = packed[block]


def separator_solve(choice, offsets_ref, arrived, seps_ref, reply_ref, even_ref, odd_ref, solved_ref):
    leaves = reply_ref.shape[0] // CAP
    even_ref[...] = jnp.zeros_like(even_ref)
    odd_ref[...] = jnp.zeros_like(odd_ref)
    places = []
    for leaf in range(leaves):
        for rank, total_ref in enumerate((even_ref, odd_ref)):
            place = offsets_ref[CAP * choice + rank, leaf]
            places.append(place)
            total_ref[place] = total_ref[place] + arrived(leaf, rank)
    rhs, rhs_turned = unpack_both(even_ref[:QB] + odd_ref[:QB])
    solved = stacked_product(seps_ref[choice, 0], rhs) + stacked_product(
        seps_ref[choice, 1], rhs_turned
    )
    solved_ref[:QB] = pack(solved)
    solved_ref[QB] = jnp.zeros((8, LANES), f32)
    for slot, place in enumerate(places):
        reply_ref[slot] = solved_ref[place]


def separator_kernel(
    stage, step, place_ref, offsets_ref, arrived_ref, seps_ref, reply_ref, *scratch
):
    sweep, first = stage_place(place_ref, stage)
    separator_solve(
        first if step == 0 else 1 - first,
        offsets_ref,
        lambda leaf, rank: arrived_ref[CAP * leaf + rank],
        seps_ref,
        reply_ref,
        *scratch,
    )


def first_separator_kernel(
    place_ref,
    arrived_ref,
    seps_ref,
    forward_in_hbm,
    back_in_hbm,
    offsets_ref,
    reply_ref,
    forward_out_hbm,
    back_out_hbm,
    notes_ref,
    semaphore,
    *scratch,
):
    sweep, first = stage_place(place_ref, 0)
    leaves = arrived_ref.shape[0]
    notes = arrived_ref[:, CAP * 8, :]
    whole = jnp.concatenate([notes, jnp.zeros((LANES - leaves, LANES), f32)], axis=0)
    notes_ref[...] = whole.T[:8].astype(jnp.int32)
    copy = pltpu.make_async_copy(notes_ref, offsets_ref, semaphore)
    copy.start()
    copy.wait()
    separator_solve(
        first,
        offsets_ref,
        lambda leaf, rank: arrived_ref[leaf, 8 * rank : 8 * rank + 8, :],
        seps_ref,
        reply_ref,
        *scratch,
    )


def leaf_finish(choice, own_slots_ref, other_slots_ref, returned_ref, backs_ref, base):
    blocks = []
    for block in range(NB):
        slot = jnp.where(choice == 0, own_slots_ref[block], other_slots_ref[block])
        blocks.append(returned_ref[slot])
    mine, mine_turned = unpack_both(jnp.stack(blocks, axis=0))
    return (
        base
        + stacked_product(backs_ref[choice, 0], mine)
        + stacked_product(backs_ref[choice, 1], mine_turned)
    )


def leaf_begin(
    sweep,
    choice,
    trace,
    trace_turned,
    own_slots_ref,
    other_slots_ref,
    u_ref,
    y_ref,
    forward,
    send_ref,
    base_ref,
):
    driven = stacked_product(forward, jnp.concatenate([trace, trace_turned], axis=0))
    packed = pack(driven[: NB * RB]) + u_ref[choice, sweep]
    send_blocks(choice, own_slots_ref, other_slots_ref, packed, send_ref)
    base_ref[...] = driven[NB * RB :] + y_ref[choice, sweep]


def trace_rows(sweep, field_ref):
    return field_ref[pl.ds(pl.multiple_of((1 - sweep) * TR, TR), TR), :]


def middle_kernel(
    stage,
    place_ref,
    own_slots_ref,
    other_slots_ref,
    u_ref,
    y_ref,
    forwards_hbm,
    backs_ref,
    returned_ref,
    base_refs,
    field_ref,
    send_ref,
    next_base_ref,
    forward_ref,
    semaphore,
):
    sweep, first = stage_place(place_ref, stage)
    copy = pltpu.make_async_copy(forwards_hbm.at[1 - first, sweep], forward_ref, semaphore)
    copy.start()
    base = base_refs[0][...] if base_refs else y_ref[first, sweep]
    field_ref[...] = leaf_finish(
        first, own_slots_ref, other_slots_ref, returned_ref, backs_ref, base
    )
    trace = trace_rows(sweep, field_ref)
    copy.wait()
    leaf_begin(
        sweep,
        1 - first,
        trace,
        turned(trace),
        own_slots_ref,
        other_slots_ref,
        u_ref,
        y_ref,
        forward_ref[...],
        send_ref,
        next_base_ref,
    )


def last_kernel(
    stage,
    place_ref,
    own_slots_ref,
    other_slots_ref,
    backs_ref,
    returned_ref,
    base_ref,
    field_ref,
    trace_ref,
):
    sweep, first = stage_place(place_ref, stage)
    field_ref[...] = leaf_finish(
        1 - first, own_slots_ref, other_slots_ref, returned_ref, backs_ref, base_ref[...]
    )
    trace_ref[...] = pack(trace_rows(sweep, field_ref))


def enter_kernel(
    stage,
    place_ref,
    own_slots_ref,
    other_slots_ref,
    u_ref,
    y_ref,
    forwards_ref,
    trace_ref,
    send_ref,
    next_base_ref,
):
    sweep, first = stage_place(place_ref, stage)
    trace, trace_turned = unpack_both(trace_ref[...])
    leaf_begin(
        sweep,
        first,
        trace,
        trace_turned,
        own_slots_ref,
        other_slots_ref,
        u_ref,
        y_ref,
        forwards_ref[first, sweep],
        send_ref,
        next_base_ref,
    )


def final_kernel(
    place_ref,
    own_slots_ref,
    other_slots_ref,
    backs_ref,
    returned_ref,
    base_ref,
    field_refs,
    own_ref,
    other_ref,
    parts_ref,
    semaphores,
):
    row = place_ref[0] // 2
    core = place_ref[0] % 2
    sweep_now, first = stage_place(place_ref, 3)
    spots, finals = [], []
    for sweep in range(2):
        for position in range(2):
            layer = position if sweep == 0 else 1 - position
            spot = 2 * sweep + jnp.where(core == layer, 0, 1)
            spots.append(spot)
            for stage in range(4):
                active = row == stage if sweep == 0 else row == 3 - stage
                if 2 * stage + position == len(field_refs):
                    finals.append(active)
                    continue

                @pl.when(active)
                def _():
                    pltpu.make_async_copy(
                        field_refs[2 * stage + position],
                        parts_ref.at[spot],
                        semaphores.at[2 * sweep + position],
                    ).start()

    field = leaf_finish(
        1 - first, own_slots_ref, other_slots_ref, returned_ref, backs_ref, base_ref[...]
    )
    for sweep in range(2):

        @pl.when(finals[sweep])
        def _():
            parts_ref[spots[2 * sweep + 1]] = field

        @pl.when(jnp.logical_not(finals[sweep]))
        def _():
            wait_for(field_refs[0], parts_ref.at[0], semaphores.at[2 * sweep + 1])

        wait_for(field_refs[0], parts_ref.at[0], semaphores.at[2 * sweep])
    group = lane_ids(P_SIZE) // GROUP
    joined = pick(group, [parts_ref[index] for index in range(4)])
    rows = joined.T.reshape(2, 2, 2, HALF, P_SIZE)
    own_ref[...] = rows[:, 0]
    other_ref[...] = rows[:, 1]


def output_kernel(place_ref, own_ref, other_ref, down_ref, up_ref):
    core = place_ref[0] % 2
    for sweep, field_ref in enumerate((down_ref, up_ref)):
        for part in range(2):
            field_ref[part, pl.ds(pl.multiple_of(core * HALF, HALF), HALF), :] = own_ref[sweep, part]
            field_ref[part, pl.ds(pl.multiple_of((1 - core) * HALF, HALF), HALF), :] = other_ref[
                sweep, part
            ]


def call(
    kernel, outs, in_specs, out_specs, scratch=(), cost=None, limit=VMEM_LIMIT, aliases=None
):
    return pl.pallas_call(
        kernel,
        out_shape=outs,
        in_specs=in_specs,
        out_specs=out_specs,
        scratch_shapes=list(scratch),
        compiler_params=pltpu.CompilerParams(vmem_limit_bytes=limit),
        cost_estimate=cost,
        input_output_aliases=aliases or {},
    )


def shape(*dims, dtype=f32):
    return jax.ShapeDtypeStruct(dims, dtype)


def cost_of(flops, size):
    return pl.CostEstimate(flops=flops, bytes_accessed=size, transcendentals=0)


def across_cores(value):
    layers = lax.axis_size("layer")
    return lax.ppermute(value, "layer", [(index, index ^ 1) for index in range(layers)])


def exchange(value):
    return lax.all_to_all(value, "front", split_axis=0, concat_axis=0, tiled=True)


def to_next_stage(value, stage):
    moves = [(stage, stage + 1), (3 - stage, 2 - stage)]
    pairs = [(2 * a + core, 2 * b + core) for a, b in moves for core in range(2)]
    return lax.ppermute(value, "layer", pairs)


def body(
    sources_down,
    sources_up,
    leaf_inverse,
    coupling,
    sep_inverse,
    inject_top,
    inject_bottom,
    targets,
    offsets,
):
    leaves = lax.axis_size("front")
    slots = leaves * CAP
    place = lax.axis_index("layer").reshape(1).astype(jnp.int32)
    leaf = leaf_inverse[0, 0]
    rows = coupling[0, 0]
    sep = sep_inverse[0, 0]
    own_targets = targets[0, 0, :, 0]
    other_targets = across_cores(own_targets)
    other_offsets = across_cores(offsets[0, 0])
    other_sep = across_cores(sep)

    source_scratch = pltpu.VMEM((2, S, P_SIZE), f32)
    leaf_scratch = pltpu.VMEM((2, P_SIZE, P_SIZE), f32)
    rows_scratch = pltpu.VMEM((2, NB * RB, P_SIZE), f32)
    inject_scratch = pltpu.VMEM((2, TR, P_SIZE), f32)
    u_shape = shape(2, NB, 8, LANES)
    y_shape = shape(2, P_SIZE, LANES)
    own_u, to_other_u, own_y, to_other_y = call(
        source_kernel,
        (u_shape, u_shape, y_shape, y_shape),
        [smem] + [hbm] * 4,
        (vmem,) * 4,
        [
            source_scratch,
            source_scratch,
            leaf_scratch,
            rows_scratch,
            pltpu.SemaphoreType.DMA((4,)),
        ],
        cost_of(600_000_000, 2_500_000),
        ALMOST_ALL_VMEM,
    )(place, sources_down[0, 0], sources_up[0, 0], leaf, rows)
    other_u = across_cores(to_other_u)

    slot_shape = shape(slots, 8, LANES)
    field_shape = shape(P_SIZE, LANES)
    slots_shape = shape(NB, dtype=jnp.int32)
    own_slots, other_slots, send = call(
        first_kernel,
        (slots_shape, slots_shape, shape(leaves, (CAP + 1) * 8, LANES)),
        [smem] * 5 + [vmem] * 2,
        (smem, smem, vmem),
    )(place, own_targets, other_targets, offsets[0, 0], other_offsets, own_u, other_u)
    arrived = exchange(send)

    own_forward, own_back, seps = call(
        operator_kernel,
        (
            shape(2, NB * RB + P_SIZE, 2 * TR),
            shape(2, P_SIZE, NB * RB),
            shape(2, 2, 2 * Q, Q, dtype=bf16),
        ),
        [hbm] * 7,
        (vmem,) * 3,
        [
            leaf_scratch,
            rows_scratch,
            inject_scratch,
            inject_scratch,
            pltpu.VMEM((2, 2, Q, Q), f32),
            pltpu.SemaphoreType.DMA((6,)),
        ],
        cost_of(4_000_000_000, 5_000_000),
    )(send, leaf, rows, inject_top[0, 0], inject_bottom[0, 0], sep, other_sep)
    separator_scratch = [pltpu.VMEM((QB + 1, 8, LANES), f32)] * 3
    places, reply, own_forward, own_back = call(
        first_separator_kernel,
        (
            shape(8, LANES, dtype=jnp.int32),
            slot_shape,
            shape(*own_forward.shape),
            shape(*own_back.shape),
        ),
        [smem, vmem, vmem, hbm, hbm],
        (smem, vmem, hbm, hbm),
        [pltpu.VMEM((8, LANES), jnp.int32), pltpu.SemaphoreType.DMA] + separator_scratch,
        cost_of(100_000_000, 1_100_000),
        aliases={3: 2, 4: 3},
    )(place, arrived, seps, own_forward, own_back)
    other_y = across_cores(to_other_y)
    other_back = across_cores(own_back)
    other_forward = across_cores(own_forward)

    u, y, backs, forwards = call(
        gather_kernel,
        (
            shape(2, 2, NB, 8, LANES),
            shape(2, 2, P_SIZE, LANES),
            shape(2, 2, 2 * P_SIZE, NB * RB, dtype=bf16),
            shape(2, 2, 2 * (NB * RB + P_SIZE), 2 * TR, dtype=bf16),
        ),
        [hbm] * 8,
        (vmem,) * 4,
        [
            pltpu.VMEM((2, 2, P_SIZE, NB * RB), f32),
            pltpu.VMEM((2, 2, NB * RB + P_SIZE, 2 * TR), f32),
            pltpu.SemaphoreType.DMA((8,)),
        ],
        cost_of(10_000_000, 12_000_000),
    )(own_u, other_u, own_y, other_y, own_back, other_back, own_forward, other_forward)

    def separator(stage, step, arrived):
        return call(
            functools.partial(separator_kernel, stage, step),
            slot_shape,
            [smem] * 2 + [vmem] * 2,
            vmem,
            separator_scratch,
            cost_of(100_000_000, 1_100_000),
        )(place, places, arrived, seps)

    fields = []
    base = None
    trace = None
    for stage in range(4):
        if stage > 0:
            send, base = call(
                functools.partial(enter_kernel, stage),
                (slot_shape, field_shape),
                [smem] * 3 + [vmem] * 4,
                (vmem, vmem),
                cost=cost_of(100_000_000, 2_000_000),
            )(place, own_slots, other_slots, u, y, forwards, trace)
            reply = separator(stage, 0, exchange(send))
        returned = exchange(reply)
        bases = [] if base is None else [base]

        def middle(*refs, stage=stage, count=len(bases)):
            head, rest = refs[:8], refs[8:]
            middle_kernel(stage, *head, rest[:count], *rest[count:])

        field, send, base = call(
            middle,
            (field_shape, slot_shape, field_shape),
            [smem] * 3 + [vmem] * 2 + [hbm] + [vmem] * (2 + len(bases)),
            (vmem,) * 3,
            [
                pltpu.VMEM((2 * (NB * RB + P_SIZE), 2 * TR), bf16),
                pltpu.SemaphoreType.DMA,
            ],
            cost_of(300_000_000, 3_000_000),
        )(place, own_slots, other_slots, u, y, forwards, backs, returned, *bases)
        fields.append(field)
        returned = exchange(separator(stage, 1, exchange(send)))
        if stage == 3:
            break
        field, trace = call(
            functools.partial(last_kernel, stage),
            (field_shape, shape(TR // RB, 8, LANES)),
            [smem] * 3 + [vmem] * 3,
            (vmem, vmem),
            cost=cost_of(200_000_000, 2_000_000),
        )(place, own_slots, other_slots, backs, returned, base)
        fields.append(field)
        trace = to_next_stage(trace, stage)

    half_shape = shape(2, 2, HALF, P_SIZE)

    def final(*refs):
        final_kernel(*refs[:6], refs[6 : 6 + len(fields)], *refs[6 + len(fields) :])

    own, to_other = call(
        final,
        (half_shape, half_shape),
        [smem] * 3 + [vmem] * 3 + [hbm] * len(fields),
        (vmem, vmem),
        [pltpu.VMEM((4, P_SIZE, LANES), f32), pltpu.SemaphoreType.DMA((4,))],
    )(place, own_slots, other_slots, backs, returned, base, *fields)
    down, up = call(
        output_kernel,
        (shape(2, S, P_SIZE), shape(2, S, P_SIZE)),
        [smem, vmem, vmem],
        (vmem, vmem),
    )(place, own, across_cores(to_other))
    return down[None, None], up[None, None]


def solution(mesh):
    whole = P("layer", "front", None, None, None)
    return jax.shard_map(
        body,
        mesh=mesh,
        in_specs=(whole,) * 7 + (P("layer", "front", None, None), P("layer", "front", None)),
        out_specs=(whole, whole),
        check_vma=False,
    )
```

```python
import functools

import jax
import jax.numpy as jnp
from jax import lax
from jax.experimental import pallas as pl
from jax.experimental.pallas import tpu as pltpu
from jax.sharding import PartitionSpec as P


P_SIZE = 256
Q = 256
TR = 128
RB = 32
S = 32
NB = 16
QB = 8
CAP = 2
HALF = 16
GROUP = 32
LANES = 128

f32 = jnp.float32
bf16 = jnp.bfloat16
VMEM_LIMIT = 40 * 1024 * 1024
ALMOST_ALL_VMEM = 60 * 1024 * 1024
smem = pl.BlockSpec(memory_space=pltpu.SMEM)
vmem = pl.BlockSpec(memory_space=pltpu.VMEM)
hbm = pl.BlockSpec(memory_space=pl.ANY)
NN = (((1,), (0,)), ((), ()))
NT = (((1,), (1,)), ((), ()))


def halves(value):
    high = value.astype(bf16)
    return high, (value - high.astype(f32)).astype(bf16)


def dot(first, second, dims=NN):
    return lax.dot_general(first, second, dims, preferred_element_type=f32)


def product(first, second, dims=NN):
    first_high, first_low = halves(first)
    second_high, second_low = halves(second)
    return (
        dot(first_high, second_high, dims)
        + dot(first_high, second_low, dims)
        + dot(first_low, second_high, dims)
    )


def narrow_product(first, second):
    first_high, first_low = halves(first)
    second_high, second_low = halves(second)
    both = dot(first_high, jnp.concatenate([second_high, second_low], axis=1))
    return both[:, :LANES] + both[:, LANES:] + dot(first_low, second_high)


def stacked(value):
    return jnp.concatenate(halves(value), axis=0)


def stacked_product(first, second):
    rows = first.shape[0] // 2
    both = dot(first, jnp.concatenate(halves(second), axis=1))
    return (both[:rows, :LANES] + both[:rows, LANES:]) + (both[rows:, :LANES] + both[rows:, LANES:])


def complex_pair(first, second, dims=NN):
    real = product(first[0], second[0], dims) - product(first[1], second[1], dims)
    imag = product(first[0], second[1], dims) + product(first[1], second[0], dims)
    return real, imag


def lane_ids(rows):
    return lax.broadcasted_iota(jnp.int32, (rows, LANES), 1)


def turned(value):
    lanes = lane_ids(value.shape[0])
    ahead = pltpu.roll(value, LANES - HALF, 1)
    behind = pltpu.roll(value, HALF, 1)
    return jnp.where(lanes % GROUP < HALF, -ahead, behind)


def pick(group, choices):
    return jnp.where(
        group == 0,
        choices[0],
        jnp.where(group == 1, choices[1], jnp.where(group == 2, choices[2], choices[3])),
    )


def rotations(value):
    return [value] + [pltpu.roll(value, GROUP * turn, 1) for turn in (1, 2, 3)]


def spread_group(rolled, group, source):
    return pick(group, [rolled[(place - source) % 4] for place in range(4)])


def unpack(packed):
    count = packed.shape[0]
    flat = packed.reshape(count * 8, LANES)
    group = lane_ids(count * 8) // GROUP
    rolled = rotations(flat)
    parts = [spread_group(rolled, group, k).reshape(count, 8, LANES) for k in range(4)]
    return jnp.stack(parts, axis=1).reshape(count * RB, LANES)


def unpack_both(packed):
    count = packed.shape[0]
    flat = packed.reshape(count * 8, LANES)
    return unpack(packed), unpack(turned(flat).reshape(count, 8, LANES))


def pack(spread):
    count = spread.shape[0] // RB
    parts = spread.reshape(count, 4, 8, LANES)
    group = lax.broadcasted_iota(jnp.int32, (count, 8, LANES), 2) // GROUP
    return pick(group, [parts[:, k] for k in range(4)])


def source_kernel(
    place_ref,
    down_hbm,
    up_hbm,
    leaf_hbm,
    coupling_hbm,
    own_u_ref,
    other_u_ref,
    own_y_ref,
    other_y_ref,
    down_ref,
    up_ref,
    leaf_ref,
    coupling_ref,
    semaphores,
):
    copies = [
        pltpu.make_async_copy(source, target, semaphores.at[index])
        for index, (source, target) in enumerate(
            (
                (down_hbm, down_ref),
                (up_hbm, up_ref),
                (leaf_hbm, leaf_ref),
                (coupling_hbm, coupling_ref),
            )
        )
    ]
    for copy in copies:
        copy.start()
    core = place_ref[0] % 2
    own_row = pl.multiple_of(core * HALF, HALF)
    other_row = pl.multiple_of((1 - core) * HALF, HALF)
    copies[0].wait()
    copies[1].wait()
    rows, turned_rows = [], []
    for source in (down_ref, up_ref):
        for start in (own_row, other_row):
            real = source[0, pl.ds(start, HALF), :]
            imag = source[1, pl.ds(start, HALF), :]
            rows += [real, imag]
            turned_rows += [-imag, real]
    copies[2].wait()
    y = product(leaf_ref[0], jnp.concatenate(rows, axis=0), NT) + product(
        leaf_ref[1], jnp.concatenate(turned_rows, axis=0), NT
    )
    rolled = rotations(y)
    y_group = lane_ids(P_SIZE) // GROUP
    for sweep in range(2):
        for side, y_ref in enumerate((own_y_ref, other_y_ref)):
            y_ref[sweep] = spread_group(rolled, y_group, 2 * sweep + side)
    copies[3].wait()
    u = narrow_product(coupling_ref[0], y) + narrow_product(coupling_ref[1], turned(y))
    parts = u.reshape(NB, 4, 8, LANES)
    u_group = lane_ids(NB * 8) // GROUP
    for sweep in range(2):
        for side, u_ref in enumerate((own_u_ref, other_u_ref)):
            choices = []
            for k in range(4):
                part = parts[:, k].reshape(NB * 8, LANES)
                turn = (k - 2 * sweep - side) % 4
                choices.append(pltpu.roll(part, GROUP * turn, 1) if turn else part)
            u_ref[sweep] = pick(u_group, choices).reshape(NB, 8, LANES)


def operator_kernel(
    after_ref,
    leaf_hbm,
    coupling_hbm,
    top_hbm,
    bottom_hbm,
    own_sep_hbm,
    other_sep_hbm,
    forward_ref,
    back_ref,
    seps_ref,
    leaf_ref,
    coupling_ref,
    top_ref,
    bottom_ref,
    sep_ref,
    semaphores,
):
    copies = [
        pltpu.make_async_copy(source, target, semaphores.at[index])
        for index, (source, target) in enumerate(
            (
                (leaf_hbm, leaf_ref),
                (top_hbm, top_ref),
                (bottom_hbm, bottom_ref),
                (coupling_hbm, coupling_ref),
                (own_sep_hbm, sep_ref.at[0]),
                (other_sep_hbm, sep_ref.at[1]),
            )
        )
    ]
    for copy in copies:
        copy.start()
    for copy in copies[:3]:
        copy.wait()
    leaf = (leaf_ref[0], leaf_ref[1])
    inject = tuple(
        jnp.concatenate([top_ref[part], bottom_ref[part]], axis=0) for part in range(2)
    )
    local = complex_pair(leaf, inject, NT)
    copies[3].wait()
    coupling = (coupling_ref[0], coupling_ref[1])
    update = complex_pair(coupling, local)
    for sweep in range(2):
        for part in range(2):
            columns = slice(sweep * TR, sweep * TR + TR)
            place = slice(part * TR, part * TR + TR)
            forward_ref[sweep, : NB * RB, place] = update[part][:, columns]
            forward_ref[sweep, NB * RB :, place] = local[part][:, columns]
    back = complex_pair(leaf, coupling, NT)
    back_ref[0] = back[0]
    back_ref[1] = back[1]
    for side in range(2):
        copies[4 + side].wait()
        for part in range(2):
            seps_ref[side, part] = stacked(sep_ref[side, part])


def gather_kernel(
    own_u_hbm,
    other_u_hbm,
    own_y_hbm,
    other_y_hbm,
    own_back_hbm,
    other_back_hbm,
    own_forward_hbm,
    other_forward_hbm,
    u_ref,
    y_ref,
    backs_ref,
    forwards_ref,
    back_ref,
    forward_ref,
    semaphores,
):
    copies = [
        pltpu.make_async_copy(source, target, semaphores.at[index])
        for index, (source, target) in enumerate(
            (
                (own_back_hbm, back_ref.at[0]),
                (own_forward_hbm, forward_ref.at[0]),
                (other_back_hbm, back_ref.at[1]),
                (other_forward_hbm, forward_ref.at[1]),
                (own_u_hbm, u_ref.at[0]),
                (other_u_hbm, u_ref.at[1]),
                (own_y_hbm, y_ref.at[0]),
                (other_y_hbm, y_ref.at[1]),
            )
        )
    ]
    for copy in copies:
        copy.start()
    for side in range(2):
        copies[2 * side].wait()
        for part in range(2):
            backs_ref[side, part] = stacked(back_ref[side, part])
        copies[2 * side + 1].wait()
        for sweep in range(2):
            forwards_ref[side, sweep] = stacked(forward_ref[side, sweep])
    for copy in copies[4:]:
        copy.wait()


def stage_place(place_ref, stage):
    row = place_ref[0] // 2
    core = place_ref[0] % 2
    sweep = jnp.where(row == stage, 0, 1)
    first = jnp.where(sweep == core, 0, 1)
    return sweep, first


def wait_for(source_ref, target_ref, semaphore):
    pltpu.make_async_copy(source_ref, target_ref, semaphore).wait()


def send_blocks(choice, own_slots_ref, other_slots_ref, packed, send_ref):
    for block in range(NB):
        slot = jnp.where(choice == 0, own_slots_ref[block], other_slots_ref[block])
        send_ref[slot] = packed[block]


def first_kernel(
    place_ref,
    own_targets_ref,
    other_targets_ref,
    own_offsets_ref,
    other_offsets_ref,
    own_u_ref,
    other_u_ref,
    own_slots_ref,
    other_slots_ref,
    send_ref,
):
    leaves = send_ref.shape[0]
    sweep, first = stage_place(place_ref, 0)
    lanes = lane_ids(leaves)
    rows = lax.broadcasted_iota(jnp.int32, (leaves, LANES), 0)
    notes = jnp.full((leaves, LANES), QB, jnp.int32)
    all_slots = []
    for side, (targets_ref, offsets_ref, slots_ref) in enumerate(
        (
            (own_targets_ref, own_offsets_ref, own_slots_ref),
            (other_targets_ref, other_offsets_ref, other_slots_ref),
        )
    ):
        targets = [targets_ref[block] for block in range(NB)]
        slots = []
        for block in range(NB):
            rank = jnp.int32(0)
            for earlier in range(block):
                rank = rank + jnp.where(targets[earlier] == targets[block], 1, 0)
            slot = targets[block] * CAP + rank
            slots_ref[block] = slot
            slots.append(slot)
            here = (rows == targets[block]) & (lanes == CAP * side + rank)
            notes = jnp.where(here, offsets_ref[block], notes)
        all_slots.append(slots)
    send_ref[:, CAP * 8 :, :] = jnp.broadcast_to(
        notes.astype(f32)[:, None, :], (leaves, 8, LANES)
    )
    packed = jnp.where(first == 0, own_u_ref[sweep], other_u_ref[sweep])
    for block in range(NB):
        slot = jnp.where(first == 0, all_slots[0][block], all_slots[1][block])
        row = pl.multiple_of((slot % CAP) * 8, 8)
        send_ref[slot // CAP, pl.ds(row, 8), :] = packed[block]


def separator_solve(choice, offsets_ref, arrived, seps_ref, reply_ref, even_ref, odd_ref, solved_ref):
    leaves = reply_ref.shape[0] // CAP
    even_ref[...] = jnp.zeros_like(even_ref)
    odd_ref[...] = jnp.zeros_like(odd_ref)
    places = []
    for leaf in range(leaves):
        for rank, total_ref in enumerate((even_ref, odd_ref)):
            place = offsets_ref[CAP * choice + rank, leaf]
            places.append(place)
            total_ref[place] = total_ref[place] + arrived(leaf, rank)
    rhs, rhs_turned = unpack_both(even_ref[:QB] + odd_ref[:QB])
    solved = stacked_product(seps_ref[choice, 0], rhs) + stacked_product(
        seps_ref[choice, 1], rhs_turned
    )
    solved_ref[:QB] = pack(solved)
    solved_ref[QB] = jnp.zeros((8, LANES), f32)
    for slot, place in enumerate(places):
        reply_ref[slot] = solved_ref[place]


def separator_kernel(
    stage, step, place_ref, offsets_ref, arrived_ref, seps_ref, reply_ref, *scratch
):
    sweep, first = stage_place(place_ref, stage)
    separator_solve(
        first if step == 0 else 1 - first,
        offsets_ref,
        lambda leaf, rank: arrived_ref[CAP * leaf + rank],
        seps_ref,
        reply_ref,
        *scratch,
    )


def first_separator_kernel(
    place_ref,
    arrived_ref,
    seps_ref,
    forward_in_hbm,
    back_in_hbm,
    offsets_ref,
    reply_ref,
    forward_out_hbm,
    back_out_hbm,
    notes_ref,
    semaphore,
    *scratch,
):
    sweep, first = stage_place(place_ref, 0)
    leaves = arrived_ref.shape[0]
    notes = arrived_ref[:, CAP * 8, :]
    whole = jnp.concatenate([notes, jnp.zeros((LANES - leaves, LANES), f32)], axis=0)
    notes_ref[...] = whole.T[:8].astype(jnp.int32)
    copy = pltpu.make_async_copy(notes_ref, offsets_ref, semaphore)
    copy.start()
    copy.wait()
    separator_solve(
        first,
        offsets_ref,
        lambda leaf, rank: arrived_ref[leaf, 8 * rank : 8 * rank + 8, :],
        seps_ref,
        reply_ref,
        *scratch,
    )


def leaf_finish(choice, own_slots_ref, other_slots_ref, returned_ref, backs_ref, base):
    blocks = []
    for block in range(NB):
        slot = jnp.where(choice == 0, own_slots_ref[block], other_slots_ref[block])
        blocks.append(returned_ref[slot])
    mine, mine_turned = unpack_both(jnp.stack(blocks, axis=0))
    return (
        base
        + stacked_product(backs_ref[choice, 0], mine)
        + stacked_product(backs_ref[choice, 1], mine_turned)
    )


def leaf_begin(
    sweep,
    choice,
    trace,
    trace_turned,
    own_slots_ref,
    other_slots_ref,
    u_ref,
    y_ref,
    forward,
    send_ref,
    base_ref,
):
    driven = stacked_product(forward, jnp.concatenate([trace, trace_turned], axis=0))
    packed = pack(driven[: NB * RB]) + u_ref[choice, sweep]
    send_blocks(choice, own_slots_ref, other_slots_ref, packed, send_ref)
    base_ref[...] = driven[NB * RB :] + y_ref[choice, sweep]


def trace_rows(sweep, field_ref):
    return field_ref[pl.ds(pl.multiple_of((1 - sweep) * TR, TR), TR), :]


def middle_kernel(
    stage,
    place_ref,
    own_slots_ref,
    other_slots_ref,
    u_ref,
    y_ref,
    forwards_hbm,
    backs_ref,
    returned_ref,
    base_refs,
    field_ref,
    send_ref,
    next_base_ref,
    forward_ref,
    semaphore,
):
    sweep, first = stage_place(place_ref, stage)
    copy = pltpu.make_async_copy(forwards_hbm.at[1 - first, sweep], forward_ref, semaphore)
    copy.start()
    base = base_refs[0][...] if base_refs else y_ref[first, sweep]
    field_ref[...] = leaf_finish(
        first, own_slots_ref, other_slots_ref, returned_ref, backs_ref, base
    )
    trace = trace_rows(sweep, field_ref)
    copy.wait()
    leaf_begin(
        sweep,
        1 - first,
        trace,
        turned(trace),
        own_slots_ref,
        other_slots_ref,
        u_ref,
        y_ref,
        forward_ref[...],
        send_ref,
        next_base_ref,
    )


def last_kernel(
    stage,
    place_ref,
    own_slots_ref,
    other_slots_ref,
    backs_ref,
    returned_ref,
    base_ref,
    field_ref,
    trace_ref,
):
    sweep, first = stage_place(place_ref, stage)
    field_ref[...] = leaf_finish(
        1 - first, own_slots_ref, other_slots_ref, returned_ref, backs_ref, base_ref[...]
    )
    trace_ref[...] = pack(trace_rows(sweep, field_ref))


def enter_kernel(
    stage,
    place_ref,
    own_slots_ref,
    other_slots_ref,
    u_ref,
    y_ref,
    forwards_ref,
    trace_ref,
    send_ref,
    next_base_ref,
):
    sweep, first = stage_place(place_ref, stage)
    trace, trace_turned = unpack_both(trace_ref[...])
    leaf_begin(
        sweep,
        first,
        trace,
        trace_turned,
        own_slots_ref,
        other_slots_ref,
        u_ref,
        y_ref,
        forwards_ref[first, sweep],
        send_ref,
        next_base_ref,
    )


def final_kernel(
    place_ref,
    own_slots_ref,
    other_slots_ref,
    backs_ref,
    returned_ref,
    base_ref,
    field_refs,
    own_ref,
    other_ref,
    parts_ref,
    semaphores,
):
    row = place_ref[0] // 2
    core = place_ref[0] % 2
    sweep_now, first = stage_place(place_ref, 3)
    spots, finals = [], []
    for sweep in range(2):
        for position in range(2):
            layer = position if sweep == 0 else 1 - position
            spot = 2 * sweep + jnp.where(core == layer, 0, 1)
            spots.append(spot)
            for stage in range(4):
                active = row == stage if sweep == 0 else row == 3 - stage
                if 2 * stage + position == len(field_refs):
                    finals.append(active)
                    continue

                @pl.when(active)
                def _():
                    pltpu.make_async_copy(
                        field_refs[2 * stage + position],
                        parts_ref.at[spot],
                        semaphores.at[2 * sweep + position],
                    ).start()

    field = leaf_finish(
        1 - first, own_slots_ref, other_slots_ref, returned_ref, backs_ref, base_ref[...]
    )
    for sweep in range(2):

        @pl.when(finals[sweep])
        def _():
            parts_ref[spots[2 * sweep + 1]] = field

        @pl.when(jnp.logical_not(finals[sweep]))
        def _():
            wait_for(field_refs[0], parts_ref.at[0], semaphores.at[2 * sweep + 1])

        wait_for(field_refs[0], parts_ref.at[0], semaphores.at[2 * sweep])
    group = lane_ids(P_SIZE) // GROUP
    joined = pick(group, [parts_ref[index] for index in range(4)])
    rows = joined.T.reshape(2, 2, 2, HALF, P_SIZE)
    own_ref[...] = rows[:, 0]
    other_ref[...] = rows[:, 1]


def output_kernel(place_ref, own_ref, other_ref, down_ref, up_ref):
    core = place_ref[0] % 2
    for sweep, field_ref in enumerate((down_ref, up_ref)):
        for part in range(2):
            field_ref[part, pl.ds(pl.multiple_of(core * HALF, HALF), HALF), :] = own_ref[sweep, part]
            field_ref[part, pl.ds(pl.multiple_of((1 - core) * HALF, HALF), HALF), :] = other_ref[
                sweep, part
            ]


def call(
    kernel, outs, in_specs, out_specs, scratch=(), cost=None, limit=VMEM_LIMIT, aliases=None
):
    return pl.pallas_call(
        kernel,
        out_shape=outs,
        in_specs=in_specs,
        out_specs=out_specs,
        scratch_shapes=list(scratch),
        compiler_params=pltpu.CompilerParams(vmem_limit_bytes=limit),
        cost_estimate=cost,
        input_output_aliases=aliases or {},
    )


def shape(*dims, dtype=f32):
    return jax.ShapeDtypeStruct(dims, dtype)


def cost_of(flops, size):
    return pl.CostEstimate(flops=flops, bytes_accessed=size, transcendentals=0)


def across_cores(value):
    layers = lax.axis_size("layer")
    return lax.ppermute(value, "layer", [(index, index ^ 1) for index in range(layers)])


def exchange(value):
    return lax.all_to_all(value, "front", split_axis=0, concat_axis=0, tiled=True)


def to_next_stage(value, stage):
    moves = [(stage, stage + 1), (3 - stage, 2 - stage)]
    pairs = [(2 * a + core, 2 * b + core) for a, b in moves for core in range(2)]
    return lax.ppermute(value, "layer", pairs)


def body(
    sources_down,
    sources_up,
    leaf_inverse,
    coupling,
    sep_inverse,
    inject_top,
    inject_bottom,
    targets,
    offsets,
):
    leaves = lax.axis_size("front")
    slots = leaves * CAP
    place = lax.axis_index("layer").reshape(1).astype(jnp.int32)
    leaf = leaf_inverse[0, 0]
    rows = coupling[0, 0]
    sep = sep_inverse[0, 0]
    own_targets = targets[0, 0, :, 0]
    other_targets = across_cores(own_targets)
    other_offsets = across_cores(offsets[0, 0])
    other_sep = across_cores(sep)

    source_scratch = pltpu.VMEM((2, S, P_SIZE), f32)
    leaf_scratch = pltpu.VMEM((2, P_SIZE, P_SIZE), f32)
    rows_scratch = pltpu.VMEM((2, NB * RB, P_SIZE), f32)
    inject_scratch = pltpu.VMEM((2, TR, P_SIZE), f32)
    u_shape = shape(2, NB, 8, LANES)
    y_shape = shape(2, P_SIZE, LANES)
    own_u, to_other_u, own_y, to_other_y = call(
        source_kernel,
        (u_shape, u_shape, y_shape, y_shape),
        [smem] + [hbm] * 4,
        (vmem,) * 4,
        [
            source_scratch,
            source_scratch,
            leaf_scratch,
            rows_scratch,
            pltpu.SemaphoreType.DMA((4,)),
        ],
        cost_of(600_000_000, 2_500_000),
        ALMOST_ALL_VMEM,
    )(place, sources_down[0, 0], sources_up[0, 0], leaf, rows)
    other_u = across_cores(to_other_u)

    slot_shape = shape(slots, 8, LANES)
    field_shape = shape(P_SIZE, LANES)
    slots_shape = shape(NB, dtype=jnp.int32)
    own_slots, other_slots, send = call(
        first_kernel,
        (slots_shape, slots_shape, shape(leaves, (CAP + 1) * 8, LANES)),
        [smem] * 5 + [vmem] * 2,
        (smem, smem, vmem),
    )(place, own_targets, other_targets, offsets[0, 0], other_offsets, own_u, other_u)
    arrived = exchange(send)

    own_forward, own_back, seps = call(
        operator_kernel,
        (
            shape(2, NB * RB + P_SIZE, 2 * TR),
            shape(2, P_SIZE, NB * RB),
            shape(2, 2, 2 * Q, Q, dtype=bf16),
        ),
        [hbm] * 7,
        (vmem,) * 3,
        [
            leaf_scratch,
            rows_scratch,
            inject_scratch,
            inject_scratch,
            pltpu.VMEM((2, 2, Q, Q), f32),
            pltpu.SemaphoreType.DMA((6,)),
        ],
        cost_of(4_000_000_000, 5_000_000),
    )(send, leaf, rows, inject_top[0, 0], inject_bottom[0, 0], sep, other_sep)
    separator_scratch = [pltpu.VMEM((QB + 1, 8, LANES), f32)] * 3
    places, reply, own_forward, own_back = call(
        first_separator_kernel,
        (
            shape(8, LANES, dtype=jnp.int32),
            slot_shape,
            shape(*own_forward.shape),
            shape(*own_back.shape),
        ),
        [smem, vmem, vmem, hbm, hbm],
        (smem, vmem, hbm, hbm),
        [pltpu.VMEM((8, LANES), jnp.int32), pltpu.SemaphoreType.DMA] + separator_scratch,
        cost_of(100_000_000, 1_100_000),
        aliases={3: 2, 4: 3},
    )(place, arrived, seps, own_forward, own_back)
    other_y = across_cores(to_other_y)
    other_back = across_cores(own_back)
    other_forward = across_cores(own_forward)

    u, y, backs, forwards = call(
        gather_kernel,
        (
            shape(2, 2, NB, 8, LANES),
            shape(2, 2, P_SIZE, LANES),
            shape(2, 2, 2 * P_SIZE, NB * RB, dtype=bf16),
            shape(2, 2, 2 * (NB * RB + P_SIZE), 2 * TR, dtype=bf16),
        ),
        [hbm] * 8,
        (vmem,) * 4,
        [
            pltpu.VMEM((2, 2, P_SIZE, NB * RB), f32),
            pltpu.VMEM((2, 2, NB * RB + P_SIZE, 2 * TR), f32),
            pltpu.SemaphoreType.DMA((8,)),
        ],
        cost_of(10_000_000, 12_000_000),
    )(own_u, other_u, own_y, other_y, own_back, other_back, own_forward, other_forward)

    def separator(stage, step, arrived):
        return call(
            functools.partial(separator_kernel, stage, step),
            slot_shape,
            [smem] * 2 + [vmem] * 2,
            vmem,
            separator_scratch,
            cost_of(100_000_000, 1_100_000),
        )(place, places, arrived, seps)

    fields = []
    base = None
    trace = None
    for stage in range(4):
        if stage > 0:
            send, base = call(
                functools.partial(enter_kernel, stage),
                (slot_shape, field_shape),
                [smem] * 3 + [vmem] * 4,
                (vmem, vmem),
                cost=cost_of(100_000_000, 2_000_000),
            )(place, own_slots, other_slots, u, y, forwards, trace)
            reply = separator(stage, 0, exchange(send))
        returned = exchange(reply)
        bases = [] if base is None else [base]

        def middle(*refs, stage=stage, count=len(bases)):
            head, rest = refs[:8], refs[8:]
            middle_kernel(stage, *head, rest[:count], *rest[count:])

        field, send, base = call(
            middle,
            (field_shape, slot_shape, field_shape),
            [smem] * 3 + [vmem] * 2 + [hbm] + [vmem] * (2 + len(bases)),
            (vmem,) * 3,
            [
                pltpu.VMEM((2 * (NB * RB + P_SIZE), 2 * TR), bf16),
                pltpu.SemaphoreType.DMA,
            ],
            cost_of(300_000_000, 3_000_000),
        )(place, own_slots, other_slots, u, y, forwards, backs, returned, *bases)
        fields.append(field)
        returned = exchange(separator(stage, 1, exchange(send)))
        if stage == 3:
            break
        field, trace = call(
            functools.partial(last_kernel, stage),
            (field_shape, shape(TR // RB, 8, LANES)),
            [smem] * 3 + [vmem] * 3,
            (vmem, vmem),
            cost=cost_of(200_000_000, 2_000_000),
        )(place, own_slots, other_slots, backs, returned, base)
        fields.append(field)
        trace = to_next_stage(trace, stage)

    half_shape = shape(2, 2, HALF, P_SIZE)

    def final(*refs):
        final_kernel(*refs[:6], refs[6 : 6 + len(fields)], *refs[6 + len(fields) :])

    own, to_other = call(
        final,
        (half_shape, half_shape),
        [smem] * 3 + [vmem] * 3 + [hbm] * len(fields),
        (vmem, vmem),
        [pltpu.VMEM((4, P_SIZE, LANES), f32), pltpu.SemaphoreType.DMA((4,))],
    )(place, own_slots, other_slots, backs, returned, base, *fields)
    down, up = call(
        output_kernel,
        (shape(2, S, P_SIZE), shape(2, S, P_SIZE)),
        [smem, vmem, vmem],
        (vmem, vmem),
    )(place, own, across_cores(to_other))
    return down[None, None], up[None, None]


def solution(mesh):
    whole = P("layer", "front", None, None, None)
    return jax.shard_map(
        body,
        mesh=mesh,
        in_specs=(whole,) * 7 + (P("layer", "front", None, None), P("layer", "front", None)),
        out_specs=(whole, whole),
        check_vma=False,
    )
```
